32 devices in a mesh: seq: 4 (over y, x), dp: 8 (over z, core).
Axes of the slice: x: 2, y: 2, z: 4, core: 2. Of those that a mesh axis runs over, the one named last changes fastest.
Arguments:
- tokens: float32 [64, 512, 768], P('dp', 'seq')
- positions: int32 [64, 128], P('dp'), may hold values from 0 to 511, as said below
- counts: int32 [64], P('dp'), may hold values from 44 to 128, as said below
- cotangent: float32 [64, 128, 768], P('dp'), may hold values from -6 to 6
- attn_weights: float32 [4, 768, 768], P(None, ('seq', 'dp'))
- ffn_in: float32 [768, 3072], P(('seq', 'dp')), may hold values from -0.21875 to 0.21875
- ffn_out: float32 [3072, 768], P(('seq', 'dp')), may hold values from -0.109375 to 0.109375
- vectors: float32 [9216], P(('seq', 'dp'))
- attn_first: float32 [4, 768, 768], P(None, ('seq', 'dp')), may hold values from -0.005859375 to 0.005859375
- ffn_in_first: float32 [768, 3072], P(('seq', 'dp')), may hold values from -0.005859375 to 0.005859375
- ffn_out_first: float32 [3072, 768], P(('seq', 'dp')), may hold values from -0.005859375 to 0.005859375
- vector_first: float32 [9216], P(('seq', 'dp')), may hold values from -0.0234375 to 0.0234375
- attn_second: float32 [4, 768, 768], P(None, ('seq', 'dp')), may hold values from 7.0550676e-08 to 1.1288108e-06
- ffn_in_second: float32 [768, 3072], P(('seq', 'dp')), may hold values from 7.0550676e-08 to 1.1288108e-06
- ffn_out_second: float32 [3072, 768], P(('seq', 'dp')), may hold values from 7.0550676e-08 to 1.1288108e-06
- vector_second: float32 [9216], P(('seq', 'dp')), may hold values from 1.1288108e-06 to 1.8060973e-05
Outputs:
- output: float32 [64, 512, 768], P('dp', 'seq')
- grad_tokens: float32 [64, 512, 768], P('dp', 'seq')
- grad_attn: float32 [4, 768, 768], P(None, ('seq', 'dp'))
- grad_ffn_in: float32 [768, 3072], P(('seq', 'dp'))
- grad_ffn_out: float32 [3072, 768], P(('seq', 'dp'))
- grad_vectors: float32 [9216], P(('seq', 'dp'))
- new_attn_first: float32 [4, 768, 768], P(None, ('seq', 'dp'))
- new_ffn_in_first: float32 [768, 3072], P(('seq', 'dp'))
- new_ffn_out_first: float32 [3072, 768], P(('seq', 'dp'))
- new_vector_first: float32 [9216], P(('seq', 'dp'))
- new_attn_second: float32 [4, 768, 768], P(None, ('seq', 'dp'))
- new_ffn_in_second: float32 [768, 3072], P(('seq', 'dp'))
- new_ffn_out_second: float32 [3072, 768], P(('seq', 'dp'))
- new_vector_second: float32 [9216], P(('seq', 'dp'))
- new_attn: float32 [4, 768, 768], P(None, ('seq', 'dp'))
- new_ffn_in: float32 [768, 3072], P(('seq', 'dp'))
- new_ffn_out: float32 [3072, 768], P(('seq', 'dp'))
- new_vectors: float32 [9216], P(('seq', 'dp'))
- low_attn: bfloat16 [4, 768, 768], P(None, ('seq', 'dp'))
- low_ffn_in: bfloat16 [768, 3072], P(('seq', 'dp'))
- low_ffn_out: bfloat16 [3072, 768], P(('seq', 'dp'))
- lamb_norms: float32 [2, 6], replicated
- trust_ratio: float32 [6], replicated
- grad_norm: float32 [], replicated
The draws below stay inside these ranges and needn't reach their ends.
Inputs may be any that keep to these rules, and one draw needn't show every extreme that they name: Each row lists distinct positions of its sequence; only the first counts[s] entries of row s are masked positions, the others are ignored. `counts`: some sequence has exactly 128 masked positions.
All inputs are finite; a program needn't handle non-finite values.
Results may differ from the reference program's by a relative error of at most 0.014.
The reference program's roundings to bfloat16 on the way count: a program that leaves them out, or rounds other values in their place, can miss the bound.
Values may be sent and summed in bfloat16 or wider, within the bound.
A program may use at most 256 MiB of HBM per device.

```python
import math
import jax
import jax.numpy as jnp
from jax import lax

D = 768
H = 12
HD = 64
FF = 3072
SEQ_LEN = 512
MAXM = 128
STEP = 5
NSEQ = 64
VEC = 9216
PARAMS = 7087104


def draw_tokens(key, part):
    key = jax.random.fold_in(key, 11)
    base_key, row_key = jax.random.split(key)
    row_draw = jax.random.uniform(row_key, (NSEQ, SEQ_LEN, 1), jnp.float32, -1.0, 1.0)
    base = jax.random.normal(base_key, (NSEQ, SEQ_LEN, D), jnp.float32)
    columns = jnp.exp(jnp.linspace(math.log(0.55), math.log(1.65), D, dtype=jnp.float32))
    row_scale = jnp.exp(row_draw * 0.7)
    return base * columns * row_scale


def draw_positions(key, part):
    key = jax.random.fold_in(key, 12)
    perm_key, offset_key = jax.random.split(key)
    strata = jax.vmap(lambda single: jax.random.permutation(single, MAXM))(jax.random.split(perm_key, NSEQ))
    offsets = jax.random.randint(offset_key, (NSEQ, MAXM), 0, SEQ_LEN // MAXM)
    return (strata.astype(jnp.int32) * (SEQ_LEN // MAXM) + offsets).astype(jnp.int32)


def draw_counts(key, part):
    key = jax.random.fold_in(key, 13)
    div_key, pick_key = jax.random.split(key)
    divisor = jax.random.randint(div_key, (NSEQ,), 8, 24)
    base = MAXM * 8 // divisor
    chosen = jax.random.randint(pick_key, (), 0, NSEQ)
    return jnp.where(jnp.arange(NSEQ) == chosen, MAXM, base).astype(jnp.int32)


def draw_attn_weights(key, part):
    key = jax.random.fold_in(key, 14)
    base = jax.random.normal(key, (4, D, D), jnp.float32) / math.sqrt(D)
    factors = jnp.array([1.0, 1.0, 1.0, 6.0], jnp.float32).reshape(4, 1, 1)
    return base * factors


def draw_vectors(key, part):
    key = jax.random.fold_in(key, 15)
    noise_key, gain_key = jax.random.split(key)
    biases = 0.3 * jax.random.normal(noise_key, (VEC,), jnp.float32)
    rising = jnp.exp(jnp.linspace(math.log(0.6), math.log(1.8), D, dtype=jnp.float32))
    jitter = jax.random.uniform(gain_key, (2, D), jnp.float32, 0.85, 1.15)
    return jnp.concatenate([biases[:4 * D], rising * jitter[0], biases[5 * D:6 * D], rising * jitter[1], biases[7 * D:]])


def level_of(key, dims, shards, smallest, top_value):
    level = 1.0
    for dim, shards_of in shards:
        draws = jax.random.uniform(jax.random.fold_in(jax.random.fold_in(key, 6), dim), (shards_of,), jnp.float32, smallest / len(shards), top_value / len(shards))
        level = level * jnp.repeat(jnp.exp(draws), dims[dim] // shards_of).reshape((-1,) + (1,) * (len(dims) - 1 - dim))
    return level


def centred(key, extent, width, bound, shards=(), kind=jnp.bfloat16):
    values = jax.random.normal(key, extent, jnp.float32) * width
    if len(shards) > 0:
        values = level_of(key, extent, shards, -0.22, 0.18) * values
    return jnp.clip(values, min=-bound, max=bound).astype(kind)


def setup_inputs(seed: int = 0) -> dict:
    streams_of = jax.random.split(jax.random.key(seed), 17)
    return {
        "tokens": draw_tokens(jax.random.fold_in(streams_of[16], 71), 0),
        "positions": draw_positions(jax.random.fold_in(streams_of[16], 71), 0),
        "counts": draw_counts(jax.random.fold_in(streams_of[16], 71), 0),
        "cotangent": centred(streams_of[3], (NSEQ, MAXM, D), 1.0, 6.0, ((0, 8),), jnp.float32),
        "attn_weights": draw_attn_weights(jax.random.fold_in(streams_of[16], 71), 0),
        "ffn_in": centred(streams_of[5], (D, FF), D ** -0.5, 0.21875, ((0, 32),), jnp.float32),
        "ffn_out": centred(streams_of[6], (FF, D), FF ** -0.5, 0.109375, ((0, 32),), jnp.float32),
        "vectors": draw_vectors(jax.random.fold_in(streams_of[16], 71), 0),
        "attn_first": centred(streams_of[8], (4, D, D), (1.0 / PARAMS ** 0.5), 0.005859375, ((1, 32),), jnp.float32),
        "ffn_in_first": centred(streams_of[9], (D, FF), (1.0 / PARAMS ** 0.5), 0.005859375, ((0, 32),), jnp.float32),
        "ffn_out_first": centred(streams_of[10], (FF, D), (1.0 / PARAMS ** 0.5), 0.005859375, ((0, 32),), jnp.float32),
        "vector_first": centred(streams_of[11], (VEC,), (4.0 / PARAMS ** 0.5), 0.0234375, ((0, 32),), jnp.float32),
        "attn_second": jnp.clip(jnp.exp(math.log(1.1288108225926408e-06) - 2.7725887 * jax.random.uniform(streams_of[12], (4, D, D), jnp.float32) ** level_of(streams_of[12], (4, D, D), ((1, 32),), -0.2, 0.2)), 7.055067641204005e-08, 1.1288108225926408e-06),
        "ffn_in_second": jnp.clip(jnp.exp(math.log(1.1288108225926408e-06) - 2.7725887 * jax.random.uniform(streams_of[13], (D, FF), jnp.float32) ** level_of(streams_of[13], (D, FF), ((0, 32),), -0.2, 0.2)), 7.055067641204005e-08, 1.1288108225926408e-06),
        "ffn_out_second": jnp.clip(jnp.exp(math.log(1.1288108225926408e-06) - 2.7725887 * jax.random.uniform(streams_of[14], (FF, D), jnp.float32) ** level_of(streams_of[14], (FF, D), ((0, 32),), -0.2, 0.2)), 7.055067641204005e-08, 1.1288108225926408e-06),
        "vector_second": jnp.clip(jnp.exp(math.log(1.8060973161482252e-05) - 2.7725887 * jax.random.uniform(streams_of[15], (VEC,), jnp.float32) ** level_of(streams_of[15], (VEC,), ((0, 32),), -0.2, 0.2)), 1.1288108225926408e-06, 1.8060973161482252e-05),
    }


decay_rate = 0.5
step_rate = 0.3
weight_decay = 0.01
adam_eps = 1e-06
norm_eps = 1e-12
highest = lax.Precision.HIGHEST

@jax.custom_vjp
def low(v):
    return lax.optimization_barrier(v.astype(jnp.bfloat16)).astype(jnp.float32)

@jax.custom_vjp
def low_back(v):
    return v

def low_keep(v):
    return (low(v), None)

def low_pass(kept, grad):
    return (grad,)

def back_keep(v):
    return (v, None)

def back_low(kept, grad):
    return (low(grad),)
low.defvjp(low_keep, low_pass)
low_back.defvjp(back_keep, back_low)

def layer_norm(hidden, gain_vec, shift_vec):
    center = hidden - lax.optimization_barrier(jnp.mean(hidden, -1, keepdims=True))
    spread = lax.optimization_barrier(jnp.mean(center * center, -1, keepdims=True))
    return center * lax.rsqrt(spread + norm_eps) * gain_vec + shift_vec

def split_vectors(vectors):
    pieces = [vectors[index * D:(index + 1) * D] for index in range(8)]
    return pieces + [vectors[8 * D:]]

def project(inputs, matrix):
    return jnp.einsum('gld,de->gle', inputs, matrix, precision=highest)

def forward(tokens, attn_weights, ffn_in, ffn_out, vectors):
    attn_low = low(attn_weights)
    in_low = low(ffn_in)
    out_low = low(ffn_out)
    bias_query, bias_value, bias_out, bias_feed, gain_one, shift_one, gain_two, shift_two, bias_inner = split_vectors(low(vectors))
    group = tokens.shape[0]
    head_shape = (group, SEQ_LEN, H, HD)
    tokens_low = low(tokens)
    query = low(low_back(project(tokens_low, attn_low[0]) + bias_query)).reshape(head_shape)
    keys = low(low_back(project(tokens_low, attn_low[1]))).reshape(head_shape)
    values = low(low_back(project(tokens_low, attn_low[2]) + bias_value)).reshape(head_shape)
    scores = low_back(jnp.einsum('gqhe,gkhe->ghqk', query, keys, precision=highest) * HD ** (-0.5))
    attn_probs = low(jax.nn.softmax(scores, axis=-1))
    context = jnp.einsum('ghqk,gkhe->gqhe', attn_probs, values, precision=highest).reshape(group, SEQ_LEN, D)
    context = low(low_back(context))
    attended = low_back(project(context, attn_low[3]) + bias_out)
    first_norm = layer_norm(tokens + attended, gain_one, shift_one)
    inner_pre = low_back(project(low(first_norm), in_low) + bias_inner)
    active = low(jax.nn.gelu(inner_pre, approximate=False))
    feed_out = low_back(project(active, out_low) + bias_feed)
    return layer_norm(first_norm + feed_out, gain_two, shift_two)

def adam_direction(first_old, second_old, clipped):
    first_new = decay_rate * first_old + (1.0 - decay_rate) * clipped
    second_new = decay_rate * second_old + (1.0 - decay_rate) * clipped * clipped
    correct = 1.0 - decay_rate ** STEP
    direction = first_new / correct / (jnp.sqrt(second_new / correct) + adam_eps)
    return (first_new, second_new, direction)

def reference(tokens, positions, counts, cotangent, attn_weights, ffn_in, ffn_out, vectors, attn_first, ffn_in_first, ffn_out_first, vector_first, attn_second, ffn_in_second, ffn_out_second, vector_second):
    group = math.gcd(NSEQ, max(1, 4096 // SEQ_LEN))
    turns = NSEQ // group
    params = (attn_weights, ffn_in, ffn_out, vectors)
    slot_ids = jnp.arange(MAXM, dtype=jnp.int32)
    seq_ids = jnp.arange(group, dtype=jnp.int32)[:, None] * jnp.ones((1, MAXM), jnp.int32)

    def one_group(totals, turn):
        start = (turn * group).astype(jnp.int32)
        tokens_in = lax.dynamic_slice_in_dim(tokens, start, group, 0)
        where_in = lax.dynamic_slice_in_dim(positions, start, group, 0)
        count_in = lax.dynamic_slice_in_dim(counts, start, group, 0)
        cot_in = lax.dynamic_slice_in_dim(cotangent, start, group, 0)
        live_slots = (slot_ids[None, :] < count_in[:, None]).astype(jnp.float32)
        dense_grad = jnp.zeros((group, SEQ_LEN, D), jnp.float32).at[seq_ids, where_in].add(cot_in * live_slots[:, :, None])
        result, pull = jax.vjp(forward, tokens_in, *params)
        grads = pull(dense_grad)
        totals = tuple((total + piece for total, piece in zip(totals, grads[1:])))
        return (totals, (result, grads[0]))
    zeros_init = tuple((jnp.zeros_like(param) for param in params))
    totals, (results, token_grads) = lax.scan(one_group, zeros_init, jnp.arange(turns, dtype=jnp.int32))
    output = results.reshape(NSEQ, SEQ_LEN, D)
    grad_tokens = token_grads.reshape(NSEQ, SEQ_LEN, D)
    square_sum = sum((jnp.sum(total * total) for total in totals))
    grad_norm = jnp.sqrt(square_sum)
    clip_factor = 1.0 / jnp.maximum(grad_norm, 1.0)
    clipped = tuple((total * clip_factor for total in totals))
    firsts = (attn_first, ffn_in_first, ffn_out_first, vector_first)
    seconds = (attn_second, ffn_in_second, ffn_out_second, vector_second)
    moved = [adam_direction(firsts[index], seconds[index], clipped[index]) for index in range(4)]
    directions = [moved[index][2] + weight_decay * params[index] for index in range(3)]
    weight_sq = jnp.concatenate([lax.optimization_barrier(jnp.sum(attn_weights * attn_weights, axis=(1, 2))), jnp.sum(ffn_in * ffn_in)[None], jnp.sum(ffn_out * ffn_out)[None]])
    dir_sq = jnp.concatenate([lax.optimization_barrier(jnp.sum(directions[0] * directions[0], axis=(1, 2))), jnp.sum(directions[1] * directions[1])[None], jnp.sum(directions[2] * directions[2])[None]])
    lamb_norms = jnp.sqrt(jnp.stack([weight_sq, dir_sq]))
    trust_ratio = lamb_norms[0] / lamb_norms[1]
    new_attn = attn_weights - step_rate * trust_ratio[:4, None, None] * directions[0]
    new_ffn_in = ffn_in - step_rate * trust_ratio[4] * directions[1]
    new_ffn_out = ffn_out - step_rate * trust_ratio[5] * directions[2]
    new_vectors = vectors - step_rate * moved[3][2]
    return (output, grad_tokens, clipped[0], clipped[1], clipped[2], clipped[3], moved[0][0], moved[1][0], moved[2][0], moved[3][0], moved[0][1], moved[1][1], moved[2][1], moved[3][1], new_attn, new_ffn_in, new_ffn_out, new_vectors, new_attn.astype(jnp.bfloat16), new_ffn_in.astype(jnp.bfloat16), new_ffn_out.astype(jnp.bfloat16), lamb_norms, trust_ratio, grad_norm)
```

```python
import jax
import jax.numpy as jnp
from jax import lax
from jax.sharding import PartitionSpec as P

H = 12
HD = 64
STEP = 5


decay_rate = 0.5
step_rate = 0.3
weight_decay = 0.01
adam_eps = 1e-06
norm_eps = 1e-12


def layer_norm(hidden, gain_vec, shift_vec):
    center = hidden - jnp.mean(hidden, -1, keepdims=True)
    spread = jnp.mean(center * center, -1, keepdims=True)
    return center * lax.rsqrt(spread + norm_eps) * gain_vec + shift_vec


def gelu_exact(inputs):
    return jax.nn.gelu(inputs, approximate=False)


def column_sum(inputs):
    return jnp.sum(inputs.astype(jnp.float32), axis=0)


def adam_direction(first_old, second_old, clipped):
    first_new = decay_rate * first_old + (1.0 - decay_rate) * clipped
    second_new = decay_rate * second_old + (1.0 - decay_rate) * clipped * clipped
    correct = 1.0 - decay_rate**STEP
    direction = first_new / correct / (jnp.sqrt(second_new / correct) + adam_eps)
    return (first_new, second_new, direction)


def body(
    tokens,
    positions,
    counts,
    cotangent,
    attn_weights,
    ffn_in,
    ffn_out,
    vectors,
    attn_first,
    ffn_in_first,
    ffn_out_first,
    vector_first,
    attn_second,
    ffn_in_second,
    ffn_out_second,
    vector_second,
):
    bf16 = jnp.bfloat16
    f32 = jnp.float32
    sequences, block_size, model_width = tokens.shape
    head_count = H
    head_size = HD
    parts = lax.axis_size("seq")
    length = block_size * parts
    own = sequences // parts
    rows = own * length
    slots = positions.shape[1]
    score_scale = head_size ** (-0.5)
    attn_full = lax.all_gather(attn_weights.astype(bf16), ("seq", "dp"), axis=1, tiled=True)
    in_full = lax.all_gather(ffn_in.astype(bf16), ("seq", "dp"), axis=0, tiled=True)
    out_full = lax.all_gather(ffn_out.astype(bf16), ("seq", "dp"), axis=0, tiled=True)
    vec_full = lax.all_gather(vectors.astype(bf16), ("seq", "dp"), axis=0, tiled=True)
    vec_float = vec_full.astype(f32)
    pieces = [vec_float[index * model_width : (index + 1) * model_width] for index in range(8)]
    bias_query, bias_value, bias_out, bias_feed, gain_one, shift_one, gain_two, shift_two = pieces
    bias_inner = vec_float[8 * model_width :]
    token_high = tokens.astype(bf16)
    token_rest = (tokens - token_high.astype(f32)).astype(bf16)
    flat_low = lax.all_to_all(token_high, "seq", 0, 1, tiled=True).reshape(rows, model_width)
    flat_rest = lax.all_to_all(token_rest, "seq", 0, 1, tiled=True).reshape(rows, model_width)
    flat_tokens = flat_low.astype(f32) + flat_rest.astype(f32)
    first_own = lax.axis_index("seq") * own
    my_places = lax.dynamic_slice_in_dim(positions, first_own, own, 0)
    my_counts = lax.dynamic_slice_in_dim(counts, first_own, own, 0)
    my_cotangent = lax.dynamic_slice_in_dim(cotangent, first_own, own, 0)
    hit = my_places[:, :, None] == jnp.arange(length, dtype=jnp.int32)[None, None, :]
    hit_low = hit.astype(bf16)
    live = jnp.arange(slots, dtype=jnp.int32)[None, :] < my_counts[:, None]

    def pick(dense):
        return jnp.einsum(
            "sjl,sld->sjd",
            hit_low,
            dense.reshape(own, length, -1),
            preferred_element_type=f32,
        ).reshape(own * slots, -1)

    projected = jnp.einsum("rd,kde->kre", flat_low, attn_full[:3], preferred_element_type=f32)
    query_low = (projected[0] + bias_query).astype(bf16)
    key_low = projected[1].astype(bf16)
    value_low = (projected[2] + bias_value).astype(bf16)
    query_heads = query_low.reshape(own, length, head_count, head_size)
    key_heads = key_low.reshape(own, length, head_count, head_size)
    value_heads = value_low.reshape(own, length, head_count, head_size)

    def softmax_of(query_part):
        scores = (
            jnp.einsum("sqhe,skhe->shqk", query_part, key_heads, preferred_element_type=f32)
            * score_scale
        )
        exponent = jnp.exp(scores - jnp.max(scores, -1, keepdims=True))
        return exponent / jnp.sum(exponent, -1, keepdims=True)

    probs_all = softmax_of(query_heads).astype(bf16)
    context = jnp.einsum("shqk,skhe->sqhe", probs_all, value_heads, preferred_element_type=f32)
    context_low = context.reshape(rows, model_width).astype(bf16)

    def front(token_part, context_part):
        attended = jnp.dot(context_part, attn_full[3], preferred_element_type=f32) + bias_out
        return layer_norm(token_part + attended, gain_one, shift_one)

    def inner_of(low):
        return jnp.dot(low, in_full, preferred_element_type=f32) + bias_inner

    def feed_of(active):
        return jnp.dot(active.astype(bf16), out_full, preferred_element_type=f32) + bias_feed

    norm_all = front(flat_tokens, context_low)
    feed_all = feed_of(gelu_exact(inner_of(norm_all.astype(bf16))))
    output = layer_norm(norm_all + feed_all, gain_two, shift_two)
    output = lax.all_to_all(
        output.astype(bf16).reshape(own, length, model_width), "seq", 1, 0, tiled=True
    ).astype(f32)

    context_slot = pick(context_low).astype(bf16)
    token_slot = pick(flat_low) + pick(flat_rest)
    attended = jnp.dot(context_slot, attn_full[3], preferred_element_type=f32) + bias_out
    first_norm, first_pull = jax.vjp(layer_norm, token_slot + attended, gain_one, shift_one)
    first_low = first_norm.astype(bf16)
    active, gelu_pull = jax.vjp(gelu_exact, inner_of(first_low))
    active_low = active.astype(bf16)
    feed_out = feed_of(active)
    _, second_pull = jax.vjp(layer_norm, first_norm + feed_out, gain_two, shift_two)
    slot_grad = jnp.where(live[:, :, None], my_cotangent, 0.0).reshape(own * slots, model_width)
    grad_sum_two, grad_gain_two, grad_shift_two = second_pull(slot_grad)
    feed_back = grad_sum_two.astype(bf16)
    grad_bias_feed = column_sum(feed_back)
    grad_out_matrix = jnp.einsum("rf,rd->fd", active_low, feed_back, preferred_element_type=f32)
    grad_active = jnp.einsum("rd,fd->rf", feed_back, out_full, preferred_element_type=f32)
    (grad_inner,) = gelu_pull(grad_active)
    inner_back = grad_inner.astype(bf16)
    grad_bias_inner = column_sum(inner_back)
    grad_in_matrix = jnp.einsum("rd,rf->df", first_low, inner_back, preferred_element_type=f32)
    grad_first = grad_sum_two + jnp.einsum(
        "rf,df->rd", inner_back, in_full, preferred_element_type=f32
    )
    grad_sum_one, grad_gain_one, grad_shift_one = first_pull(grad_first)
    attended_back = grad_sum_one.astype(bf16)
    grad_bias_out = column_sum(attended_back)
    grad_attn_out = jnp.einsum(
        "rd,re->de", context_slot, attended_back, preferred_element_type=f32
    )
    context_back = jnp.einsum(
        "re,de->rd", attended_back, attn_full[3], preferred_element_type=f32
    ).astype(bf16)
    context_back = context_back.reshape(own, slots, head_count, head_size)
    query_slot = pick(query_low).astype(bf16).reshape(own, slots, head_count, head_size)
    attn_probs = softmax_of(query_slot)
    probs_low = attn_probs.astype(bf16)
    grad_probs = jnp.einsum(
        "sqhe,skhe->shqk", context_back, value_heads, preferred_element_type=f32
    )
    row_delta = jnp.sum(attn_probs * grad_probs, -1, keepdims=True)
    scores_back = (attn_probs * (grad_probs - row_delta)).astype(bf16)
    query_back = (
        (
            jnp.einsum("shqk,skhe->sqhe", scores_back, key_heads, preferred_element_type=f32)
            * score_scale
        )
        .reshape(own * slots, model_width)
        .astype(bf16)
    )
    value_back = jnp.einsum("shqk,sqhe->skhe", probs_low, context_back, preferred_element_type=f32)
    value_back = value_back.astype(bf16).reshape(rows, model_width)
    key_back = (
        jnp.einsum("shqk,sqhe->skhe", scores_back, query_slot, preferred_element_type=f32)
        * score_scale
    )
    key_back = key_back.astype(bf16).reshape(rows, model_width)
    token_slot_low = pick(flat_low).astype(bf16)
    grad_qkv = jnp.stack(
        [
            jnp.einsum("rd,re->de", token_slot_low, query_back, preferred_element_type=f32),
            jnp.einsum("rd,re->de", flat_low, key_back, preferred_element_type=f32),
            jnp.einsum("rd,re->de", flat_low, value_back, preferred_element_type=f32),
        ]
    )
    slot_tokens = grad_sum_one + jnp.einsum(
        "re,de->rd", query_back, attn_full[0], preferred_element_type=f32
    )
    slot_high = slot_tokens.astype(bf16)
    slot_rest = (slot_tokens - slot_high.astype(f32)).astype(bf16)

    def spread(part):
        return jnp.einsum(
            "sjl,sjd->sld",
            hit_low,
            part.reshape(own, slots, model_width),
            preferred_element_type=f32,
        )

    grad_tokens = (
        spread(slot_high)
        + spread(slot_rest)
        + (
            jnp.einsum("re,de->rd", key_back, attn_full[1], preferred_element_type=f32)
            + jnp.einsum("re,de->rd", value_back, attn_full[2], preferred_element_type=f32)
        ).reshape(own, length, model_width)
    )
    grad_tokens = lax.all_to_all(
        grad_tokens.astype(bf16), "seq", 1, 0, tiled=True
    ).astype(f32)
    grad_attn_all = jnp.concatenate([grad_qkv, grad_attn_out[None]], 0)
    grad_vector_all = jnp.concatenate(
        [
            column_sum(query_back),
            column_sum(value_back),
            grad_bias_out,
            grad_bias_feed,
            grad_gain_one,
            grad_shift_one,
            grad_gain_two,
            grad_shift_two,
            grad_bias_inner,
        ]
    )

    def scatter(part, axis):
        return lax.psum_scatter(
            part.astype(bf16), ("seq", "dp"), scatter_dimension=axis, tiled=True
        ).astype(f32)

    shares = (
        scatter(grad_attn_all, 1),
        scatter(grad_in_matrix, 0),
        scatter(grad_out_matrix, 0),
        scatter(grad_vector_all, 0),
    )
    square_sum = lax.psum(sum((jnp.sum(total * total) for total in shares)), ("seq", "dp"))
    grad_norm = jnp.sqrt(square_sum)
    clip_factor = 1.0 / jnp.maximum(grad_norm, 1.0)
    clipped = tuple((share * clip_factor for share in shares))
    params = (attn_weights, ffn_in, ffn_out, vectors)
    firsts = (attn_first, ffn_in_first, ffn_out_first, vector_first)
    seconds = (attn_second, ffn_in_second, ffn_out_second, vector_second)
    moved = [adam_direction(firsts[index], seconds[index], clipped[index]) for index in range(4)]
    directions = [moved[index][2] + weight_decay * params[index] for index in range(3)]
    weight_sq = jnp.concatenate(
        [
            jnp.sum(attn_weights * attn_weights, axis=(1, 2)),
            jnp.sum(ffn_in * ffn_in)[None],
            jnp.sum(ffn_out * ffn_out)[None],
        ]
    )
    dir_sq = jnp.concatenate(
        [
            jnp.sum(directions[0] * directions[0], axis=(1, 2)),
            jnp.sum(directions[1] * directions[1])[None],
            jnp.sum(directions[2] * directions[2])[None],
        ]
    )
    lamb_sq = lax.psum(jnp.stack([weight_sq, dir_sq]), ("seq", "dp"))
    lamb_norms = jnp.sqrt(lamb_sq)
    trust_ratio = lamb_norms[0] / lamb_norms[1]
    new_attn = attn_weights - step_rate * trust_ratio[:4, None, None] * directions[0]
    new_ffn_in = ffn_in - step_rate * trust_ratio[4] * directions[1]
    new_ffn_out = ffn_out - step_rate * trust_ratio[5] * directions[2]
    new_vectors = vectors - step_rate * moved[3][2]
    return (
        output,
        grad_tokens,
        clipped[0],
        clipped[1],
        clipped[2],
        clipped[3],
        moved[0][0],
        moved[1][0],
        moved[2][0],
        moved[3][0],
        moved[0][1],
        moved[1][1],
        moved[2][1],
        moved[3][1],
        new_attn,
        new_ffn_in,
        new_ffn_out,
        new_vectors,
        new_attn.astype(bf16),
        new_ffn_in.astype(bf16),
        new_ffn_out.astype(bf16),
        lamb_norms,
        trust_ratio,
        grad_norm,
    )


def solution(mesh):
    return jax.shard_map(
        body,
        mesh=mesh,
        in_specs=(
            P("dp", "seq", None),
            P("dp", None),
            P("dp"),
            P("dp", None, None),
            P(None, ("seq", "dp"), None),
            P(("seq", "dp"), None),
            P(("seq", "dp"), None),
            P(("seq", "dp")),
            P(None, ("seq", "dp"), None),
            P(("seq", "dp"), None),
            P(("seq", "dp"), None),
            P(("seq", "dp")),
            P(None, ("seq", "dp"), None),
            P(("seq", "dp"), None),
            P(("seq", "dp"), None),
            P(("seq", "dp")),
        ),
        out_specs=(
            P("dp", "seq", None),
            P("dp", "seq", None),
            P(None, ("seq", "dp"), None),
            P(("seq", "dp"), None),
            P(("seq", "dp"), None),
            P(("seq", "dp")),
            P(None, ("seq", "dp"), None),
            P(("seq", "dp"), None),
            P(("seq", "dp"), None),
            P(("seq", "dp")),
            P(None, ("seq", "dp"), None),
            P(("seq", "dp"), None),
            P(("seq", "dp"), None),
            P(("seq", "dp")),
            P(None, ("seq", "dp"), None),
            P(("seq", "dp"), None),
            P(("seq", "dp"), None),
            P(("seq", "dp")),
            P(None, ("seq", "dp"), None),
            P(("seq", "dp"), None),
            P(("seq", "dp"), None),
            P(),
            P(),
            P(),
        ),
        check_vma=False,
    )
```

```python
import functools
import jax
import jax.numpy as jnp
from jax import lax
from jax.sharding import PartitionSpec as P
from jax.experimental import pallas as pl
from jax.experimental.pallas import tpu as pltpu

H = 12
HD = 64
STEP = 5

decay_rate = 0.5
step_rate = 0.3
weight_decay = 0.01
adam_eps = 1e-06
norm_eps = 1e-12
f32 = jnp.float32
bf16 = jnp.bfloat16
MESH = pl.DeviceIdType.MESH


class Place:
    def __init__(self, mesh, shard_rows):
        self.seq = mesh.shape["seq"]
        self.dp = mesh.shape["dp"]
        self.merge = 2
        while (self.merge * shard_rows) % 16:
            self.merge *= 2
        self.seq_bits = self.seq.bit_length() - 1
        self.far_bits = (self.dp // self.merge).bit_length() - 1
        self.bits = self.seq_bits + self.far_bits
        self.groups = self.seq * self.dp // self.merge
        self.devices = self.seq * self.dp

    def here(self):
        self.s = lax.axis_index("seq")
        self.d = lax.axis_index("dp")
        self.member = lax.rem(self.d, self.merge)
        self.core = lax.rem(self.d, 2)
        self.weight = []
        self.bit = []
        for dim in range(self.bits):
            if dim < self.seq_bits:
                w = 1 << (self.seq_bits - 1 - dim)
                self.bit.append(lax.rem(self.s // w, 2))
            else:
                w = self.merge << (self.bits - 1 - dim)
                self.bit.append(lax.rem(self.d // w, 2))
            self.weight.append(w)

    def across(self, dim):
        flip = self.weight[dim] * (1 - 2 * self.bit[dim])
        if dim < self.seq_bits:
            return (self.s + flip, self.d)
        return (self.s, self.d + flip)

    def other_core(self):
        return (self.s, self.d + 1 - 2 * self.core)

    def mates(self):
        base = self.d - self.member
        return [
            (self.s, base + lax.rem(self.member + k, self.merge)) for k in range(1, self.merge)
        ]

    def row_mates(self):
        return [(lax.rem(self.s + k, self.seq), self.d) for k in range(1, self.seq)]

    def greet(self):
        barrier = pltpu.get_barrier_semaphore()
        everyone = self.mates() + self.row_mates()
        everyone += [self.across(dim) for dim in range(self.seq_bits, self.bits)]
        for device in everyone:
            pl.semaphore_signal(barrier, inc=1, device_id=device, device_id_type=MESH)
        pl.semaphore_wait(barrier, len(everyone))

    def box(self, free):
        return tuple(slice(None) if dim in free else self.bit[dim] for dim in range(self.bits))


def erf(x):
    x = jnp.clip(x, -3.832506856900711, 3.832506856900711)
    x2 = x * x
    top = jnp.float32(0.00022905065861350646)
    for c in (
        0.0034082910107109506,
        0.050955695062380861,
        0.18520832239976145,
        1.128379143519084,
    ):
        top = top * x2 + jnp.float32(c)
    low = jnp.float32(-1.1791602954361697e-7)
    for c in (
        0.000023547966471313185,
        0.0010179625278914885,
        0.014070470171167667,
        0.11098505178285362,
        0.49746925110067538,
        1.0,
    ):
        low = low * x2 + jnp.float32(c)
    return x * top / low


def dot(a, b):
    return jnp.dot(a, b, preferred_element_type=f32)


def dot_t(a, b):
    return lax.dot_general(a, b, (((1,), (1,)), ((), ())), preferred_element_type=f32)


def t_dot(a, b):
    return lax.dot_general(a, b, (((0,), (0,)), ((), ())), preferred_element_type=f32)


def normalize(x):
    center = x - jnp.mean(x, -1, keepdims=True)
    inverse = lax.rsqrt(jnp.mean(center * center, -1, keepdims=True) + norm_eps)
    return center * inverse, inverse


class Flows:
    def __init__(self, place, chunks, send, recv):
        self.place = place
        self.chunks = chunks
        self.send = send
        self.recv = recv
        self.stages = place.bits

    def number(self, chunk, part, stage):
        return (chunk * 3 + part) * (self.stages + 1) + stage


class Gather(Flows):
    def copy(self, chunk, part, stage):
        place = self.place
        buf, rows, columns, order = self.chunks[chunk].part(part, place)
        n = self.number(chunk, part, stage)
        box = place.box(order[:stage]) + (rows, columns)
        return pltpu.make_async_remote_copy(
            src_ref=buf.at[box],
            dst_ref=buf.at[box],
            send_sem=self.send.at[n],
            recv_sem=self.recv.at[n],
            device_id=place.across(order[stage]),
            device_id_type=MESH,
        )

    def hand(self, chunk):
        place = self.place
        buf, rows, columns = self.chunks[chunk].half(place)
        n = self.number(chunk, 0, self.stages)
        box = tuple(slice(None) for _ in range(place.bits)) + (rows, columns)
        return pltpu.make_async_remote_copy(
            src_ref=buf.at[box],
            dst_ref=buf.at[box],
            send_sem=self.send.at[n],
            recv_sem=self.recv.at[n],
            device_id=place.other_core(),
            device_id_type=MESH,
        )

    def step(self, t):
        for chunk in range(len(self.chunks)):
            stage = t - chunk
            if 0 <= stage <= self.stages:
                for part in range(3):
                    if stage > 0:
                        self.copy(chunk, part, stage - 1).wait_recv()
                    if stage < self.stages:
                        self.copy(chunk, part, stage).start()
                if stage == self.stages:
                    self.hand(chunk).start()
            if stage == self.stages + 1:
                self.hand(chunk).wait_recv()

    def last_step(self, chunk):
        return chunk + self.stages + 1

    def finish(self):
        for chunk in range(len(self.chunks)):
            for part in range(3):
                for stage in range(self.stages):
                    self.copy(chunk, part, stage).wait_send()
            self.hand(chunk).wait_send()


class Chunk:
    def __init__(self, buf, first, width, orders, cuts=None):
        self.buf, self.first, self.width, self.orders, self.cuts = buf, first, width, orders, cuts

    def half(self, place):
        half = self.width // 2
        start = pl.multiple_of(self.first + place.core * half, 128)
        return self.buf, slice(None), pl.ds(start, half)

    def part(self, part, place):
        half = self.width // 2
        if self.cuts is None:
            third = half // 3
            start = pl.multiple_of(self.first + place.core * half + part * third, 128)
            return self.buf, slice(None), pl.ds(start, third), self.orders[part]
        start = pl.multiple_of(self.first + place.core * half, 128)
        rows = pl.ds(self.cuts[part], self.cuts[part + 1] - self.cuts[part])
        return self.buf, rows, pl.ds(start, half), self.orders[part]


def weight_chunks(place, attn, first_ffn, second_ffn, reverse):
    seq = list(range(place.seq_bits))
    far = list(range(place.seq_bits, place.bits))[::-1]
    left = far + seq[::-1]
    right = far + seq
    chunks = []

    def orders(index):
        a, b = (seq, seq[::-1]) if index % 2 else (seq[::-1], seq)
        if index % 4 < 2:
            third = a + far
        else:
            third = a[:1] + far + a[1:]
        out = [left, right, third]
        return [order[::-1] for order in out] if reverse else out

    width = attn.shape[-1]
    for m in range(4):
        chunks.append(Chunk(attn.at[m], 0, width, orders(m)))
    for j in range(first_ffn.shape[-1] // width):
        chunks.append(Chunk(first_ffn, j * width, width, orders(j)))
    rows = second_ffn.shape[-2]
    third = rows // 3 // 16 * 16
    for j in range(3):
        chunks.append(
            Chunk(second_ffn, j * width // 3, width // 3, orders(j), (0, third, 2 * third, rows))
        )
    return chunks


def forward_kernel(
    place,
    vec_rows,
    vec_count,
    tokens_ref,
    places_ref,
    attn_ref,
    in_ref,
    out_ref,
    vec_ref,
    attn_hbm,
    in_hbm,
    out_hbm,
    vec_hbm,
    high_hbm,
    query_hbm,
    key_hbm,
    value_hbm,
    norm_hbm,
    active_hbm,
    slot_low_hbm,
    slot_hbm,
    slot_active_hbm,
    slot_slope_hbm,
    attn_buf,
    in_buf,
    out_buf,
    vec_buf,
    vec_acc,
    vec,
    attn_in,
    in_in,
    out_in,
    joined,
    send_high,
    send_rest,
    high,
    rest,
    query,
    key,
    value,
    norm,
    active,
    slot_low,
    slot,
    slot_active,
    slot_slope,
    flow_send,
    flow_recv,
    mate_send,
    mate_recv,
    local_sem,
    token_send,
    token_recv,
    vec_send,
    vec_recv,
    save_sem,
):
    place.here()
    place.greet()
    merge, seq = place.merge, place.seq
    width = tokens_ref.shape[-1]
    block = tokens_ref.shape[1]
    own = tokens_ref.shape[0] // seq
    length = block * seq
    rows = own * length
    slots = places_ref.shape[1]
    mine = place.box(())

    sources = (attn_ref, in_ref, out_ref)
    stages = (attn_in, in_in, out_in)
    mate_copies = []
    for index in range(3):
        for k, device in enumerate(place.mates()):
            n = index * (merge - 1) + k
            copy = pltpu.make_async_remote_copy(
                src_ref=sources[index],
                dst_ref=stages[index].at[place.member],
                send_sem=mate_send.at[n],
                recv_sem=mate_recv.at[n],
                device_id=device,
                device_id_type=MESH,
            )
            copy.start()
            mate_copies.append(copy)
    local = []
    for index in range(3):
        copy = pltpu.make_async_copy(
            sources[index], stages[index].at[place.member], local_sem.at[index]
        )
        copy.start()
        local.append(copy)
    vec_mates = []
    vec_buf.at[mine][place.member] = vec_ref[...]
    for k, device in enumerate(place.mates()):
        copy = pltpu.make_async_remote_copy(
            src_ref=vec_ref,
            dst_ref=vec_buf.at[mine].at[place.member],
            send_sem=vec_send.at[k],
            recv_sem=vec_recv.at[k],
            device_id=device,
            device_id_type=MESH,
        )
        copy.start()
        vec_mates.append(copy)

    def split(i, _):
        x = tokens_ref[i]
        top = x.astype(bf16)
        send_high[i] = top
        send_rest[i] = (x - top.astype(f32)).astype(bf16)
        return 0

    lax.fori_loop(0, own * seq, split, 0)
    token_copies = []
    my_columns = pl.ds(pl.multiple_of(place.s * block, block), block)
    for half, (source, target) in enumerate(((send_high, high), (send_rest, rest))):
        for k, device in enumerate(place.row_mates()):
            n = half * (seq - 1) + k
            token_copies.append(
                pltpu.make_async_remote_copy(
                    src_ref=source.at[pl.ds(device[0] * own, own)],
                    dst_ref=target.at[:, my_columns],
                    send_sem=token_send.at[n],
                    recv_sem=token_recv.at[n],
                    device_id=device,
                    device_id_type=MESH,
                )
            )
        target.at[:, my_columns][...] = source[pl.ds(place.s * own, own)]
    for copy in token_copies[: seq - 1]:
        copy.start()

    flows = Gather(place, weight_chunks(place, attn_buf, in_buf, out_buf, False), flow_send, flow_recv)

    def join(chunks, part):
        count = part.shape[1]
        for i in range(merge):
            joined[i * count : (i + 1) * count, : part.shape[-1]] = part[i]
        for chunk in chunks:
            buf, _, columns = chunk.half(place)
            buf.at[mine + (slice(None), columns)][...] = joined[: merge * count, columns].astype(bf16)

    for k in range(3):
        local[k].wait()
        for copy in mate_copies[k * (merge - 1) : (k + 1) * (merge - 1)]:
            copy.wait_recv()
        if k == 0:
            for m in range(4):
                join(flows.chunks[m : m + 1], attn_in.at[:, m])
        elif k == 1:
            join(flows.chunks[4:-3], in_in)
        else:
            join(flows.chunks[-3:], out_in)

    def vec_copy(stage):
        order = list(range(place.bits))
        box = place.box(order[:stage])
        return pltpu.make_async_remote_copy(
            src_ref=vec_buf.at[box],
            dst_ref=vec_buf.at[box],
            send_sem=vec_send.at[merge - 1 + stage],
            recv_sem=vec_recv.at[merge - 1 + stage],
            device_id=place.across(order[stage]),
            device_id_type=MESH,
        )

    for copy in vec_mates:
        copy.wait_recv()
    vec_copy(0).start()
    flows.step(0)
    for t in range(1, flows.stages + 1):
        vec_copy(t - 1).wait_recv()
        if t < flows.stages:
            vec_copy(t).start()
        flows.step(t)
    for copy in token_copies[seq - 1 :]:
        copy.start()

    vec_acc[...] = jnp.zeros_like(vec_acc)
    for owner in range(place.devices):
        group, member = divmod(owner, merge)
        bits = tuple((group >> (place.bits - 1 - dim)) & 1 for dim in range(place.bits))
        first, shift = divmod(vec_count * owner, 128)
        count = (shift + vec_count + 127) // 128
        vec_acc[first : first + count] += vec_buf.at[bits][member, :count]
    per = width // 128
    vec_acc[...] = vec_acc[...].astype(bf16).astype(f32)
    for row in range(vec_rows):
        vec[row : row + 1] = jnp.concatenate(
            [vec_acc[row * per + k : row * per + k + 1] for k in range(per)], axis=1
        )
    saves = []

    def save(source, target):
        copy = pltpu.make_async_copy(source, target, save_sem.at[len(saves)])
        copy.start()
        saves.append(copy)

    save(vec, vec_hbm)

    for copy in token_copies[: seq - 1]:
        copy.wait_recv()
    tile = min(256, length)
    per_seq = length // tile
    save(high, high_hbm)
    scale = HD**-0.5

    for m, target in enumerate((query, key, value)):
        flows.step(flows.last_step(m))
        matrix = attn_buf.at[m].reshape(width, width)

        def project(i, _):
            sequence, at = i // per_seq, pl.ds(pl.multiple_of(lax.rem(i, per_seq) * tile, tile), tile)
            result = dot(high[sequence, at], matrix[...])
            if m == 0:
                result = (result + vec[0:1]).astype(bf16) * scale
            elif m == 2:
                result = result + vec[1:2]
            target[sequence, at] = result.astype(bf16)
            return 0

        lax.fori_loop(0, own * per_seq, project, 0)
        save(target, (query_hbm, key_hbm, value_hbm)[m])

    context = send_high.reshape(own, length, width)
    for copy in token_copies[: seq - 1]:
        copy.wait_send()
    pairs = width // 128
    turns = own * pairs
    lane = lax.broadcasted_iota(jnp.int32, (1, 128), 1)

    def attend(i, _):
        for k in range(3):
            @pl.when(i == (k + 1) * turns // 4)
            def _():
                flows.step(flows.last_step(3 + k))

        sequence, pair = i // pairs, lax.rem(i, pairs)
        at = pl.ds(pl.multiple_of(pair * 128, 128), 128)
        keys, values = key[sequence, :, at], value[sequence, :, at]
        for q in range(per_seq):
            places = slice(q * tile, (q + 1) * tile)
            queries = query[sequence, places, at]
            heads = []
            for head in range(2):
                picked = jnp.where(lane // HD == head, queries, jnp.zeros_like(queries))
                scores = dot_t(picked, keys)
                exponent = jnp.exp(scores - jnp.max(scores, -1, keepdims=True))
                total = jnp.sum(exponent, -1, keepdims=True)
                heads.append(dot(exponent.astype(bf16), values) / total)
            context[sequence, places, at] = jnp.where(lane < HD, heads[0], heads[1]).astype(bf16)
        return 0

    lax.fori_loop(0, turns, attend, 0)
    flows.step(flows.last_step(6))

    for copy in token_copies[seq - 1 :]:
        copy.wait_recv()
    out_matrix = attn_buf.at[3].reshape(width, width)

    def front(i, _):
        sequence, at = i // per_seq, pl.ds(pl.multiple_of(lax.rem(i, per_seq) * tile, tile), tile)
        x = high[sequence, at].astype(f32) + rest[sequence, at].astype(f32)
        x = x + (dot(context[sequence, at], out_matrix[...]) + vec[2:3])
        x, _ = normalize(x)
        norm[sequence, at] = x * vec[4:5] + vec[5:6]
        return 0

    lax.fori_loop(0, own * per_seq, front, 0)
    save(norm, norm_hbm)

    place_ids = lax.broadcasted_iota(jnp.int32, (length, slots), 0)
    for sequence in range(own):
        at = pl.ds(sequence * slots, slots)
        hits = places_ref[pl.ds(place.s * own + sequence, 1)] == place_ids
        hits = jnp.where(hits, 1.0, 0.0).astype(bf16)
        slot_high = t_dot(hits, high[sequence])
        slot_low[0, at] = slot_high.astype(bf16)
        slot_context = t_dot(hits, context[sequence]).astype(bf16)
        slot_low[1, at] = slot_context
        slot_low[2, at] = t_dot(hits, query[sequence]).astype(bf16)
        slot[0, at] = slot_high
        slot[1, at] = t_dot(hits, rest[sequence])
        x = slot[0, at] + slot[1, at]
        x = x + (dot(slot_context, out_matrix[...]) + vec[2:3])
        x, inverse = normalize(x)
        slot[0, at] = x
        slot[2, at] = jnp.broadcast_to(inverse, x.shape)
        x = x * vec[4:5] + vec[5:6]
        slot[1, at] = x
        slot_low[3, at] = x.astype(bf16)
    save(slot_low, slot_low_hbm)
    save(slot, slot_hbm)
    save(attn_buf, attn_hbm)

    in_matrix = in_buf.reshape(width, in_buf.shape[-1])
    for j in range(in_buf.shape[-1] // width):
        if j > 0:
            flows.step(flows.last_step(6 + j))
        at = pl.ds(j * width, width)
        bias = vec[8 + j : 9 + j]

        def hidden(i, _):
            sequence, here = i // per_seq, pl.ds(pl.multiple_of(lax.rem(i, per_seq) * tile, tile), tile)
            x = dot(norm[sequence, here].astype(bf16), in_matrix[:, at]) + bias
            active[sequence, here, at] = (0.5 * x * (1.0 + erf(x * 0.5**0.5))).astype(bf16)
            return 0

        lax.fori_loop(0, own * per_seq, hidden, 0)
        x = dot(slot_low[3], in_matrix[:, at]) + bias
        half = 0.5 * (1.0 + erf(x * 0.5**0.5))
        slot_active[:, at] = (x * half).astype(bf16)
        slot_slope[:, at] = half + x * jnp.exp(-0.5 * x * x) * 0.3989422804014327
    save(active, active_hbm)
    save(slot_active, slot_active_hbm)
    save(slot_slope, slot_slope_hbm)
    save(in_buf, in_hbm)
    for t in range(flows.last_step(9) + 1, flows.last_step(len(flows.chunks) - 1) + 1):
        flows.step(t)
    save(out_buf, out_hbm)
    flows.finish()
    for copy in mate_copies + vec_mates + token_copies[seq - 1 :]:
        copy.wait_send()
    for stage in range(flows.stages):
        vec_copy(stage).wait_send()
    for copy in saves:
        copy.wait()


def forward_call(mesh, tokens, positions, attn_weights, ffn_in, ffn_out, vectors):
    place = Place(mesh, ffn_in.shape[0])
    sequences, block, width = tokens.shape
    inner = ffn_in.shape[1]
    slots = positions.shape[1]
    own = sequences // place.seq
    length = block * place.seq
    vec_count = vectors.shape[0]
    vec_rows = vec_count * place.devices // width
    owner = lax.axis_index("seq") * place.dp + lax.axis_index("dp")
    padded = lax.dynamic_update_slice_in_dim(
        jnp.zeros((1024,), f32), vectors.astype(bf16).astype(f32), lax.rem(vec_count * owner, 128), 0
    ).reshape(8, 128)
    bits = (2,) * place.bits
    r = ffn_in.shape[0]
    joint = r * place.merge
    joint_out = ffn_out.shape[0] * place.merge
    flow_count = (4 + inner // width + 3) * 3 * (place.bits + 1)
    attn_shape = (4,) + bits + (joint, width)
    in_shape = bits + (joint, inner)
    out_shape = bits + (joint_out, width)
    seq_shape = (own, length, width)
    rows = own * slots
    results = [
        (attn_shape, bf16),
        (in_shape, bf16),
        (out_shape, bf16),
        ((16, width), f32),
        (seq_shape, bf16),
        (seq_shape, bf16),
        (seq_shape, bf16),
        (seq_shape, bf16),
        (seq_shape, f32),
        ((own, length, inner), bf16),
        ((4, rows, width), bf16),
        ((3, rows, width), f32),
        ((rows, inner), bf16),
        ((rows, inner), f32),
    ]
    vmem = pl.BlockSpec(memory_space=pltpu.VMEM)
    hbm = pl.BlockSpec(memory_space=pl.ANY)
    dma = pltpu.SemaphoreType.DMA
    mates = place.merge - 1
    return pl.pallas_call(
        functools.partial(forward_kernel, place, vec_rows, vec_count),
        out_shape=[jax.ShapeDtypeStruct(*one) for one in results],
        in_specs=[vmem, vmem, hbm, hbm, hbm, vmem],
        out_specs=[hbm] * len(results),
        scratch_shapes=[
            pltpu.VMEM(attn_shape, bf16),
            pltpu.VMEM(in_shape, bf16),
            pltpu.VMEM(out_shape, bf16),
            pltpu.VMEM(bits + (place.merge, 8, 128), f32),
            pltpu.VMEM((vec_rows * width // 128 + 8, 128), f32),
            pltpu.VMEM((16, width), f32),
            pltpu.VMEM((place.merge,) + attn_weights.shape, f32),
            pltpu.VMEM((place.merge,) + ffn_in.shape, f32),
            pltpu.VMEM((place.merge,) + ffn_out.shape, f32),
            pltpu.VMEM((joint_out, inner), f32),
            pltpu.VMEM((sequences, block, width), bf16),
            pltpu.VMEM((sequences, block, width), bf16),
            pltpu.VMEM(seq_shape, bf16),
            pltpu.VMEM(seq_shape, bf16),
            pltpu.VMEM(seq_shape, bf16),
            pltpu.VMEM(seq_shape, bf16),
            pltpu.VMEM(seq_shape, bf16),
            pltpu.VMEM(seq_shape, f32),
            pltpu.VMEM((own, length, inner), bf16),
            pltpu.VMEM((4, rows, width), bf16),
            pltpu.VMEM((3, rows, width), f32),
            pltpu.VMEM((rows, inner), bf16),
            pltpu.VMEM((rows, inner), f32),
            dma((flow_count,)),
            dma((flow_count,)),
            dma((3 * mates,)),
            dma((3 * mates,)),
            dma((3,)),
            dma((2 * (place.seq - 1),)),
            dma((2 * (place.seq - 1),)),
            dma((mates + place.bits,)),
            dma((mates + place.bits,)),
            dma((len(results),)),
        ],
        compiler_params=pltpu.CompilerParams(
            collective_id=0, has_side_effects=True, vmem_limit_bytes=64 * 2**20 - 2**18
        ),
    )(tokens, positions, attn_weights, ffn_in, ffn_out, padded)


def layer_norm(hidden, gain_vec, shift_vec):
    center = hidden - jnp.mean(hidden, -1, keepdims=True)
    spread = jnp.mean(center * center, -1, keepdims=True)
    return center * lax.rsqrt(spread + norm_eps) * gain_vec + shift_vec


def gelu_exact(inputs):
    return jax.nn.gelu(inputs, approximate=False)


def column_sum(inputs):
    return jnp.sum(inputs.astype(jnp.float32), axis=0)


def adam_direction(first_old, second_old, clipped):
    first_new = decay_rate * first_old + (1.0 - decay_rate) * clipped
    second_new = decay_rate * second_old + (1.0 - decay_rate) * clipped * clipped
    correct = 1.0 - decay_rate**STEP
    direction = first_new / correct / (jnp.sqrt(second_new / correct) + adam_eps)
    return (first_new, second_new, direction)


def body(
    mesh,
    tokens,
    positions,
    counts,
    cotangent,
    attn_weights,
    ffn_in,
    ffn_out,
    vectors,
    attn_first,
    ffn_in_first,
    ffn_out_first,
    vector_first,
    attn_second,
    ffn_in_second,
    ffn_out_second,
    vector_second,
):
    bf16 = jnp.bfloat16
    f32 = jnp.float32
    sequences, block_size, model_width = tokens.shape
    head_count = H
    head_size = HD
    parts = lax.axis_size("seq")
    length = block_size * parts
    own = sequences // parts
    rows = own * length
    slots = positions.shape[1]
    score_scale = head_size ** (-0.5)
    results = forward_call(mesh, tokens, positions, attn_weights, ffn_in, ffn_out, vectors)
    attn_full = results[0].reshape(4, model_width, model_width)
    in_full = results[1].reshape(model_width, -1)
    out_full = results[2].reshape(-1, model_width)
    vec_float = results[3]
    pieces = [vec_float[index] for index in range(8)]
    bias_query, bias_value, bias_out, bias_feed, gain_one, shift_one, gain_two, shift_two = pieces
    flat_low = results[4].reshape(rows, model_width)
    query_low, key_low, value_low = (part.reshape(rows, model_width) for part in results[5:8])
    norm_all = results[8].reshape(rows, model_width)
    token_slot_low, context_slot, query_slot, first_low = (results[10][k] for k in range(4))
    normal_one, first_norm, inverse_one = (results[11][k] for k in range(3))
    active_low = results[12]
    slope = results[13]
    first_own = lax.axis_index("seq") * own
    my_places = lax.dynamic_slice_in_dim(positions, first_own, own, 0)
    my_counts = lax.dynamic_slice_in_dim(counts, first_own, own, 0)
    my_cotangent = lax.dynamic_slice_in_dim(cotangent, first_own, own, 0)
    hit = my_places[:, :, None] == jnp.arange(length, dtype=jnp.int32)[None, None, :]
    hit_low = hit.astype(bf16)
    live = jnp.arange(slots, dtype=jnp.int32)[None, :] < my_counts[:, None]

    query_heads = query_low.reshape(own, length, head_count, head_size)
    key_heads = key_low.reshape(own, length, head_count, head_size)
    value_heads = value_low.reshape(own, length, head_count, head_size)

    def softmax_of(query_part):
        scores = (
            jnp.einsum("sqhe,skhe->shqk", query_part, key_heads, preferred_element_type=f32)
        )
        exponent = jnp.exp(scores - jnp.max(scores, -1, keepdims=True))
        return exponent / jnp.sum(exponent, -1, keepdims=True)

    def feed_of(active):
        return jnp.dot(active, out_full, preferred_element_type=f32) + bias_feed

    feed_all = feed_of(results[9].reshape(rows, -1))
    output = layer_norm(norm_all + feed_all, gain_two, shift_two)
    output = lax.all_to_all(
        output.astype(bf16).reshape(own, length, model_width), "seq", 1, 0, tiled=True
    ).astype(f32)

    feed_out = feed_of(active_low)
    _, second_pull = jax.vjp(layer_norm, first_norm + feed_out, gain_two, shift_two)
    slot_grad = jnp.where(live[:, :, None], my_cotangent, 0.0).reshape(own * slots, model_width)
    grad_sum_two, grad_gain_two, grad_shift_two = second_pull(slot_grad)
    feed_back = grad_sum_two.astype(bf16)
    grad_bias_feed = column_sum(feed_back)
    grad_out_matrix = jnp.einsum("rf,rd->fd", active_low, feed_back, preferred_element_type=f32)
    grad_active = jnp.einsum("rd,fd->rf", feed_back, out_full, preferred_element_type=f32)
    inner_back = (grad_active * slope).astype(bf16)
    grad_bias_inner = column_sum(inner_back)
    grad_in_matrix = jnp.einsum("rd,rf->df", first_low, inner_back, preferred_element_type=f32)
    grad_first = grad_sum_two + jnp.einsum(
        "rf,df->rd", inner_back, in_full, preferred_element_type=f32
    )
    scaled = grad_first * gain_one
    grad_sum_one = inverse_one * (
        scaled
        - jnp.mean(scaled, -1, keepdims=True)
        - normal_one * jnp.mean(scaled * normal_one, -1, keepdims=True)
    )
    grad_gain_one = column_sum(grad_first * normal_one)
    grad_shift_one = column_sum(grad_first)
    attended_back = grad_sum_one.astype(bf16)
    grad_bias_out = column_sum(attended_back)
    grad_attn_out = jnp.einsum(
        "rd,re->de", context_slot, attended_back, preferred_element_type=f32
    )
    context_back = jnp.einsum(
        "re,de->rd", attended_back, attn_full[3], preferred_element_type=f32
    ).astype(bf16)
    context_back = context_back.reshape(own, slots, head_count, head_size)
    query_slot = query_slot.reshape(own, slots, head_count, head_size)
    attn_probs = softmax_of(query_slot)
    probs_low = attn_probs.astype(bf16)
    grad_probs = jnp.einsum(
        "sqhe,skhe->shqk", context_back, value_heads, preferred_element_type=f32
    )
    row_delta = jnp.sum(attn_probs * grad_probs, -1, keepdims=True)
    scores_back = (attn_probs * (grad_probs - row_delta)).astype(bf16)
    query_back = (
        (
            jnp.einsum("shqk,skhe->sqhe", scores_back, key_heads, preferred_element_type=f32)
            * score_scale
        )
        .reshape(own * slots, model_width)
        .astype(bf16)
    )
    value_back = jnp.einsum("shqk,sqhe->skhe", probs_low, context_back, preferred_element_type=f32)
    value_back = value_back.astype(bf16).reshape(rows, model_width)
    key_back = (
        jnp.einsum("shqk,sqhe->skhe", scores_back, query_slot, preferred_element_type=f32)
    )
    key_back = key_back.astype(bf16).reshape(rows, model_width)
    grad_qkv = jnp.stack(
        [
            jnp.einsum("rd,re->de", token_slot_low, query_back, preferred_element_type=f32),
            jnp.einsum("rd,re->de", flat_low, key_back, preferred_element_type=f32),
            jnp.einsum("rd,re->de", flat_low, value_back, preferred_element_type=f32),
        ]
    )
    slot_tokens = grad_sum_one + jnp.einsum(
        "re,de->rd", query_back, attn_full[0], preferred_element_type=f32
    )
    slot_high = slot_tokens.astype(bf16)
    slot_rest = (slot_tokens - slot_high.astype(f32)).astype(bf16)

    def spread(part):
        return jnp.einsum(
            "sjl,sjd->sld",
            hit_low,
            part.reshape(own, slots, model_width),
            preferred_element_type=f32,
        )

    grad_tokens = (
        spread(slot_high)
        + spread(slot_rest)
        + (
            jnp.einsum("re,de->rd", key_back, attn_full[1], preferred_element_type=f32)
            + jnp.einsum("re,de->rd", value_back, attn_full[2], preferred_element_type=f32)
        ).reshape(own, length, model_width)
    )
    grad_tokens = lax.all_to_all(
        grad_tokens.astype(bf16), "seq", 1, 0, tiled=True
    ).astype(f32)
    grad_attn_all = jnp.concatenate([grad_qkv, grad_attn_out[None]], 0)
    grad_vector_all = jnp.concatenate(
        [
            column_sum(query_back),
            column_sum(value_back),
            grad_bias_out,
            grad_bias_feed,
            grad_gain_one,
            grad_shift_one,
            grad_gain_two,
            grad_shift_two,
            grad_bias_inner,
        ]
    )

    def scatter(part, axis):
        return lax.psum_scatter(
            part.astype(bf16), ("seq", "dp"), scatter_dimension=axis, tiled=True
        ).astype(f32)

    shares = (
        scatter(grad_attn_all, 1),
        scatter(grad_in_matrix, 0),
        scatter(grad_out_matrix, 0),
        scatter(grad_vector_all, 0),
    )
    square_sum = lax.psum(sum((jnp.sum(total * total) for total in shares)), ("seq", "dp"))
    grad_norm = jnp.sqrt(square_sum)
    clip_factor = 1.0 / jnp.maximum(grad_norm, 1.0)
    clipped = tuple((share * clip_factor for share in shares))
    params = (attn_weights, ffn_in, ffn_out, vectors)
    firsts = (attn_first, ffn_in_first, ffn_out_first, vector_first)
    seconds = (attn_second, ffn_in_second, ffn_out_second, vector_second)
    moved = [adam_direction(firsts[index], seconds[index], clipped[index]) for index in range(4)]
    directions = [moved[index][2] + weight_decay * params[index] for index in range(3)]
    weight_sq = jnp.concatenate(
        [
            jnp.sum(attn_weights * attn_weights, axis=(1, 2)),
            jnp.sum(ffn_in * ffn_in)[None],
            jnp.sum(ffn_out * ffn_out)[None],
        ]
    )
    dir_sq = jnp.concatenate(
        [
            jnp.sum(directions[0] * directions[0], axis=(1, 2)),
            jnp.sum(directions[1] * directions[1])[None],
            jnp.sum(directions[2] * directions[2])[None],
        ]
    )
    lamb_sq = lax.psum(jnp.stack([weight_sq, dir_sq]), ("seq", "dp"))
    lamb_norms = jnp.sqrt(lamb_sq)
    trust_ratio = lamb_norms[0] / lamb_norms[1]
    new_attn = attn_weights - step_rate * trust_ratio[:4, None, None] * directions[0]
    new_ffn_in = ffn_in - step_rate * trust_ratio[4] * directions[1]
    new_ffn_out = ffn_out - step_rate * trust_ratio[5] * directions[2]
    new_vectors = vectors - step_rate * moved[3][2]
    return (
        output,
        grad_tokens,
        clipped[0],
        clipped[1],
        clipped[2],
        clipped[3],
        moved[0][0],
        moved[1][0],
        moved[2][0],
        moved[3][0],
        moved[0][1],
        moved[1][1],
        moved[2][1],
        moved[3][1],
        new_attn,
        new_ffn_in,
        new_ffn_out,
        new_vectors,
        new_attn.astype(bf16),
        new_ffn_in.astype(bf16),
        new_ffn_out.astype(bf16),
        lamb_norms,
        trust_ratio,
        grad_norm,
    )


def solution(mesh):
    return jax.shard_map(
        functools.partial(body, mesh),
        mesh=mesh,
        in_specs=(
            P("dp", "seq", None),
            P("dp", None),
            P("dp"),
            P("dp", None, None),
            P(None, ("seq", "dp"), None),
            P(("seq", "dp"), None),
            P(("seq", "dp"), None),
            P(("seq", "dp")),
            P(None, ("seq", "dp"), None),
            P(("seq", "dp"), None),
            P(("seq", "dp"), None),
            P(("seq", "dp")),
            P(None, ("seq", "dp"), None),
            P(("seq", "dp"), None),
            P(("seq", "dp"), None),
            P(("seq", "dp")),
        ),
        out_specs=(
            P("dp", "seq", None),
            P("dp", "seq", None),
            P(None, ("seq", "dp"), None),
            P(("seq", "dp"), None),
            P(("seq", "dp"), None),
            P(("seq", "dp")),
            P(None, ("seq", "dp"), None),
            P(("seq", "dp"), None),
            P(("seq", "dp"), None),
            P(("seq", "dp")),
            P(None, ("seq", "dp"), None),
            P(("seq", "dp"), None),
            P(("seq", "dp"), None),
            P(("seq", "dp")),
            P(None, ("seq", "dp"), None),
            P(("seq", "dp"), None),
            P(("seq", "dp"), None),
            P(("seq", "dp")),
            P(None, ("seq", "dp"), None),
            P(("seq", "dp"), None),
            P(("seq", "dp"), None),
            P(),
            P(),
            P(),
        ),
        check_vma=False,
    )
```

```python
import functools
import jax
import jax.numpy as jnp
from jax import lax
from jax.sharding import PartitionSpec as P
from jax.experimental import pallas as pl
from jax.experimental.pallas import tpu as pltpu

H = 12
HD = 64
STEP = 5

decay_rate = 0.5
step_rate = 0.3
weight_decay = 0.01
adam_eps = 1e-06
norm_eps = 1e-12
f32 = jnp.float32
bf16 = jnp.bfloat16
MESH = pl.DeviceIdType.MESH


class Place:
    def __init__(self, mesh, shard_rows):
        self.seq = mesh.shape["seq"]
        self.dp = mesh.shape["dp"]
        self.merge = 2
        while (self.merge * shard_rows) % 16:
            self.merge *= 2
        self.seq_bits = self.seq.bit_length() - 1
        self.far_bits = (self.dp // self.merge).bit_length() - 1
        self.bits = self.seq_bits + self.far_bits
        self.groups = self.seq * self.dp // self.merge
        self.devices = self.seq * self.dp
        self.levels = self.devices.bit_length() - 1

    def here(self):
        self.s = lax.axis_index("seq")
        self.d = lax.axis_index("dp")
        self.member = lax.rem(self.d, self.merge)
        self.core = lax.rem(self.d, 2)
        self.weight = []
        self.bit = []
        for dim in range(self.bits):
            if dim < self.seq_bits:
                w = 1 << (self.seq_bits - 1 - dim)
                self.bit.append(lax.rem(self.s // w, 2))
            else:
                w = self.merge << (self.bits - 1 - dim)
                self.bit.append(lax.rem(self.d // w, 2))
            self.weight.append(w)

    def across(self, dim):
        flip = self.weight[dim] * (1 - 2 * self.bit[dim])
        if dim < self.seq_bits:
            return (self.s + flip, self.d)
        return (self.s, self.d + flip)

    def other_core(self):
        return (self.s, self.d + 1 - 2 * self.core)

    def mates(self):
        base = self.d - self.member
        return [
            (self.s, base + lax.rem(self.member + k, self.merge)) for k in range(1, self.merge)
        ]

    def row_mates(self):
        return [(lax.rem(self.s + k, self.seq), self.d) for k in range(1, self.seq)]

    def greet(self):
        barrier = pltpu.get_barrier_semaphore()
        everyone = self.mates() + self.row_mates()
        everyone += [self.across(dim) for dim in range(self.seq_bits, self.bits)]
        for device in everyone:
            pl.semaphore_signal(barrier, inc=1, device_id=device, device_id_type=MESH)
        pl.semaphore_wait(barrier, len(everyone))

    def greet_all(self):
        barrier = pltpu.get_barrier_semaphore()
        me = self.s * self.dp + self.d

        def signal(k, _):
            other = lax.rem(me + k, self.devices)
            device = (other // self.dp, lax.rem(other, self.dp))
            pl.semaphore_signal(barrier, inc=1, device_id=device, device_id_type=MESH)
            return 0

        lax.fori_loop(1, self.devices, signal, 0)
        pl.semaphore_wait(barrier, self.devices - 1)

    def partner(self, level):
        inside = self.levels - self.bits
        if level >= inside:
            return self.across(level - inside)
        w = 1 << level
        return (self.s, self.d + w * (1 - 2 * lax.rem(self.d // w, 2)))

    def box(self, free):
        return tuple(slice(None) if dim in free else self.bit[dim] for dim in range(self.bits))


def erf(x):
    x = jnp.clip(x, -3.832506856900711, 3.832506856900711)
    x2 = x * x
    top = jnp.float32(0.00022905065861350646)
    for c in (
        0.0034082910107109506,
        0.050955695062380861,
        0.18520832239976145,
        1.128379143519084,
    ):
        top = top * x2 + jnp.float32(c)
    low = jnp.float32(-1.1791602954361697e-7)
    for c in (
        0.000023547966471313185,
        0.0010179625278914885,
        0.014070470171167667,
        0.11098505178285362,
        0.49746925110067538,
        1.0,
    ):
        low = low * x2 + jnp.float32(c)
    return x * top / low


def dot(a, b):
    return jnp.dot(a, b, preferred_element_type=f32)


def dot_t(a, b):
    return lax.dot_general(a, b, (((1,), (1,)), ((), ())), preferred_element_type=f32)


def t_dot(a, b):
    return lax.dot_general(a, b, (((0,), (0,)), ((), ())), preferred_element_type=f32)


def normalize(x):
    center = x - jnp.mean(x, -1, keepdims=True)
    inverse = lax.rsqrt(jnp.mean(center * center, -1, keepdims=True) + norm_eps)
    return center * inverse, inverse


class Flows:
    def __init__(self, place, chunks, send, recv):
        self.place = place
        self.chunks = chunks
        self.send = send
        self.recv = recv
        self.stages = place.bits

    def number(self, chunk, part, stage):
        return (chunk * 3 + part) * (self.stages + 1) + stage


class Gather(Flows):
    def copy(self, chunk, part, stage):
        place = self.place
        buf, rows, columns, order = self.chunks[chunk].part(part, place)
        n = self.number(chunk, part, stage)
        box = place.box(order[:stage]) + (rows, columns)
        return pltpu.make_async_remote_copy(
            src_ref=buf.at[box],
            dst_ref=buf.at[box],
            send_sem=self.send.at[n],
            recv_sem=self.recv.at[n],
            device_id=place.across(order[stage]),
            device_id_type=MESH,
        )

    def hand(self, chunk):
        place = self.place
        buf, rows, columns = self.chunks[chunk].half(place)
        n = self.number(chunk, 0, self.stages)
        box = tuple(slice(None) for _ in range(place.bits)) + (rows, columns)
        return pltpu.make_async_remote_copy(
            src_ref=buf.at[box],
            dst_ref=buf.at[box],
            send_sem=self.send.at[n],
            recv_sem=self.recv.at[n],
            device_id=place.other_core(),
            device_id_type=MESH,
        )

    def step(self, t):
        for chunk in range(len(self.chunks)):
            stage = t - chunk
            if 0 <= stage <= self.stages:
                for part in range(3):
                    if stage > 0:
                        self.copy(chunk, part, stage - 1).wait_recv()
                    if stage < self.stages:
                        self.copy(chunk, part, stage).start()
                if stage == self.stages:
                    self.hand(chunk).start()
            if stage == self.stages + 1:
                self.hand(chunk).wait_recv()

    def last_step(self, chunk):
        return chunk + self.stages + 1

    def finish(self):
        for chunk in range(len(self.chunks)):
            for part in range(3):
                for stage in range(self.stages):
                    self.copy(chunk, part, stage).wait_send()
            self.hand(chunk).wait_send()


class Chunk:
    def __init__(self, buf, first, width, orders, cuts=None):
        self.buf, self.first, self.width, self.orders, self.cuts = buf, first, width, orders, cuts

    def half(self, place):
        half = self.width // 2
        start = pl.multiple_of(self.first + place.core * half, 128)
        return self.buf, slice(None), pl.ds(start, half)

    def part(self, part, place):
        half = self.width // 2
        if self.cuts is None:
            third = half // 3
            start = pl.multiple_of(self.first + place.core * half + part * third, 128)
            return self.buf, slice(None), pl.ds(start, third), self.orders[part]
        start = pl.multiple_of(self.first + place.core * half, 128)
        rows = pl.ds(self.cuts[part], self.cuts[part + 1] - self.cuts[part])
        return self.buf, rows, pl.ds(start, half), self.orders[part]


def weight_chunks(place, attn, first_ffn, second_ffn, reverse):
    seq = list(range(place.seq_bits))
    far = list(range(place.seq_bits, place.bits))[::-1]
    left = far + seq[::-1]
    right = far + seq
    chunks = []

    def orders(index):
        a, b = (seq, seq[::-1]) if index % 2 else (seq[::-1], seq)
        if index % 4 < 2:
            third = a + far
        else:
            third = a[:1] + far + a[1:]
        out = [left, right, third]
        return [order[::-1] for order in out] if reverse else out

    width = attn.shape[-1]
    for m in range(4):
        chunks.append(Chunk(attn.at[m], 0, width, orders(m)))
    for j in range(first_ffn.shape[-1] // width):
        chunks.append(Chunk(first_ffn, j * width, width, orders(j)))
    rows = second_ffn.shape[-2]
    third = rows // 3 // 16 * 16
    for j in range(3):
        chunks.append(
            Chunk(second_ffn, j * width // 3, width // 3, orders(j), (0, third, 2 * third, rows))
        )
    return chunks


def forward_kernel(
    place,
    vec_rows,
    vec_count,
    tokens_ref,
    places_ref,
    attn_ref,
    in_ref,
    out_ref,
    vec_ref,
    attn_hbm,
    in_hbm,
    out_hbm,
    vec_hbm,
    high_hbm,
    query_hbm,
    key_hbm,
    value_hbm,
    norm_hbm,
    active_hbm,
    slot_low_hbm,
    slot_hbm,
    slot_active_hbm,
    slot_slope_hbm,
    attn_buf,
    in_buf,
    out_buf,
    vec_buf,
    vec_acc,
    vec,
    attn_in,
    in_in,
    out_in,
    joined,
    send_high,
    send_rest,
    high,
    rest,
    query,
    key,
    value,
    norm,
    active,
    slot_low,
    slot,
    slot_active,
    slot_slope,
    flow_send,
    flow_recv,
    mate_send,
    mate_recv,
    local_sem,
    token_send,
    token_recv,
    vec_send,
    vec_recv,
    save_sem,
):
    place.here()
    place.greet()
    merge, seq = place.merge, place.seq
    width = tokens_ref.shape[-1]
    block = tokens_ref.shape[1]
    own = tokens_ref.shape[0] // seq
    length = block * seq
    rows = own * length
    slots = places_ref.shape[1]
    mine = place.box(())

    sources = (attn_ref, in_ref, out_ref)
    stages = (attn_in, in_in, out_in)
    mate_copies = []
    for index in range(3):
        for k, device in enumerate(place.mates()):
            n = index * (merge - 1) + k
            copy = pltpu.make_async_remote_copy(
                src_ref=sources[index],
                dst_ref=stages[index].at[place.member],
                send_sem=mate_send.at[n],
                recv_sem=mate_recv.at[n],
                device_id=device,
                device_id_type=MESH,
            )
            copy.start()
            mate_copies.append(copy)
    local = []
    for index in range(3):
        copy = pltpu.make_async_copy(
            sources[index], stages[index].at[place.member], local_sem.at[index]
        )
        copy.start()
        local.append(copy)
    vec_mates = []
    vec_buf.at[mine][place.member] = vec_ref[...]
    for k, device in enumerate(place.mates()):
        copy = pltpu.make_async_remote_copy(
            src_ref=vec_ref,
            dst_ref=vec_buf.at[mine].at[place.member],
            send_sem=vec_send.at[k],
            recv_sem=vec_recv.at[k],
            device_id=device,
            device_id_type=MESH,
        )
        copy.start()
        vec_mates.append(copy)

    def split(i, _):
        x = tokens_ref[i]
        top = x.astype(bf16)
        send_high[i] = top
        send_rest[i] = (x - top.astype(f32)).astype(bf16)
        return 0

    lax.fori_loop(0, own * seq, split, 0)
    token_copies = []
    my_columns = pl.ds(pl.multiple_of(place.s * block, block), block)
    for half, (source, target) in enumerate(((send_high, high), (send_rest, rest))):
        for k, device in enumerate(place.row_mates()):
            n = half * (seq - 1) + k
            token_copies.append(
                pltpu.make_async_remote_copy(
                    src_ref=source.at[pl.ds(device[0] * own, own)],
                    dst_ref=target.at[:, my_columns],
                    send_sem=token_send.at[n],
                    recv_sem=token_recv.at[n],
                    device_id=device,
                    device_id_type=MESH,
                )
            )
        target.at[:, my_columns][...] = source[pl.ds(place.s * own, own)]
    for copy in token_copies[: seq - 1]:
        copy.start()

    flows = Gather(place, weight_chunks(place, attn_buf, in_buf, out_buf, False), flow_send, flow_recv)

    def join(chunks, part):
        count = part.shape[1]
        for i in range(merge):
            joined[i * count : (i + 1) * count, : part.shape[-1]] = part[i]
        for chunk in chunks:
            buf, _, columns = chunk.half(place)
            buf.at[mine + (slice(None), columns)][...] = joined[: merge * count, columns].astype(bf16)

    for k in range(3):
        local[k].wait()
        for copy in mate_copies[k * (merge - 1) : (k + 1) * (merge - 1)]:
            copy.wait_recv()
        if k == 0:
            for m in range(4):
                join(flows.chunks[m : m + 1], attn_in.at[:, m])
        elif k == 1:
            join(flows.chunks[4:-3], in_in)
        else:
            join(flows.chunks[-3:], out_in)

    def vec_copy(stage):
        order = list(range(place.bits))
        box = place.box(order[:stage])
        return pltpu.make_async_remote_copy(
            src_ref=vec_buf.at[box],
            dst_ref=vec_buf.at[box],
            send_sem=vec_send.at[merge - 1 + stage],
            recv_sem=vec_recv.at[merge - 1 + stage],
            device_id=place.across(order[stage]),
            device_id_type=MESH,
        )

    for copy in vec_mates:
        copy.wait_recv()
    vec_copy(0).start()
    flows.step(0)
    for t in range(1, flows.stages + 1):
        vec_copy(t - 1).wait_recv()
        if t < flows.stages:
            vec_copy(t).start()
        flows.step(t)
    for copy in token_copies[seq - 1 :]:
        copy.start()

    vec_acc[...] = jnp.zeros_like(vec_acc)
    for owner in range(place.devices):
        group, member = divmod(owner, merge)
        bits = tuple((group >> (place.bits - 1 - dim)) & 1 for dim in range(place.bits))
        first, shift = divmod(vec_count * owner, 128)
        count = (shift + vec_count + 127) // 128
        vec_acc[first : first + count] += vec_buf.at[bits][member, :count]
    per = width // 128
    vec_acc[...] = vec_acc[...].astype(bf16).astype(f32)
    for row in range(vec_rows):
        vec[row : row + 1] = jnp.concatenate(
            [vec_acc[row * per + k : row * per + k + 1] for k in range(per)], axis=1
        )
    saves = []

    def save(source, target):
        copy = pltpu.make_async_copy(source, target, save_sem.at[len(saves)])
        copy.start()
        saves.append(copy)

    save(vec, vec_hbm)

    for copy in token_copies[: seq - 1]:
        copy.wait_recv()
    tile = min(256, length)
    per_seq = length // tile
    save(high, high_hbm)
    scale = HD**-0.5

    for m, target in enumerate((query, key, value)):
        flows.step(flows.last_step(m))
        matrix = attn_buf.at[m].reshape(width, width)

        def project(i, _):
            sequence, at = i // per_seq, pl.ds(pl.multiple_of(lax.rem(i, per_seq) * tile, tile), tile)
            result = dot(high[sequence, at], matrix[...])
            if m == 0:
                result = (result + vec[0:1]).astype(bf16) * scale
            elif m == 2:
                result = result + vec[1:2]
            target[sequence, at] = result.astype(bf16)
            return 0

        lax.fori_loop(0, own * per_seq, project, 0)
        save(target, (query_hbm, key_hbm, value_hbm)[m])

    context = send_high.reshape(own, length, width)
    for copy in token_copies[: seq - 1]:
        copy.wait_send()
    pairs = width // 128
    turns = own * pairs
    lane = lax.broadcasted_iota(jnp.int32, (1, 128), 1)

    def attend(i, _):
        for k in range(3):
            @pl.when(i == (k + 1) * turns // 4)
            def _():
                flows.step(flows.last_step(3 + k))

        sequence, pair = i // pairs, lax.rem(i, pairs)
        at = pl.ds(pl.multiple_of(pair * 128, 128), 128)
        keys, values = key[sequence, :, at], value[sequence, :, at]
        for q in range(per_seq):
            places = slice(q * tile, (q + 1) * tile)
            queries = query[sequence, places, at]
            heads = []
            for head in range(2):
                picked = jnp.where(lane // HD == head, queries, jnp.zeros_like(queries))
                scores = dot_t(picked, keys)
                exponent = jnp.exp(scores - jnp.max(scores, -1, keepdims=True))
                total = jnp.sum(exponent, -1, keepdims=True)
                heads.append(dot(exponent.astype(bf16), values) / total)
            context[sequence, places, at] = jnp.where(lane < HD, heads[0], heads[1]).astype(bf16)
        return 0

    lax.fori_loop(0, turns, attend, 0)
    flows.step(flows.last_step(6))

    for copy in token_copies[seq - 1 :]:
        copy.wait_recv()
    out_matrix = attn_buf.at[3].reshape(width, width)

    def front(i, _):
        sequence, at = i // per_seq, pl.ds(pl.multiple_of(lax.rem(i, per_seq) * tile, tile), tile)
        x = high[sequence, at].astype(f32) + rest[sequence, at].astype(f32)
        x = x + (dot(context[sequence, at], out_matrix[...]) + vec[2:3])
        x, _ = normalize(x)
        norm[sequence, at] = x * vec[4:5] + vec[5:6]
        return 0

    lax.fori_loop(0, own * per_seq, front, 0)
    save(norm, norm_hbm)

    place_ids = lax.broadcasted_iota(jnp.int32, (length, slots), 0)
    for sequence in range(own):
        at = pl.ds(sequence * slots, slots)
        hits = places_ref[pl.ds(place.s * own + sequence, 1)] == place_ids
        hits = jnp.where(hits, 1.0, 0.0).astype(bf16)
        slot_high = t_dot(hits, high[sequence])
        slot_low[0, at] = slot_high.astype(bf16)
        slot_context = t_dot(hits, context[sequence]).astype(bf16)
        slot_low[1, at] = slot_context
        slot_low[2, at] = t_dot(hits, query[sequence]).astype(bf16)
        slot[0, at] = slot_high
        slot[1, at] = t_dot(hits, rest[sequence])
        x = slot[0, at] + slot[1, at]
        x = x + (dot(slot_context, out_matrix[...]) + vec[2:3])
        x, inverse = normalize(x)
        slot[0, at] = x
        slot[2, at] = jnp.broadcast_to(inverse, x.shape)
        x = x * vec[4:5] + vec[5:6]
        slot[1, at] = x
        slot_low[3, at] = x.astype(bf16)
    save(slot_low, slot_low_hbm)
    save(slot, slot_hbm)
    save(attn_buf, attn_hbm)

    in_matrix = in_buf.reshape(width, in_buf.shape[-1])
    for j in range(in_buf.shape[-1] // width):
        if j > 0:
            flows.step(flows.last_step(6 + j))
        at = pl.ds(j * width, width)
        bias = vec[8 + j : 9 + j]

        def hidden(i, _):
            sequence, here = i // per_seq, pl.ds(pl.multiple_of(lax.rem(i, per_seq) * tile, tile), tile)
            x = dot(norm[sequence, here].astype(bf16), in_matrix[:, at]) + bias
            active[sequence, here, at] = (0.5 * x * (1.0 + erf(x * 0.5**0.5))).astype(bf16)
            return 0

        lax.fori_loop(0, own * per_seq, hidden, 0)
        x = dot(slot_low[3], in_matrix[:, at]) + bias
        half = 0.5 * (1.0 + erf(x * 0.5**0.5))
        slot_active[:, at] = (x * half).astype(bf16)
        slot_slope[:, at] = half + x * jnp.exp(-0.5 * x * x) * 0.3989422804014327
    save(active, active_hbm)
    save(slot_active, slot_active_hbm)
    save(slot_slope, slot_slope_hbm)
    save(in_buf, in_hbm)
    for t in range(flows.last_step(9) + 1, flows.last_step(len(flows.chunks) - 1) + 1):
        flows.step(t)
    save(out_buf, out_hbm)
    flows.finish()
    for copy in mate_copies + vec_mates + token_copies[seq - 1 :]:
        copy.wait_send()
    for stage in range(flows.stages):
        vec_copy(stage).wait_send()
    for copy in saves:
        copy.wait()


def forward_call(mesh, tokens, positions, attn_weights, ffn_in, ffn_out, vectors):
    place = Place(mesh, ffn_in.shape[0])
    sequences, block, width = tokens.shape
    inner = ffn_in.shape[1]
    slots = positions.shape[1]
    own = sequences // place.seq
    length = block * place.seq
    vec_count = vectors.shape[0]
    vec_rows = vec_count * place.devices // width
    owner = lax.axis_index("seq") * place.dp + lax.axis_index("dp")
    padded = lax.dynamic_update_slice_in_dim(
        jnp.zeros((1024,), f32), vectors.astype(bf16).astype(f32), lax.rem(vec_count * owner, 128), 0
    ).reshape(8, 128)
    bits = (2,) * place.bits
    r = ffn_in.shape[0]
    joint = r * place.merge
    joint_out = ffn_out.shape[0] * place.merge
    flow_count = (4 + inner // width + 3) * 3 * (place.bits + 1)
    attn_shape = (4,) + bits + (joint, width)
    in_shape = bits + (joint, inner)
    out_shape = bits + (joint_out, width)
    seq_shape = (own, length, width)
    rows = own * slots
    results = [
        (attn_shape, bf16),
        (in_shape, bf16),
        (out_shape, bf16),
        ((16, width), f32),
        (seq_shape, bf16),
        (seq_shape, bf16),
        (seq_shape, bf16),
        (seq_shape, bf16),
        (seq_shape, f32),
        ((own, length, inner), bf16),
        ((4, rows, width), bf16),
        ((3, rows, width), f32),
        ((rows, inner), bf16),
        ((rows, inner), f32),
    ]
    vmem = pl.BlockSpec(memory_space=pltpu.VMEM)
    hbm = pl.BlockSpec(memory_space=pl.ANY)
    dma = pltpu.SemaphoreType.DMA
    mates = place.merge - 1
    return pl.pallas_call(
        functools.partial(forward_kernel, place, vec_rows, vec_count),
        out_shape=[jax.ShapeDtypeStruct(*one) for one in results],
        in_specs=[vmem, vmem, hbm, hbm, hbm, vmem],
        out_specs=[hbm] * len(results),
        scratch_shapes=[
            pltpu.VMEM(attn_shape, bf16),
            pltpu.VMEM(in_shape, bf16),
            pltpu.VMEM(out_shape, bf16),
            pltpu.VMEM(bits + (place.merge, 8, 128), f32),
            pltpu.VMEM((vec_rows * width // 128 + 8, 128), f32),
            pltpu.VMEM((16, width), f32),
            pltpu.VMEM((place.merge,) + attn_weights.shape, f32),
            pltpu.VMEM((place.merge,) + ffn_in.shape, f32),
            pltpu.VMEM((place.merge,) + ffn_out.shape, f32),
            pltpu.VMEM((joint_out, inner), f32),
            pltpu.VMEM((sequences, block, width), bf16),
            pltpu.VMEM((sequences, block, width), bf16),
            pltpu.VMEM(seq_shape, bf16),
            pltpu.VMEM(seq_shape, bf16),
            pltpu.VMEM(seq_shape, bf16),
            pltpu.VMEM(seq_shape, bf16),
            pltpu.VMEM(seq_shape, bf16),
            pltpu.VMEM(seq_shape, f32),
            pltpu.VMEM((own, length, inner), bf16),
            pltpu.VMEM((4, rows, width), bf16),
            pltpu.VMEM((3, rows, width), f32),
            pltpu.VMEM((rows, inner), bf16),
            pltpu.VMEM((rows, inner), f32),
            dma((flow_count,)),
            dma((flow_count,)),
            dma((3 * mates,)),
            dma((3 * mates,)),
            dma((3,)),
            dma((2 * (place.seq - 1),)),
            dma((2 * (place.seq - 1),)),
            dma((mates + place.bits,)),
            dma((mates + place.bits,)),
            dma((len(results),)),
        ],
        compiler_params=pltpu.CompilerParams(
            collective_id=0, has_side_effects=True, vmem_limit_bytes=64 * 2**20 - 2**18
        ),
    )(tokens, positions, attn_weights, ffn_in, ffn_out, padded)


class Scatter(Flows):
    def __init__(self, place, chunks, send, recv, landings, finals):
        super().__init__(place, chunks, send, recv)
        self.landings = landings
        self.finals = finals

    def boxes(self, order, stage):
        place = self.place
        done = order[:stage]
        dim = order[stage]
        out, mine, came = [], [], []
        for d in range(place.bits):
            if d in done:
                picks = (place.bit[d],) * 3
            elif d == dim:
                picks = (1 - place.bit[d], place.bit[d], 1 - place.bit[d])
            else:
                picks = (slice(None),) * 3
            out.append(picks[0])
            mine.append(picks[1])
            came.append(picks[2])
        return tuple(out), tuple(mine), tuple(came)

    def copy(self, chunk, part, stage):
        buf, rows, columns, order = self.chunks[chunk].part(part, self.place)
        n = self.number(chunk, part, stage)
        out, mine, _ = self.boxes(order, stage)
        return pltpu.make_async_remote_copy(
            src_ref=buf.at[out + (rows, columns)],
            dst_ref=self.landings[chunk].at[mine + (rows, columns)],
            send_sem=self.send.at[n],
            recv_sem=self.recv.at[n],
            device_id=self.place.across(order[stage]),
            device_id_type=MESH,
        )

    def begin(self, *chunks):
        for chunk in chunks:
            for part in range(3):
                self.copy(chunk, part, 0).start()

    def advance(self, chunk, stage):
        for part in range(3):
            self.copy(chunk, part, stage).wait_recv()
            buf, rows, columns, order = self.chunks[chunk].part(part, self.place)
            _, mine, came = self.boxes(order, stage)
            tail = (rows, columns)
            total = buf.at[mine + tail][...].astype(f32)
            total = total + self.landings[chunk].at[came + tail][...].astype(f32)
            if stage + 1 < self.stages:
                buf.at[mine + tail][...] = total.astype(bf16)
                self.copy(chunk, part, stage + 1).start()
            else:
                self.finals[chunk].at[tail][...] = total

    def finish(self):
        for chunk in range(len(self.chunks)):
            for part in range(3):
                for stage in range(self.stages):
                    self.copy(chunk, part, stage).wait_send()


class Part:
    def __init__(self, buf, first, width, orders, cuts=None):
        self.buf, self.first, self.width, self.orders, self.cuts = buf, first, width, orders, cuts

    def part(self, part, place):
        if self.cuts is None:
            third = self.width // 3
            columns = pl.ds(self.first + part * third, third)
            return self.buf, slice(None), columns, self.orders[part]
        rows = pl.ds(self.cuts[part], self.cuts[part + 1] - self.cuts[part])
        return self.buf, rows, pl.ds(self.first, self.width), self.orders[part]


def gradient_chunks(place, attn, first_ffn, second_ffn):
    forward = weight_chunks(place, attn, first_ffn, second_ffn, True)
    half = attn.shape[-1]
    chunks = []
    for j in range(3):
        chunks.append(
            Part(second_ffn, j * half // 3, half // 3, forward[-3 + j].orders, forward[-3 + j].cuts)
        )
    for j in range(first_ffn.shape[-1] // half):
        chunks.append(Part(first_ffn, j * half, half, forward[4 + j].orders))
    for m in (3, 0, 1, 2):
        chunks.append(Part(attn.at[m], 0, half, forward[m].orders))
    return chunks


def column_total(x):
    return jnp.sum(x, axis=0, keepdims=True)


def backward_kernel(
    place,
    attn_hbm,
    in_hbm,
    out_hbm,
    vec,
    high_hbm,
    key_hbm,
    value_hbm,
    norm_hbm,
    active_hbm,
    slot_low_hbm,
    slot_hbm,
    slot_active_hbm,
    slot_slope_hbm,
    places_ref,
    counts_ref,
    cotangent_hbm,
    output_ref,
    grad_tokens_ref,
    final_attn_hbm,
    final_in_hbm,
    final_out_hbm,
    vec_grad_ref,
    square_ref,
    mats,
    last,
    out_buf,
    grad_attn,
    grad_in,
    grad_out,
    land_attn,
    land_in,
    land_out,
    final_attn,
    final_in,
    final_out,
    tokens_both,
    key,
    value,
    active_both,
    inner_both,
    slope,
    low_both,
    slot,
    feed_both,
    attended_both,
    query_both,
    context_back,
    sum_two,
    key_back,
    value_back,
    key_both,
    value_both,
    stage_tokens,
    stage_output,
    vec_sum,
    vec_land,
    square,
    square_land,
    flow_send,
    flow_recv,
    load_sem,
    pair_send,
    pair_recv,
    tile_sem,
    row_send,
    row_recv,
    own_sem,
    vec_send,
    vec_recv,
    final_send,
    final_recv,
    square_send,
    square_recv,
    extra_land=None,
    extra_send=None,
    extra_recv=None,
):
    place.here()
    place.greet_all()
    merge, seq = place.merge, place.seq
    width = out_buf.shape[-1]
    inner = active_both.shape[-1]
    half = width // 2
    own, length = key.shape[:2]
    block = length // seq
    slots = sum_two.shape[1]
    rows = own * slots
    tile = min(256, length)
    per_seq = length // tile
    scale = HD**-0.5
    my_half = pl.ds(pl.multiple_of(place.core * half, 128), half)
    other_half = pl.ds(pl.multiple_of((1 - place.core) * half, 128), half)
    loads = []
    pairs = []
    sum_one = slope.at[:rows, :width]
    norm_tile = [slope.at[:tile, pl.ds((1 + k) * width, width)] for k in range(2)]

    def load(source, target):
        copy = pltpu.make_async_copy(source, target, load_sem.at[len(loads)])
        copy.start()
        loads.append(copy)
        return copy

    def share(source, target):
        n = len(pairs)
        copy = pltpu.make_async_remote_copy(
            src_ref=source,
            dst_ref=target,
            send_sem=pair_send.at[n],
            recv_sem=pair_recv.at[n],
            device_id=place.other_core(),
            device_id_type=MESH,
        )
        copy.start()
        pairs.append(copy)
        return copy

    got_active = load(slot_active_hbm, active_both.at[0])
    got_out = load(out_hbm, out_buf)
    got_slot = load(slot_hbm, slot)
    got_cotangent = load(cotangent_hbm.at[pl.ds(place.s * own, own)], sum_two)
    came_active = share(slot_active_hbm, active_both.at[1])
    got_slope = load(slot_slope_hbm, slope.at[:rows])
    got_low = load(slot_low_hbm, low_both.at[0])
    came_low = share(slot_low_hbm, low_both.at[1])
    inner_parts = inner // width
    free = (slice(None),) * (place.bits + 1)
    got_in = [
        load(in_hbm.at[free + (pl.ds(j * width, width),)], mats.at[j]) for j in range(inner_parts)
    ]
    got_last = load(attn_hbm.at[3], last)
    got_key = load(key_hbm, key)
    got_value = load(value_hbm, value)
    got_tokens = load(high_hbm, tokens_both.at[0])
    came_tokens = share(high_hbm, tokens_both.at[1])

    chunks = gradient_chunks(place, grad_attn, grad_in, grad_out)
    finals = [final_out] * 3 + [final_in] * inner_parts * 2 + [final_attn.at[m] for m in (3, 0, 1, 2)]
    landings = [land_out] * 3 + [land_in] * inner_parts + [land_attn.at[m] for m in (3, 0, 1, 2)]
    finals = [final_out] * 3 + [final_in] * inner_parts + finals[-4:]
    flows = Scatter(place, chunks, flow_send, flow_recv, landings, finals)

    vec_sum[...] = jnp.zeros_like(vec_sum)
    got_active.wait()
    got_out.wait()
    got_slot.wait()
    got_cotangent.wait()
    out_matrix = out_buf.reshape(inner, width)
    x = slot[1] + (dot(active_both[0], out_matrix[...]) + vec[3:4])
    normal, inverse = normalize(x)
    for sequence in range(own):
        slot_ids = lax.broadcasted_iota(jnp.int32, (slots, 1), 0)
        live = slot_ids < counts_ref[place.s * own + sequence]
        sum_two[sequence] = jnp.where(live, sum_two[sequence], 0.0)
    grad = sum_two[...].reshape(rows, width)
    vec_sum[0, 6:7] = column_total(grad * normal)
    vec_sum[0, 7:8] = column_total(grad)
    grad = grad * vec[6:7]
    grad = inverse * (
        grad
        - jnp.mean(grad, -1, keepdims=True)
        - normal * jnp.mean(grad * normal, -1, keepdims=True)
    )
    sum_two[...] = grad.reshape(own, slots, width)
    feed_low = grad.astype(bf16)
    feed_both[0] = feed_low
    vec_sum[0, 3:4] = column_total(feed_low.astype(f32))
    came_feed = share(feed_both.at[0], feed_both.at[1])

    got_slope.wait()
    for j in range(inner_parts):
        at = pl.ds(j * width, width)
        back = dot_t(feed_both[0], out_matrix[at]) * slope[:rows, at]
        low = back.astype(bf16)
        inner_both[0, :, at] = low
        vec_sum[0, 8 + j : 9 + j] = column_total(low.astype(f32))
    came_inner = share(inner_both.at[0], inner_both.at[1])

    came_active.wait_recv()
    came_feed.wait_recv()
    all_active = active_both.reshape(2 * rows, inner)
    all_feed = feed_both.reshape(2 * rows, width)
    out_rows = grad_out.reshape(inner, half)

    def second_matrix(i, _):
        at = pl.ds(pl.multiple_of(i * half, 128), half)
        out_rows[at] = t_dot(all_active[:, at], all_feed[:, my_half]).astype(bf16)
        return 0

    lax.fori_loop(0, inner // half, second_matrix, 0)
    flows.begin(0, 1, 2)

    def tile_loads(i):
        sequence, at = i // per_seq, pl.ds(i % per_seq * tile, tile)
        return (
            pltpu.make_async_copy(norm_hbm.at[sequence, at], norm_tile[i % 2], tile_sem.at[i, 0]),
            pltpu.make_async_copy(
                active_hbm.at[sequence, at], active_both.at[i % 2], tile_sem.at[i, 1]
            ),
        )

    tiles = own * per_seq
    for i in range(min(2, tiles)):
        for copy in tile_loads(i):
            copy.start()

    got_low.wait()
    came_low.wait_recv()
    came_inner.wait_recv()
    all_inner = inner_both.reshape(2 * rows, inner)
    in_rows = grad_in.reshape(width, inner // 2)
    first_low = low_both[:, 3].reshape(2 * rows, width)
    for j in range(inner_parts):
        start = pl.multiple_of(place.core * (inner // 2) + j * half, 128)
        result = t_dot(first_low, all_inner[:, pl.ds(start, half)])
        in_rows[:, pl.ds(j * half, half)] = result.astype(bf16)
        flows.begin(3 + j)

    for copy in got_in:
        copy.wait()
    grad = sum_two[...].reshape(rows, width)
    for j in range(inner_parts):
        at = pl.ds(j * width, width)
        grad = grad + dot_t(inner_both[0, :, at], mats.at[j].reshape(width, width)[...])
    normal = slot[0]
    vec_sum[0, 4:5] = column_total(grad * normal)
    vec_sum[0, 5:6] = column_total(grad)
    grad = grad * vec[4:5]
    grad = slot[2] * (
        grad
        - jnp.mean(grad, -1, keepdims=True)
        - normal * jnp.mean(grad * normal, -1, keepdims=True)
    )
    sum_one[...] = grad
    low = grad.astype(bf16)
    attended_both[0] = low
    vec_sum[0, 2:3] = column_total(low.astype(f32))
    came_attended = share(attended_both.at[0], attended_both.at[1])
    got_attn = [load(attn_hbm.at[m], mats.at[m]) for m in range(3)]
    got_last.wait()
    context_back[...] = dot_t(low, last.reshape(width, width)[...]).astype(bf16)
    came_attended.wait_recv()
    result = t_dot(
        low_both[:, 1].reshape(2 * rows, width),
        attended_both.reshape(2 * rows, width)[:, my_half],
    )
    grad_attn.at[3].reshape(width, half)[...] = result.astype(bf16)
    flows.begin(3 + inner_parts)

    got_key.wait()
    got_value.wait()
    pair_count = width // 128
    turns = own * pair_count
    lane = lax.broadcasted_iota(jnp.int32, (1, 128), 1)
    during = [(0, 0), (1, 0), (0, 1), (2, 0), (1, 1), (3, 0), (0, 2), (2, 1)]

    def attend(i, _):
        for n, item in enumerate(during):
            @pl.when(i == n + 2)
            def _():
                flows.advance(*item)

        sequence, pair = i // pair_count, lax.rem(i, pair_count)
        at = pl.ds(pl.multiple_of(pair * 128, 128), 128)
        slot_at = pl.ds(pl.multiple_of(sequence * slots, slots), slots)
        keys, values = key[sequence, :, at], value[sequence, :, at]
        queries, backs = low_both[0, 2, slot_at, at], context_back[slot_at, at]
        zero = jnp.zeros_like(queries)
        outs = []
        for head in range(2):
            chosen = lane // HD == head
            scores = dot_t(jnp.where(chosen, queries, zero), keys)
            exponent = jnp.exp(scores - jnp.max(scores, -1, keepdims=True))
            probs = exponent / jnp.sum(exponent, -1, keepdims=True)
            grad_probs = dot_t(jnp.where(chosen, backs, zero), values)
            delta = jnp.sum(probs * grad_probs, -1, keepdims=True)
            scores_back = (probs * (grad_probs - delta)).astype(bf16)
            outs.append(
                (
                    dot(scores_back, keys) * scale,
                    t_dot(scores_back, queries),
                    t_dot(probs.astype(bf16), backs),
                )
            )
        left = lane < HD
        query_both[0, slot_at, at] = jnp.where(left, outs[0][0], outs[1][0]).astype(bf16)
        key_back[sequence, :, at] = jnp.where(left, outs[0][1], outs[1][1]).astype(bf16)
        value_back[sequence, :, at] = jnp.where(left, outs[0][2], outs[1][2]).astype(bf16)
        return 0

    lax.fori_loop(0, turns, attend, 0)
    came_query = share(query_both.at[0], query_both.at[1])
    came_key = share(key_back.at[:, :, other_half], key_both.at[1])
    came_value = share(value_back.at[:, :, other_half], value_both.at[1])
    key_both[0] = key_back[:, :, my_half]
    value_both[0] = value_back[:, :, my_half]
    total = jnp.zeros((1, width), f32)
    for sequence in range(own):
        total = total + column_total(value_back[sequence].astype(f32))
    vec_sum[0, 1:2] = total
    vec_sum[0, 0:1] = column_total(query_both[0].astype(f32))

    def vec_copy(stage):
        return pltpu.make_async_remote_copy(
            src_ref=vec_sum.at[stage],
            dst_ref=vec_land.at[stage],
            send_sem=vec_send.at[stage],
            recv_sem=vec_recv.at[stage],
            device_id=place.partner(stage),
            device_id_type=MESH,
        )

    vec_copy(0).start()

    def vec_next(stage):
        vec_copy(stage).wait_recv()
        vec_sum[stage + 1] = vec_sum[stage] + vec_land[stage]
        if stage + 1 < place.levels:
            vec_copy(stage + 1).start()

    came_query.wait_recv()
    result = t_dot(
        low_both[:, 0].reshape(2 * rows, width), query_both.reshape(2 * rows, width)[:, my_half]
    )
    grad_attn.at[0].reshape(width, half)[...] = result.astype(bf16)
    flows.begin(4 + inner_parts)
    got_tokens.wait()
    came_tokens.wait_recv()
    all_tokens = tokens_both.reshape(2 * own * length, width)
    for m, (came, both) in enumerate(((came_key, key_both), (came_value, value_both))):
        came.wait_recv()
        all_back = both.reshape(2 * own * length, half)
        target = grad_attn.at[1 + m].reshape(width, half)

        def weight(i, _):
            at = pl.ds(pl.multiple_of(i * tile, 128), tile)
            target[at] = t_dot(all_tokens[:, at], all_back[...]).astype(bf16)
            return 0

        lax.fori_loop(0, width // tile, weight, 0)
        flows.begin(5 + inner_parts + m)

    order = []
    for t in range(len(chunks) + flows.stages):
        for chunk in range(len(chunks)):
            if 0 <= t - chunk < flows.stages:
                item = (chunk, t - chunk)
                if item not in during:
                    order.append(item)

    def pump(count):
        for _ in range(min(count, len(order))):
            flows.advance(*order.pop(0))

    for copy in got_attn:
        copy.wait()
    query_matrix, key_matrix, value_matrix = (mats.at[m].reshape(width, width) for m in range(3))
    spread = sum_one[...] + dot_t(query_both[0], query_matrix[...])
    top = spread.astype(bf16)
    context_back[...] = top
    feed_rest = (spread - top.astype(f32)).astype(bf16)
    low_both[0, 3] = feed_rest
    place_ids = lax.broadcasted_iota(jnp.int32, (length, slots), 0)
    sends = []
    owns = []

    def send_rows(stage, target, sequence):
        for k, device in enumerate(place.row_mates()):
            n = len(sends)
            copy = pltpu.make_async_remote_copy(
                src_ref=stage.at[sequence, pl.ds(pl.multiple_of(device[0] * block, block), block)],
                dst_ref=target.at[place.s * own + sequence],
                send_sem=row_send.at[n],
                recv_sem=row_recv.at[n],
                device_id=device,
                device_id_type=MESH,
            )
            copy.start()
            sends.append(copy)
        copy = pltpu.make_async_copy(
            stage.at[sequence, pl.ds(pl.multiple_of(place.s * block, block), block)],
            target.at[place.s * own + sequence],
            own_sem.at[len(owns)],
        )
        copy.start()
        owns.append(copy)

    pump(2)
    for sequence in range(own):
        hits = places_ref[pl.ds(place.s * own + sequence, 1)] == place_ids
        hits = jnp.where(hits, 1.0, 0.0).astype(bf16)
        slot_at = pl.ds(sequence * slots, slots)
        for q in range(per_seq):
            at = slice(q * tile, (q + 1) * tile)
            result = dot_t(key_back[sequence, at], key_matrix[...])
            result = result + dot_t(value_back[sequence, at], value_matrix[...])
            result = result + dot(hits[at], context_back[slot_at])
            result = result + dot(hits[at], low_both[0, 3, slot_at])
            stage_tokens[sequence, at] = result.astype(bf16)
        send_rows(stage_tokens, grad_tokens_ref, sequence)
        vec_next(sequence)
        pump(3)

    for i in range(tiles):
        for copy in tile_loads(i):
            copy.wait()
        sequence, at = i // per_seq, pl.ds(i % per_seq * tile, tile)
        x = norm_tile[i % 2][...] + (dot(active_both[i % 2], out_matrix[...]) + vec[3:4])
        x, _ = normalize(x)
        stage_output[sequence, at] = (x * vec[6:7] + vec[7:8]).astype(bf16)
        if i + 2 < tiles:
            for copy in tile_loads(i + 2):
                copy.start()
        if (i + 1) % per_seq == 0:
            send_rows(stage_output, output_ref, sequence)
        if own + i < place.levels:
            vec_next(own + i)
        pump(3)
    for stage in range(own + tiles, place.levels):
        vec_next(stage)
    vec_grad_ref[...] = vec_sum[place.levels]
    pump(len(order))

    final = (final_attn, final_in, final_out)
    for n in range(place.levels - place.bits - 1):
        for index in range(3):
            k = n * 3 + index
            copy = pltpu.make_async_remote_copy(
                src_ref=final[index],
                dst_ref=extra_land[index].at[n],
                send_sem=extra_send.at[k],
                recv_sem=extra_recv.at[k],
                device_id=place.partner(n + 1),
                device_id_type=MESH,
            )
            copy.start()
            copy.wait()
            final[index][...] = final[index][...] + extra_land[index][n]

    hbm = (final_attn_hbm, final_in_hbm, final_out_hbm)
    final_copies = []
    for index in range(3):
        for k, device in enumerate(place.mates()):
            n = index * (merge - 1) + k
            copy = pltpu.make_async_remote_copy(
                src_ref=final[index],
                dst_ref=hbm[index].at[place.member],
                send_sem=final_send.at[n],
                recv_sem=final_recv.at[n],
                device_id=device,
                device_id_type=MESH,
            )
            copy.start()
            final_copies.append(copy)
        copy = pltpu.make_async_copy(
            final[index], hbm[index].at[place.member], own_sem.at[len(owns)]
        )
        copy.start()
        owns.append(copy)
    total = jnp.zeros((1, 1), f32)
    for part in (final_attn[...], final_in[...], final_out[...]):
        part = jnp.sum((part * part).reshape(-1, part.shape[-1]), axis=0, keepdims=True)
        total = total + jnp.sum(part, axis=1, keepdims=True)
    square[...] = jnp.broadcast_to(total, (8, 128)) * (2.0 / merge)
    all_reduce(place, square, square_land, square_send, square_recv)
    rest = vec_sum[place.levels]
    rest = jnp.sum(jnp.sum(rest * rest, axis=0, keepdims=True), axis=1, keepdims=True)
    square_ref[...] = square[...] + rest

    flows.finish()
    for copy in pairs + sends:
        copy.wait_send()
    for copy in sends:
        copy.wait_recv()
    for copy in owns:
        copy.wait()
    for copy in final_copies:
        copy.wait()
    for stage in range(place.levels):
        vec_copy(stage).wait_send()


def all_reduce(place, block, land, send, recv):
    me = place.s * place.dp + place.d

    def copy(k):
        other = lax.rem(me + k, place.devices)
        return pltpu.make_async_remote_copy(
            src_ref=block,
            dst_ref=land.at[k],
            send_sem=send.at[k],
            recv_sem=recv.at[k],
            device_id=(other // place.dp, lax.rem(other, place.dp)),
            device_id_type=MESH,
        )

    def start(k, _):
        copy(k).start()
        return 0

    def wait_recv(k, _):
        copy(k).wait_recv()
        return 0

    def wait_send(k, _):
        copy(k).wait_send()
        return 0

    lax.fori_loop(1, place.devices, start, 0)
    land[0] = block[...]
    lax.fori_loop(1, place.devices, wait_recv, 0)
    lax.fori_loop(1, place.devices, wait_send, 0)
    def add(k, total):
        return total + land[lax.rem(me - k + place.devices, place.devices)]

    block[...] = lax.fori_loop(1, place.devices, add, land[me])


def backward_call(mesh, forward, positions, counts, cotangent, rows):
    attn, ffn_in, ffn_out, vec, high, query, key, value, norm, active, slot_low, slot, slot_active, slope = forward
    place = Place(mesh, rows)
    own, length, width = high.shape
    inner = ffn_in.shape[-1]
    sequences = positions.shape[0]
    block = length // place.seq
    slots = positions.shape[1]
    count = own * slots
    half = width // 2
    bits = (2,) * place.bits
    joint, joint_out = ffn_in.shape[-2], ffn_out.shape[-2]
    merge = place.merge
    dma = pltpu.SemaphoreType.DMA
    vmem = pl.BlockSpec(memory_space=pltpu.VMEM)
    hbm = pl.BlockSpec(memory_space=pl.ANY)
    smem = pl.BlockSpec(memory_space=pltpu.SMEM)
    flow_count = (4 + inner // width + 3) * 3 * (place.bits + 1)
    tile = min(256, length)
    tiles = own * length // tile
    finals = [(4, joint, half), (joint, inner // 2), (joint_out, half)]
    extra = place.levels - place.bits - 1
    scratch = [
        pltpu.VMEM((4,) + bits + (joint, width), bf16),
        pltpu.VMEM(bits + (joint, width), bf16),
        pltpu.VMEM(bits + (joint_out, width), bf16),
    ]
    for _ in range(2):
        scratch += [
            pltpu.VMEM((4,) + bits + (joint, half), bf16),
            pltpu.VMEM(bits + (joint, inner // 2), bf16),
            pltpu.VMEM(bits + (joint_out, half), bf16),
        ]
    scratch += [pltpu.VMEM(shape, f32) for shape in finals]
    scratch += [
        pltpu.VMEM((2, own, length, width), bf16),
        pltpu.VMEM((own, length, width), bf16),
        pltpu.VMEM((own, length, width), bf16),
        pltpu.VMEM((2, count, inner), bf16),
        pltpu.VMEM((2, count, inner), bf16),
        pltpu.VMEM((max(count, tile), inner), f32),
        pltpu.VMEM((2, 4, count, width), bf16),
        pltpu.VMEM((3, count, width), f32),
        pltpu.VMEM((2, count, width), bf16),
        pltpu.VMEM((2, count, width), bf16),
        pltpu.VMEM((2, count, width), bf16),
        pltpu.VMEM((count, width), bf16),
        pltpu.VMEM((own, slots, width), f32),
        pltpu.VMEM((own, length, width), bf16),
        pltpu.VMEM((own, length, width), bf16),
        pltpu.VMEM((2, own, length, half), bf16),
        pltpu.VMEM((2, own, length, half), bf16),
        pltpu.VMEM((own, length, width), bf16),
        pltpu.VMEM((own, length, width), bf16),
        pltpu.VMEM((place.levels + 1, 16, width), f32),
        pltpu.VMEM((place.levels, 16, width), f32),
        pltpu.VMEM((8, 128), f32),
        pltpu.VMEM((place.devices, 8, 128), f32),
        dma((flow_count,)),
        dma((flow_count,)),
        dma((24,)),
        dma((16,)),
        dma((16,)),
        dma((tiles, 2)),
        dma((2 * own * (place.seq - 1),)),
        dma((2 * own * (place.seq - 1),)),
        dma((2 * own + 3,)),
        dma((place.levels,)),
        dma((place.levels,)),
        dma((3 * (merge - 1),)),
        dma((3 * (merge - 1),)),
        dma((place.devices,)),
        dma((place.devices,)),
    ]
    if extra:
        scratch += [
            [pltpu.VMEM((extra,) + shape, f32) for shape in finals],
            dma((3 * extra,)),
            dma((3 * extra,)),
        ]
    results = [
        ((sequences, block, width), bf16),
        ((sequences, block, width), bf16),
        ((merge,) + finals[0], f32),
        ((merge,) + finals[1], f32),
        ((merge,) + finals[2], f32),
        ((16, width), f32),
        ((8, 128), f32),
    ]
    return pl.pallas_call(
        functools.partial(backward_kernel, place),
        out_shape=[jax.ShapeDtypeStruct(*one) for one in results],
        in_specs=[hbm, hbm, hbm, vmem] + [hbm] * 9 + [vmem, smem, hbm],
        out_specs=[hbm] * 5 + [vmem] * 2,
        scratch_shapes=scratch,
        compiler_params=pltpu.CompilerParams(
            collective_id=1, has_side_effects=True, vmem_limit_bytes=64 * 2**20 - 2**18
        ),
    )(
        attn, ffn_in, ffn_out, vec, high, key, value, norm, active, slot_low, slot,
        slot_active, slope, positions, counts, cotangent,
    )


def adam_direction(first_old, second_old, clipped):
    first_new = decay_rate * first_old + (1.0 - decay_rate) * clipped
    second_new = decay_rate * second_old + (1.0 - decay_rate) * clipped * clipped
    correct = 1.0 - decay_rate**STEP
    direction = first_new / correct / (jnp.sqrt(second_new / correct) + adam_eps)
    return (first_new, second_new, direction)


def body(
    mesh,
    tokens,
    positions,
    counts,
    cotangent,
    attn_weights,
    ffn_in,
    ffn_out,
    vectors,
    attn_first,
    ffn_in_first,
    ffn_out_first,
    vector_first,
    attn_second,
    ffn_in_second,
    ffn_out_second,
    vector_second,
):
    results = forward_call(mesh, tokens, positions, attn_weights, ffn_in, ffn_out, vectors)
    rows = ffn_in.shape[0]
    output, grad_tokens, *final, vec_total, square_sum = backward_call(
        mesh, results, positions, counts, cotangent, rows
    )
    place = Place(mesh, rows)
    d = lax.axis_index("dp")
    member = lax.rem(d, place.merge)
    owner = lax.axis_index("seq") * place.dp + d

    def share(part, axis):
        whole = jnp.concatenate([part[0], part[1]], axis=-1)
        size = whole.shape[axis] // place.merge
        return lax.dynamic_slice_in_dim(whole, member * size, size, axis)

    vec_count = vectors.shape[0]
    shares = (
        share(final[0], 1),
        share(final[1], 0),
        share(final[2], 0),
        lax.dynamic_slice_in_dim(vec_total.reshape(-1), owner * vec_count, vec_count, 0),
    )
    square_sum = square_sum[0, 0]
    output = output.astype(f32)
    grad_tokens = grad_tokens.astype(f32)
    grad_norm = jnp.sqrt(square_sum)
    clip_factor = 1.0 / jnp.maximum(grad_norm, 1.0)
    clipped = tuple((share * clip_factor for share in shares))
    params = (attn_weights, ffn_in, ffn_out, vectors)
    firsts = (attn_first, ffn_in_first, ffn_out_first, vector_first)
    seconds = (attn_second, ffn_in_second, ffn_out_second, vector_second)
    moved = [adam_direction(firsts[index], seconds[index], clipped[index]) for index in range(4)]
    directions = [moved[index][2] + weight_decay * params[index] for index in range(3)]
    weight_sq = jnp.concatenate(
        [
            jnp.sum(attn_weights * attn_weights, axis=(1, 2)),
            jnp.sum(ffn_in * ffn_in)[None],
            jnp.sum(ffn_out * ffn_out)[None],
        ]
    )
    dir_sq = jnp.concatenate(
        [
            jnp.sum(directions[0] * directions[0], axis=(1, 2)),
            jnp.sum(directions[1] * directions[1])[None],
            jnp.sum(directions[2] * directions[2])[None],
        ]
    )
    lamb_sq = lax.psum(jnp.stack([weight_sq, dir_sq]), ("seq", "dp"))
    lamb_norms = jnp.sqrt(lamb_sq)
    trust_ratio = lamb_norms[0] / lamb_norms[1]
    new_attn = attn_weights - step_rate * trust_ratio[:4, None, None] * directions[0]
    new_ffn_in = ffn_in - step_rate * trust_ratio[4] * directions[1]
    new_ffn_out = ffn_out - step_rate * trust_ratio[5] * directions[2]
    new_vectors = vectors - step_rate * moved[3][2]
    return (
        output,
        grad_tokens,
        clipped[0],
        clipped[1],
        clipped[2],
        clipped[3],
        moved[0][0],
        moved[1][0],
        moved[2][0],
        moved[3][0],
        moved[0][1],
        moved[1][1],
        moved[2][1],
        moved[3][1],
        new_attn,
        new_ffn_in,
        new_ffn_out,
        new_vectors,
        new_attn.astype(bf16),
        new_ffn_in.astype(bf16),
        new_ffn_out.astype(bf16),
        lamb_norms,
        trust_ratio,
        grad_norm,
    )


def solution(mesh):
    return jax.shard_map(
        functools.partial(body, mesh),
        mesh=mesh,
        in_specs=(
            P("dp", "seq", None),
            P("dp", None),
            P("dp"),
            P("dp", None, None),
            P(None, ("seq", "dp"), None),
            P(("seq", "dp"), None),
            P(("seq", "dp"), None),
            P(("seq", "dp")),
            P(None, ("seq", "dp"), None),
            P(("seq", "dp"), None),
            P(("seq", "dp"), None),
            P(("seq", "dp")),
            P(None, ("seq", "dp"), None),
            P(("seq", "dp"), None),
            P(("seq", "dp"), None),
            P(("seq", "dp")),
        ),
        out_specs=(
            P("dp", "seq", None),
            P("dp", "seq", None),
            P(None, ("seq", "dp"), None),
            P(("seq", "dp"), None),
            P(("seq", "dp"), None),
            P(("seq", "dp")),
            P(None, ("seq", "dp"), None),
            P(("seq", "dp"), None),
            P(("seq", "dp"), None),
            P(("seq", "dp")),
            P(None, ("seq", "dp"), None),
            P(("seq", "dp"), None),
            P(("seq", "dp"), None),
            P(("seq", "dp")),
            P(None, ("seq", "dp"), None),
            P(("seq", "dp"), None),
            P(("seq", "dp"), None),
            P(("seq", "dp")),
            P(None, ("seq", "dp"), None),
            P(("seq", "dp"), None),
            P(("seq", "dp"), None),
            P(),
            P(),
            P(),
        ),
        check_vma=False,
    )
```

```python
import functools
import jax
import jax.numpy as jnp
from jax import lax
from jax.sharding import PartitionSpec as P
from jax.experimental import pallas as pl
from jax.experimental.pallas import tpu as pltpu

H = 12
HD = 64
STEP = 5

decay_rate = 0.5
step_rate = 0.3
weight_decay = 0.01
adam_eps = 1e-06
norm_eps = 1e-12
f32 = jnp.float32
bf16 = jnp.bfloat16
MESH = pl.DeviceIdType.MESH


class Place:
    def __init__(self, mesh, shard_rows):
        self.seq = mesh.shape["seq"]
        self.dp = mesh.shape["dp"]
        self.merge = 2
        while (self.merge * shard_rows) % 16:
            self.merge *= 2
        self.seq_bits = self.seq.bit_length() - 1
        self.far_bits = (self.dp // self.merge).bit_length() - 1
        self.bits = self.seq_bits + self.far_bits
        self.groups = self.seq * self.dp // self.merge
        self.devices = self.seq * self.dp
        self.levels = self.devices.bit_length() - 1

    def here(self):
        self.s = lax.axis_index("seq")
        self.d = lax.axis_index("dp")
        self.member = lax.rem(self.d, self.merge)
        self.core = lax.rem(self.d, 2)
        self.weight = []
        self.bit = []
        for dim in range(self.bits):
            if dim < self.seq_bits:
                w = 1 << (self.seq_bits - 1 - dim)
                self.bit.append(lax.rem(self.s // w, 2))
            else:
                w = self.merge << (self.bits - 1 - dim)
                self.bit.append(lax.rem(self.d // w, 2))
            self.weight.append(w)

    def across(self, dim):
        flip = self.weight[dim] * (1 - 2 * self.bit[dim])
        if dim < self.seq_bits:
            return (self.s + flip, self.d)
        return (self.s, self.d + flip)

    def other_core(self):
        return (self.s, self.d + 1 - 2 * self.core)

    def mates(self):
        base = self.d - self.member
        return [
            (self.s, base + lax.rem(self.member + k, self.merge)) for k in range(1, self.merge)
        ]

    def row_mates(self):
        return [(lax.rem(self.s + k, self.seq), self.d) for k in range(1, self.seq)]

    def greet(self):
        barrier = pltpu.get_barrier_semaphore()
        everyone = self.mates() + self.row_mates()
        everyone += [self.across(dim) for dim in range(self.seq_bits, self.bits)]
        for device in everyone:
            pl.semaphore_signal(barrier, inc=1, device_id=device, device_id_type=MESH)
        pl.semaphore_wait(barrier, len(everyone))

    def greet_all(self):
        barrier = pltpu.get_barrier_semaphore()
        me = self.s * self.dp + self.d

        def signal(k, _):
            other = lax.rem(me + k, self.devices)
            device = (other // self.dp, lax.rem(other, self.dp))
            pl.semaphore_signal(barrier, inc=1, device_id=device, device_id_type=MESH)
            return 0

        lax.fori_loop(1, self.devices, signal, 0)
        pl.semaphore_wait(barrier, self.devices - 1)

    def partner(self, level):
        inside = self.levels - self.bits
        if level >= inside:
            return self.across(level - inside)
        w = 1 << level
        return (self.s, self.d + w * (1 - 2 * lax.rem(self.d // w, 2)))

    def box(self, free):
        return tuple(slice(None) if dim in free else self.bit[dim] for dim in range(self.bits))


def erf(x):
    x = jnp.clip(x, -3.832506856900711, 3.832506856900711)
    x2 = x * x
    top = jnp.float32(0.00022905065861350646)
    for c in (
        0.0034082910107109506,
        0.050955695062380861,
        0.18520832239976145,
        1.128379143519084,
    ):
        top = top * x2 + jnp.float32(c)
    low = jnp.float32(-1.1791602954361697e-7)
    for c in (
        0.000023547966471313185,
        0.0010179625278914885,
        0.014070470171167667,
        0.11098505178285362,
        0.49746925110067538,
        1.0,
    ):
        low = low * x2 + jnp.float32(c)
    return x * top / low


def dot(a, b):
    return jnp.dot(a, b, preferred_element_type=f32)


def dot_t(a, b):
    return lax.dot_general(a, b, (((1,), (1,)), ((), ())), preferred_element_type=f32)


def t_dot(a, b):
    return lax.dot_general(a, b, (((0,), (0,)), ((), ())), preferred_element_type=f32)


def normalize(x):
    center = x - jnp.mean(x, -1, keepdims=True)
    inverse = lax.rsqrt(jnp.mean(center * center, -1, keepdims=True) + norm_eps)
    return center * inverse, inverse


FIRST = 3
LAG = 2
DURING = 5


class Flows:
    def __init__(self, place, chunks, send, recv):
        self.place = place
        self.chunks = chunks
        self.send = send
        self.recv = recv
        self.stages = place.bits

    def number(self, chunk, part, stage):
        return (chunk * 3 + part) * (self.stages + 1) + stage


class Gather(Flows):
    def copy(self, chunk, part, stage):
        place = self.place
        buf, rows, columns, order = self.chunks[chunk].part(part, place)
        n = self.number(chunk, part, stage)
        box = place.box(order[:stage]) + (rows, columns)
        return pltpu.make_async_remote_copy(
            src_ref=buf.at[box],
            dst_ref=buf.at[box],
            send_sem=self.send.at[n],
            recv_sem=self.recv.at[n],
            device_id=place.across(order[stage]),
            device_id_type=MESH,
        )

    def hand(self, chunk):
        place = self.place
        buf, rows, columns = self.chunks[chunk].half(place)
        n = self.number(chunk, 0, self.stages)
        box = tuple(slice(None) for _ in range(place.bits)) + (rows, columns)
        return pltpu.make_async_remote_copy(
            src_ref=buf.at[box],
            dst_ref=buf.at[box],
            send_sem=self.send.at[n],
            recv_sem=self.recv.at[n],
            device_id=place.other_core(),
            device_id_type=MESH,
        )

    def start(self, chunk):
        return max(0, chunk - FIRST)

    def lag(self, chunk):
        return 1 if chunk < 3 else LAG

    def step(self, t):
        for chunk in range(len(self.chunks)):
            stage, late = divmod(t - self.start(chunk), self.lag(chunk))
            if late or stage < 0:
                continue
            if stage <= self.stages:
                for part in range(3):
                    if stage > 0:
                        self.copy(chunk, part, stage - 1).wait_recv()
                    if stage < self.stages:
                        self.copy(chunk, part, stage).start()
                if stage == self.stages:
                    self.hand(chunk).start()
            if stage == self.stages + 1:
                self.hand(chunk).wait_recv()

    def last_step(self, chunk):
        return self.start(chunk) + self.lag(chunk) * (self.stages + 1)

    def pump(self, t):
        while self.now <= t:
            self.step(self.now)
            self.now += 1

    now = 0

    def finish(self):
        for chunk in range(len(self.chunks)):
            for part in range(3):
                for stage in range(self.stages):
                    self.copy(chunk, part, stage).wait_send()
            self.hand(chunk).wait_send()


class Chunk:
    def __init__(self, buf, first, width, orders, cuts=None):
        self.buf, self.first, self.width, self.orders, self.cuts = buf, first, width, orders, cuts

    def half(self, place):
        half = self.width // 2
        start = pl.multiple_of(self.first + place.core * half, 128)
        return self.buf, slice(None), pl.ds(start, half)

    def part(self, part, place):
        half = self.width // 2
        if self.cuts is None:
            third = half // 3
            start = pl.multiple_of(self.first + place.core * half + part * third, 128)
            return self.buf, slice(None), pl.ds(start, third), self.orders[part]
        start = pl.multiple_of(self.first + place.core * half, 128)
        rows = pl.ds(self.cuts[part], self.cuts[part + 1] - self.cuts[part])
        return self.buf, rows, pl.ds(start, half), self.orders[part]


def weight_chunks(place, attn, first_ffn, second_ffn, reverse):
    seq = list(range(place.seq_bits))
    far = list(range(place.seq_bits, place.bits))[::-1]
    left = far + seq[::-1]
    right = far + seq
    chunks = []

    def orders(index):
        a, b = (seq, seq[::-1]) if index % 2 else (seq[::-1], seq)
        if index % 4 < 2:
            third = a + far
        else:
            third = a[:1] + far + a[1:]
        out = [left, right, third]
        return [order[::-1] for order in out] if reverse else out

    width = attn.shape[-1]
    for m in range(4):
        chunks.append(Chunk(attn.at[m], 0, width, orders(m)))
    for j in range(first_ffn.shape[-1] // width):
        chunks.append(Chunk(first_ffn, j * width, width, orders(j)))
    rows = second_ffn.shape[-2]
    third = rows // 3 // 16 * 16
    for j in range(3):
        chunks.append(
            Chunk(second_ffn, j * width // 3, width // 3, orders(j), (0, third, 2 * third, rows))
        )
    return chunks


def forward_kernel(
    place,
    vec_rows,
    vec_count,
    tokens_ref,
    places_ref,
    attn_ref,
    in_ref,
    out_ref,
    vec_ref,
    attn_hbm,
    in_hbm,
    out_hbm,
    vec_hbm,
    high_hbm,
    query_hbm,
    key_hbm,
    value_hbm,
    output_hbm,
    slot_low_hbm,
    slot_hbm,
    slot_active_hbm,
    slot_slope_hbm,
    attn_buf,
    in_buf,
    out_buf,
    vec_buf,
    vec_acc,
    vec,
    attn_in,
    in_in,
    out_in,
    joined,
    send_high,
    send_rest,
    high,
    rest,
    query,
    key,
    value,
    norm,
    active,
    slot_low,
    slot,
    slot_active,
    slot_slope,
    flow_send,
    flow_recv,
    mate_send,
    mate_recv,
    local_sem,
    token_send,
    token_recv,
    vec_send,
    vec_recv,
    save_sem,
):
    place.here()
    place.greet()
    merge, seq = place.merge, place.seq
    width = tokens_ref.shape[-1]
    block = tokens_ref.shape[1]
    own = tokens_ref.shape[0] // seq
    length = block * seq
    rows = own * length
    slots = places_ref.shape[1]
    mine = place.box(())

    sources = (attn_ref, in_ref, out_ref)
    stages = (attn_in, in_in, out_in)
    mate_copies = []
    for index in range(3):
        for k, device in enumerate(place.mates()):
            n = index * (merge - 1) + k
            copy = pltpu.make_async_remote_copy(
                src_ref=sources[index],
                dst_ref=stages[index].at[place.member],
                send_sem=mate_send.at[n],
                recv_sem=mate_recv.at[n],
                device_id=device,
                device_id_type=MESH,
            )
            copy.start()
            mate_copies.append(copy)
    local = []
    for index in range(3):
        copy = pltpu.make_async_copy(
            sources[index], stages[index].at[place.member], local_sem.at[index]
        )
        copy.start()
        local.append(copy)
    vec_mates = []
    vec_buf.at[mine][place.member] = vec_ref[...]
    for k, device in enumerate(place.mates()):
        copy = pltpu.make_async_remote_copy(
            src_ref=vec_ref,
            dst_ref=vec_buf.at[mine].at[place.member],
            send_sem=vec_send.at[k],
            recv_sem=vec_recv.at[k],
            device_id=device,
            device_id_type=MESH,
        )
        copy.start()
        vec_mates.append(copy)

    def split(i, _):
        x = tokens_ref[i]
        top = x.astype(bf16)
        send_high[i] = top
        send_rest[i] = (x - top.astype(f32)).astype(bf16)
        return 0

    lax.fori_loop(0, own * seq, split, 0)
    token_copies = []
    my_columns = pl.ds(pl.multiple_of(place.s * block, block), block)
    for half, (source, target) in enumerate(((send_high, high), (send_rest, rest))):
        for k, device in enumerate(place.row_mates()):
            n = half * (seq - 1) + k
            token_copies.append(
                pltpu.make_async_remote_copy(
                    src_ref=source.at[pl.ds(device[0] * own, own)],
                    dst_ref=target.at[:, my_columns],
                    send_sem=token_send.at[n],
                    recv_sem=token_recv.at[n],
                    device_id=device,
                    device_id_type=MESH,
                )
            )
        target.at[:, my_columns][...] = source[pl.ds(place.s * own, own)]
    for copy in token_copies[: seq - 1]:
        copy.start()

    flows = Gather(place, weight_chunks(place, attn_buf, in_buf, out_buf, False), flow_send, flow_recv)

    def join(chunks, part):
        count = part.shape[1]
        for i in range(merge):
            joined[i * count : (i + 1) * count, : part.shape[-1]] = part[i]
        for chunk in chunks:
            buf, _, columns = chunk.half(place)
            buf.at[mine + (slice(None), columns)][...] = joined[: merge * count, columns].astype(bf16)

    for k in range(3):
        local[k].wait()
        for copy in mate_copies[k * (merge - 1) : (k + 1) * (merge - 1)]:
            copy.wait_recv()
        if k == 0:
            for m in range(4):
                join(flows.chunks[m : m + 1], attn_in.at[:, m])
        elif k == 1:
            join(flows.chunks[4:-3], in_in)
        else:
            join(flows.chunks[-3:], out_in)

    def vec_copy(stage):
        order = list(range(place.bits))
        box = place.box(order[:stage])
        return pltpu.make_async_remote_copy(
            src_ref=vec_buf.at[box],
            dst_ref=vec_buf.at[box],
            send_sem=vec_send.at[merge - 1 + stage],
            recv_sem=vec_recv.at[merge - 1 + stage],
            device_id=place.across(order[stage]),
            device_id_type=MESH,
        )

    for copy in vec_mates:
        copy.wait_recv()
    vec_copy(0).start()
    flows.pump(0)
    for t in range(1, flows.stages + 1):
        flows.pump(t)
        vec_copy(t - 1).wait_recv()
        if t < flows.stages:
            vec_copy(t).start()
    for copy in token_copies[seq - 1 :]:
        copy.start()

    vec_acc[...] = jnp.zeros_like(vec_acc)
    for owner in range(place.devices):
        group, member = divmod(owner, merge)
        bits = tuple((group >> (place.bits - 1 - dim)) & 1 for dim in range(place.bits))
        first, shift = divmod(vec_count * owner, 128)
        count = (shift + vec_count + 127) // 128
        vec_acc[first : first + count] += vec_buf.at[bits][member, :count]
    per = width // 128
    vec_acc[...] = vec_acc[...].astype(bf16).astype(f32)
    for row in range(vec_rows):
        vec[row : row + 1] = jnp.concatenate(
            [vec_acc[row * per + k : row * per + k + 1] for k in range(per)], axis=1
        )
    saves = []

    def save(source, target):
        copy = pltpu.make_async_copy(source, target, save_sem.at[len(saves)])
        copy.start()
        saves.append(copy)

    save(vec, vec_hbm)

    for copy in token_copies[: seq - 1]:
        copy.wait_recv()
    tile = min(256, length)
    per_seq = length // tile
    save(high, high_hbm)
    scale = HD**-0.5

    for m, target in enumerate((query, key, value)):
        flows.pump(flows.last_step(m))
        matrix = attn_buf.at[m].reshape(width, width)

        def project(i, _):
            sequence, at = i // per_seq, pl.ds(pl.multiple_of(lax.rem(i, per_seq) * tile, tile), tile)
            result = dot(high[sequence, at], matrix[...])
            if m == 0:
                result = (result + vec[0:1]).astype(bf16) * scale
            elif m == 2:
                result = result + vec[1:2]
            target[sequence, at] = result.astype(bf16)
            return 0

        lax.fori_loop(0, own * per_seq, project, 0)
        save(target, (query_hbm, key_hbm, value_hbm)[m])

    context = send_high.reshape(own, length, width)
    for copy in token_copies[: seq - 1]:
        copy.wait_send()
    pairs = width // 128
    turns = own * pairs
    lane = lax.broadcasted_iota(jnp.int32, (1, 128), 1)

    def attend(i, _):
        for k in range(during):
            @pl.when(i == (k + 1) * turns // (during + 1))
            def _():
                flows.step(flows.now + k)

        sequence, pair = i // pairs, lax.rem(i, pairs)
        at = pl.ds(pl.multiple_of(pair * 128, 128), 128)
        keys, values = key[sequence, :, at], value[sequence, :, at]
        for q in range(per_seq):
            places = slice(q * tile, (q + 1) * tile)
            queries = query[sequence, places, at]
            heads = []
            for head in range(2):
                picked = jnp.where(lane // HD == head, queries, jnp.zeros_like(queries))
                scores = dot_t(picked, keys)
                exponent = jnp.exp(scores - jnp.max(scores, -1, keepdims=True))
                total = jnp.sum(exponent, -1, keepdims=True)
                heads.append(dot(exponent.astype(bf16), values) / total)
            context[sequence, places, at] = jnp.where(lane < HD, heads[0], heads[1]).astype(bf16)
        return 0

    during = DURING
    lax.fori_loop(0, turns, attend, 0)
    flows.now += during
    flows.pump(flows.last_step(4))

    for copy in token_copies[seq - 1 :]:
        copy.wait_recv()
    out_matrix = attn_buf.at[3].reshape(width, width)

    def front(i, _):
        sequence, at = i // per_seq, pl.ds(pl.multiple_of(lax.rem(i, per_seq) * tile, tile), tile)
        x = high[sequence, at].astype(f32) + rest[sequence, at].astype(f32)
        x = x + (dot(context[sequence, at], out_matrix[...]) + vec[2:3])
        x, _ = normalize(x)
        norm[sequence, at] = x * vec[4:5] + vec[5:6]
        return 0

    lax.fori_loop(0, own * per_seq, front, 0)

    place_ids = lax.broadcasted_iota(jnp.int32, (length, slots), 0)
    for sequence in range(own):
        at = pl.ds(sequence * slots, slots)
        hits = places_ref[pl.ds(place.s * own + sequence, 1)] == place_ids
        hits = jnp.where(hits, 1.0, 0.0).astype(bf16)
        slot_high = t_dot(hits, high[sequence])
        slot_low[0, at] = slot_high.astype(bf16)
        slot_context = t_dot(hits, context[sequence]).astype(bf16)
        slot_low[1, at] = slot_context
        slot_low[2, at] = t_dot(hits, query[sequence]).astype(bf16)
        slot[0, at] = slot_high
        slot[1, at] = t_dot(hits, rest[sequence])
        x = slot[0, at] + slot[1, at]
        x = x + (dot(slot_context, out_matrix[...]) + vec[2:3])
        x, inverse = normalize(x)
        slot[0, at] = x
        slot[2, at] = jnp.broadcast_to(inverse, x.shape)
        x = x * vec[4:5] + vec[5:6]
        slot[1, at] = x
        slot_low[3, at] = x.astype(bf16)
    save(slot_low, slot_low_hbm)
    save(attn_buf, attn_hbm)

    in_matrix = in_buf.reshape(width, in_buf.shape[-1])
    for j in range(in_buf.shape[-1] // width):
        flows.pump(flows.last_step(4 + j))
        at = pl.ds(j * width, width)
        bias = vec[8 + j : 9 + j]

        def hidden(i, _):
            sequence, here = i // per_seq, pl.ds(pl.multiple_of(lax.rem(i, per_seq) * tile, tile), tile)
            x = dot(norm[sequence, here].astype(bf16), in_matrix[:, at]) + bias
            active[sequence, here, at] = (0.5 * x * (1.0 + erf(x * 0.5**0.5))).astype(bf16)
            return 0

        lax.fori_loop(0, own * per_seq, hidden, 0)
        x = dot(slot_low[3], in_matrix[:, at]) + bias
        half = 0.5 * (1.0 + erf(x * 0.5**0.5))
        slot_active[:, at] = (x * half).astype(bf16)
        slot_slope[:, at] = half + x * jnp.exp(-0.5 * x * x) * 0.3989422804014327
    save(slot_active, slot_active_hbm)
    save(slot_slope, slot_slope_hbm)
    save(in_buf, in_hbm)

    out_matrix = out_buf.reshape(out_buf.shape[-2] * place.groups, width)
    wide = width // 3
    for j in range(3):
        flows.pump(flows.last_step(len(flows.chunks) - 3 + j))
        at = slice(j * wide, (j + 1) * wide)
        save(out_buf.at[tuple(slice(None) for _ in range(place.bits + 1)) + (at,)],
             out_hbm.at[tuple(slice(None) for _ in range(place.bits + 1)) + (at,)])
        bias = vec[3:4, at]
        slot[1, :, at] = slot[1, :, at] + (dot(slot_active[...], out_matrix[:, at]) + bias)
        if j == 2:
            save(slot, slot_hbm)

        def feed(i, _):
            sequence, here = i // per_seq, pl.ds(pl.multiple_of(lax.rem(i, per_seq) * tile, tile), tile)
            x = dot(active[sequence, here], out_matrix[:, at]) + bias
            norm[sequence, here, at] = norm[sequence, here, at] + x
            return 0

        lax.fori_loop(0, own * per_seq, feed, 0)
    for copy in token_copies[seq - 1 :]:
        copy.wait_send()
    output = send_rest.reshape(own, length, width)

    def back(i, _):
        sequence, here = i // per_seq, pl.ds(pl.multiple_of(lax.rem(i, per_seq) * tile, tile), tile)
        x, _ = normalize(norm[sequence, here])
        output[sequence, here] = (x * vec[6:7] + vec[7:8]).astype(bf16)
        return 0

    lax.fori_loop(0, own * per_seq, back, 0)
    save(output, output_hbm)
    flows.finish()
    for copy in mate_copies + vec_mates:
        copy.wait_send()
    for stage in range(flows.stages):
        vec_copy(stage).wait_send()
    for copy in saves:
        copy.wait()


def forward_call(mesh, tokens, positions, attn_weights, ffn_in, ffn_out, vectors):
    place = Place(mesh, ffn_in.shape[0])
    sequences, block, width = tokens.shape
    inner = ffn_in.shape[1]
    slots = positions.shape[1]
    own = sequences // place.seq
    length = block * place.seq
    vec_count = vectors.shape[0]
    vec_rows = vec_count * place.devices // width
    owner = lax.axis_index("seq") * place.dp + lax.axis_index("dp")
    padded = lax.dynamic_update_slice_in_dim(
        jnp.zeros((1024,), f32), vectors.astype(bf16).astype(f32), lax.rem(vec_count * owner, 128), 0
    ).reshape(8, 128)
    bits = (2,) * place.bits
    r = ffn_in.shape[0]
    joint = r * place.merge
    joint_out = ffn_out.shape[0] * place.merge
    flow_count = (4 + inner // width + 3) * 3 * (place.bits + 1)
    attn_shape = (4,) + bits + (joint, width)
    in_shape = bits + (joint, inner)
    out_shape = bits + (joint_out, width)
    seq_shape = (own, length, width)
    rows = own * slots
    results = [
        (attn_shape, bf16),
        (in_shape, bf16),
        (out_shape, bf16),
        ((16, width), f32),
        (seq_shape, bf16),
        (seq_shape, bf16),
        (seq_shape, bf16),
        (seq_shape, bf16),
        (seq_shape, bf16),
        ((4, rows, width), bf16),
        ((3, rows, width), f32),
        ((rows, inner), bf16),
        ((rows, inner), f32),
    ]
    vmem = pl.BlockSpec(memory_space=pltpu.VMEM)
    hbm = pl.BlockSpec(memory_space=pl.ANY)
    dma = pltpu.SemaphoreType.DMA
    mates = place.merge - 1
    return pl.pallas_call(
        functools.partial(forward_kernel, place, vec_rows, vec_count),
        out_shape=[jax.ShapeDtypeStruct(*one) for one in results],
        in_specs=[vmem, vmem, hbm, hbm, hbm, vmem],
        out_specs=[hbm] * len(results),
        scratch_shapes=[
            pltpu.VMEM(attn_shape, bf16),
            pltpu.VMEM(in_shape, bf16),
            pltpu.VMEM(out_shape, bf16),
            pltpu.VMEM(bits + (place.merge, 8, 128), f32),
            pltpu.VMEM((vec_rows * width // 128 + 8, 128), f32),
            pltpu.VMEM((16, width), f32),
            pltpu.VMEM((place.merge,) + attn_weights.shape, f32),
            pltpu.VMEM((place.merge,) + ffn_in.shape, f32),
            pltpu.VMEM((place.merge,) + ffn_out.shape, f32),
            pltpu.VMEM((joint_out, inner), f32),
            pltpu.VMEM((sequences, block, width), bf16),
            pltpu.VMEM((sequences, block, width), bf16),
            pltpu.VMEM(seq_shape, bf16),
            pltpu.VMEM(seq_shape, bf16),
            pltpu.VMEM(seq_shape, bf16),
            pltpu.VMEM(seq_shape, bf16),
            pltpu.VMEM(seq_shape, bf16),
            pltpu.VMEM(seq_shape, f32),
            pltpu.VMEM((own, length, inner), bf16),
            pltpu.VMEM((4, rows, width), bf16),
            pltpu.VMEM((3, rows, width), f32),
            pltpu.VMEM((rows, inner), bf16),
            pltpu.VMEM((rows, inner), f32),
            dma((flow_count,)),
            dma((flow_count,)),
            dma((3 * mates,)),
            dma((3 * mates,)),
            dma((3,)),
            dma((2 * (place.seq - 1),)),
            dma((2 * (place.seq - 1),)),
            dma((mates + place.bits,)),
            dma((mates + place.bits,)),
            dma((len(results) + 2,)),
        ],
        compiler_params=pltpu.CompilerParams(
            collective_id=0, has_side_effects=True, vmem_limit_bytes=64 * 2**20 - 2**18
        ),
    )(tokens, positions, attn_weights, ffn_in, ffn_out, padded)


SPACING = 4
INSIDE = 8


class Scatter(Flows):
    def __init__(self, place, chunks, send, recv, landings, finals):
        super().__init__(place, chunks, send, recv)
        self.landings = landings
        self.finals = finals

    def boxes(self, order, stage):
        place = self.place
        done = order[:stage]
        dim = order[stage]
        out, mine, came = [], [], []
        for d in range(place.bits):
            if d in done:
                picks = (place.bit[d],) * 3
            elif d == dim:
                picks = (1 - place.bit[d], place.bit[d], 1 - place.bit[d])
            else:
                picks = (slice(None),) * 3
            out.append(picks[0])
            mine.append(picks[1])
            came.append(picks[2])
        return tuple(out), tuple(mine), tuple(came)

    def copy(self, chunk, part, stage):
        buf, rows, columns, order = self.chunks[chunk].part(part, self.place)
        n = self.number(chunk, part, stage)
        out, mine, _ = self.boxes(order, stage)
        return pltpu.make_async_remote_copy(
            src_ref=buf.at[out + (rows, columns)],
            dst_ref=self.landings[chunk].at[mine + (rows, columns)],
            send_sem=self.send.at[n],
            recv_sem=self.recv.at[n],
            device_id=self.place.across(order[stage]),
            device_id_type=MESH,
        )

    def begin(self, *chunks):
        for chunk in chunks:
            for part in range(3):
                self.copy(chunk, part, 0).start()

    def advance(self, chunk, stage):
        for part in range(3):
            self.sum_up(chunk, part, stage)

    def sum_up(self, chunk, part, stage):
        self.copy(chunk, part, stage).wait_recv()
        buf, rows, columns, order = self.chunks[chunk].part(part, self.place)
        _, mine, came = self.boxes(order, stage)
        tail = (rows, columns)
        total = buf.at[mine + tail][...].astype(f32)
        total = total + self.landings[chunk].at[came + tail][...].astype(f32)
        if stage + 1 < self.stages:
            buf.at[mine + tail][...] = total.astype(bf16)
            self.copy(chunk, part, stage + 1).start()
        else:
            self.finals[chunk].at[tail][...] = total

    def finish(self):
        for chunk in range(len(self.chunks)):
            for part in range(3):
                for stage in range(self.stages):
                    self.copy(chunk, part, stage).wait_send()


class Part:
    def __init__(self, buf, first, width, orders, cuts=None):
        self.buf, self.first, self.width, self.orders, self.cuts = buf, first, width, orders, cuts

    def size(self, part):
        rows = self.buf.shape[-2]
        if self.cuts is None:
            return rows * (self.width // 3)
        return (self.cuts[part + 1] - self.cuts[part]) * self.width

    def part(self, part, place):
        if self.cuts is None:
            third = self.width // 3
            columns = pl.ds(self.first + part * third, third)
            return self.buf, slice(None), columns, self.orders[part]
        rows = pl.ds(self.cuts[part], self.cuts[part + 1] - self.cuts[part])
        return self.buf, rows, pl.ds(self.first, self.width), self.orders[part]


def gradient_chunks(place, attn, first_ffn, second_ffn):
    forward = weight_chunks(place, attn, first_ffn, second_ffn, True)
    half = attn.shape[-1]
    chunks = []
    for j in range(3):
        chunks.append(
            Part(second_ffn, j * half // 3, half // 3, forward[-3 + j].orders, forward[-3 + j].cuts)
        )
    for j in range(first_ffn.shape[-1] // half):
        chunks.append(Part(first_ffn, j * half, half, forward[4 + j].orders))
    for m in (3, 0, 1, 2):
        chunks.append(Part(attn.at[m], 0, half, forward[m].orders))
    return chunks


def column_total(x):
    return jnp.sum(x, axis=0, keepdims=True)


def backward_kernel(
    place,
    attn_hbm,
    in_hbm,
    out_hbm,
    vec,
    high_hbm,
    key_hbm,
    value_hbm,
    output_hbm,
    slot_low_hbm,
    slot_hbm,
    slot_active_hbm,
    slot_slope_hbm,
    places_ref,
    counts_ref,
    cotangent_hbm,
    output_ref,
    grad_tokens_ref,
    final_attn_hbm,
    final_in_hbm,
    final_out_hbm,
    vec_grad_ref,
    square_ref,
    mats,
    last,
    out_buf,
    grad_attn,
    grad_in,
    grad_out,
    land_attn,
    land_in,
    land_out,
    final_attn,
    final_in,
    final_out,
    tokens_both,
    key,
    value,
    active_both,
    inner_both,
    slope,
    low_both,
    slot,
    feed_both,
    attended_both,
    query_both,
    context_back,
    sum_two,
    key_back,
    value_back,
    key_both,
    value_both,
    stage_tokens,
    vec_sum,
    vec_land,
    square,
    square_land,
    flow_send,
    flow_recv,
    load_sem,
    pair_send,
    pair_recv,
    row_send,
    row_recv,
    own_sem,
    vec_send,
    vec_recv,
    final_send,
    final_recv,
    square_send,
    square_recv,
    extra_land=None,
    extra_send=None,
    extra_recv=None,
):
    place.here()
    place.greet_all()
    merge, seq = place.merge, place.seq
    width = out_buf.shape[-1]
    inner = active_both.shape[-1]
    half = width // 2
    own, length = key.shape[:2]
    block = length // seq
    slots = sum_two.shape[1]
    rows = own * slots
    tile = min(256, length)
    per_seq = length // tile
    scale = HD**-0.5
    my_half = pl.ds(pl.multiple_of(place.core * half, 128), half)
    other_half = pl.ds(pl.multiple_of((1 - place.core) * half, 128), half)
    loads = []
    pairs = []
    sum_one = slope.at[:rows, :width]

    def load(source, target):
        copy = pltpu.make_async_copy(source, target, load_sem.at[len(loads)])
        copy.start()
        loads.append(copy)
        return copy

    def share(source, target):
        n = len(pairs)
        copy = pltpu.make_async_remote_copy(
            src_ref=source,
            dst_ref=target,
            send_sem=pair_send.at[n],
            recv_sem=pair_recv.at[n],
            device_id=place.other_core(),
            device_id_type=MESH,
        )
        copy.start()
        pairs.append(copy)
        return copy

    got_slot = load(slot_hbm, slot)
    got_cotangent = load(cotangent_hbm.at[pl.ds(place.s * own, own)], sum_two)
    got_out = load(out_hbm, out_buf)
    got_slope = load(slot_slope_hbm, slope.at[:rows])
    got_active = load(slot_active_hbm, active_both.at[0])
    came_active = share(slot_active_hbm, active_both.at[1])
    got_low = load(slot_low_hbm, low_both.at[0])
    came_low = share(slot_low_hbm, low_both.at[1])
    inner_parts = inner // width
    free = (slice(None),) * (place.bits + 1)
    got_in = [
        load(in_hbm.at[free + (pl.ds(j * width, width),)], mats.at[j]) for j in range(inner_parts)
    ]
    got_last = load(attn_hbm.at[3], last)
    got_key = load(key_hbm, key)
    got_value = load(value_hbm, value)
    got_tokens = load(high_hbm, tokens_both.at[0])
    came_tokens = share(high_hbm, tokens_both.at[1])

    sends = []
    owns = []

    def send_rows(stage, target, sequence):
        for k, device in enumerate(place.row_mates()):
            n = len(sends)
            copy = pltpu.make_async_remote_copy(
                src_ref=stage.at[sequence, pl.ds(pl.multiple_of(device[0] * block, block), block)],
                dst_ref=target.at[place.s * own + sequence],
                send_sem=row_send.at[n],
                recv_sem=row_recv.at[n],
                device_id=device,
                device_id_type=MESH,
            )
            copy.start()
            sends.append(copy)
        copy = pltpu.make_async_copy(
            stage.at[sequence, pl.ds(pl.multiple_of(place.s * block, block), block)],
            target.at[place.s * own + sequence],
            own_sem.at[len(owns)],
        )
        copy.start()
        owns.append(copy)

    for sequence in range(own):
        send_rows(output_hbm, output_ref, sequence)

    chunks = gradient_chunks(place, grad_attn, grad_in, grad_out)
    finals = [final_out] * 3 + [final_in] * inner_parts * 2 + [final_attn.at[m] for m in (3, 0, 1, 2)]
    landings = [land_out] * 3 + [land_in] * inner_parts + [land_attn.at[m] for m in (3, 0, 1, 2)]
    finals = [final_out] * 3 + [final_in] * inner_parts + finals[-4:]
    flows = Scatter(place, chunks, flow_send, flow_recv, landings, finals)

    vec_sum[...] = jnp.zeros_like(vec_sum)
    got_slot.wait()
    got_cotangent.wait()
    out_matrix = out_buf.reshape(inner, width)
    normal, inverse = normalize(slot[1])
    for sequence in range(own):
        slot_ids = lax.broadcasted_iota(jnp.int32, (slots, 1), 0)
        live = slot_ids < counts_ref[place.s * own + sequence]
        sum_two[sequence] = jnp.where(live, sum_two[sequence], 0.0)
    grad = sum_two[...].reshape(rows, width)
    vec_sum[0, 6:7] = column_total(grad * normal)
    vec_sum[0, 7:8] = column_total(grad)
    grad = grad * vec[6:7]
    grad = inverse * (
        grad
        - jnp.mean(grad, -1, keepdims=True)
        - normal * jnp.mean(grad * normal, -1, keepdims=True)
    )
    sum_two[...] = grad.reshape(own, slots, width)
    feed_low = grad.astype(bf16)
    feed_both[0] = feed_low
    vec_sum[0, 3:4] = column_total(feed_low.astype(f32))
    came_feed = share(feed_both.at[0], feed_both.at[1])

    got_slope.wait()
    got_out.wait()
    for j in range(inner_parts):
        at = pl.ds(j * width, width)
        back = dot_t(feed_both[0], out_matrix[at]) * slope[:rows, at]
        low = back.astype(bf16)
        inner_both[0, :, at] = low
        vec_sum[0, 8 + j : 9 + j] = column_total(low.astype(f32))
    came_inner = share(inner_both.at[0], inner_both.at[1])

    got_active.wait()
    came_active.wait_recv()
    came_feed.wait_recv()
    all_active = active_both.reshape(2 * rows, inner)
    all_feed = feed_both.reshape(2 * rows, width)
    out_rows = grad_out.reshape(inner, half)

    def second_matrix(i, _):
        at = pl.ds(pl.multiple_of(i * half, 128), half)
        out_rows[at] = t_dot(all_active[:, at], all_feed[:, my_half]).astype(bf16)
        return 0

    lax.fori_loop(0, inner // half, second_matrix, 0)
    flows.begin(0, 1, 2)

    got_low.wait()
    came_low.wait_recv()
    came_inner.wait_recv()
    all_inner = inner_both.reshape(2 * rows, inner)
    in_rows = grad_in.reshape(width, inner // 2)
    first_low = low_both[:, 3].reshape(2 * rows, width)
    for j in range(inner_parts):
        start = pl.multiple_of(place.core * (inner // 2) + j * half, 128)
        result = t_dot(first_low, all_inner[:, pl.ds(start, half)])
        in_rows[:, pl.ds(j * half, half)] = result.astype(bf16)
        flows.begin(3 + j)

    for copy in got_in:
        copy.wait()
    grad = sum_two[...].reshape(rows, width)
    for j in range(inner_parts):
        at = pl.ds(j * width, width)
        grad = grad + dot_t(inner_both[0, :, at], mats.at[j].reshape(width, width)[...])
    normal = slot[0]
    vec_sum[0, 4:5] = column_total(grad * normal)
    vec_sum[0, 5:6] = column_total(grad)
    grad = grad * vec[4:5]
    grad = slot[2] * (
        grad
        - jnp.mean(grad, -1, keepdims=True)
        - normal * jnp.mean(grad * normal, -1, keepdims=True)
    )
    sum_one[...] = grad
    low = grad.astype(bf16)
    attended_both[0] = low
    vec_sum[0, 2:3] = column_total(low.astype(f32))
    came_attended = share(attended_both.at[0], attended_both.at[1])
    got_attn = [load(attn_hbm.at[m], mats.at[m]) for m in range(3)]
    got_last.wait()
    context_back[...] = dot_t(low, last.reshape(width, width)[...]).astype(bf16)
    came_attended.wait_recv()
    result = t_dot(
        low_both[:, 1].reshape(2 * rows, width),
        attended_both.reshape(2 * rows, width)[:, my_half],
    )
    grad_attn.at[3].reshape(width, half)[...] = result.astype(bf16)
    flows.begin(3 + inner_parts)

    got_key.wait()
    got_value.wait()
    pair_count = width // 128
    turns = own * pair_count
    lane = lax.broadcasted_iota(jnp.int32, (1, 128), 1)
    order = sorted(
        ((chunk, stage) for chunk in range(len(chunks)) for stage in range(flows.stages)),
        key=lambda item: (item[0] + SPACING * item[1], item[0]),
    )
    during = order[:INSIDE]
    order = order[INSIDE:]

    def attend(i, _):
        for n, item in enumerate(during):
            @pl.when(i == n + 2)
            def _():
                flows.advance(*item)

        sequence, pair = i // pair_count, lax.rem(i, pair_count)
        at = pl.ds(pl.multiple_of(pair * 128, 128), 128)
        slot_at = pl.ds(pl.multiple_of(sequence * slots, slots), slots)
        keys, values = key[sequence, :, at], value[sequence, :, at]
        queries, backs = low_both[0, 2, slot_at, at], context_back[slot_at, at]
        zero = jnp.zeros_like(queries)
        outs = []
        for head in range(2):
            chosen = lane // HD == head
            scores = dot_t(jnp.where(chosen, queries, zero), keys)
            exponent = jnp.exp(scores - jnp.max(scores, -1, keepdims=True))
            probs = exponent / jnp.sum(exponent, -1, keepdims=True)
            grad_probs = dot_t(jnp.where(chosen, backs, zero), values)
            delta = jnp.sum(probs * grad_probs, -1, keepdims=True)
            scores_back = (probs * (grad_probs - delta)).astype(bf16)
            outs.append(
                (
                    dot(scores_back, keys) * scale,
                    t_dot(scores_back, queries),
                    t_dot(probs.astype(bf16), backs),
                )
            )
        left = lane < HD
        query_both[0, slot_at, at] = jnp.where(left, outs[0][0], outs[1][0]).astype(bf16)
        key_back[sequence, :, at] = jnp.where(left, outs[0][1], outs[1][1]).astype(bf16)
        value_back[sequence, :, at] = jnp.where(left, outs[0][2], outs[1][2]).astype(bf16)
        return 0

    lax.fori_loop(0, turns, attend, 0)
    came_query = share(query_both.at[0], query_both.at[1])
    came_key = share(key_back.at[:, :, other_half], key_both.at[1])
    came_value = share(value_back.at[:, :, other_half], value_both.at[1])
    key_both[0] = key_back[:, :, my_half]
    value_both[0] = value_back[:, :, my_half]
    total = jnp.zeros((1, width), f32)
    for sequence in range(own):
        total = total + column_total(value_back[sequence].astype(f32))
    vec_sum[0, 1:2] = total
    vec_sum[0, 0:1] = column_total(query_both[0].astype(f32))

    def vec_copy(stage):
        return pltpu.make_async_remote_copy(
            src_ref=vec_sum.at[stage],
            dst_ref=vec_land.at[stage],
            send_sem=vec_send.at[stage],
            recv_sem=vec_recv.at[stage],
            device_id=place.partner(stage),
            device_id_type=MESH,
        )

    vec_copy(0).start()

    def vec_next(stage):
        vec_copy(stage).wait_recv()
        vec_sum[stage + 1] = vec_sum[stage] + vec_land[stage]
        if stage + 1 < place.levels:
            vec_copy(stage + 1).start()

    came_query.wait_recv()
    result = t_dot(
        low_both[:, 0].reshape(2 * rows, width), query_both.reshape(2 * rows, width)[:, my_half]
    )
    grad_attn.at[0].reshape(width, half)[...] = result.astype(bf16)
    flows.begin(4 + inner_parts)
    got_tokens.wait()
    came_tokens.wait_recv()
    all_tokens = tokens_both.reshape(2 * own * length, width)
    for m, (came, both) in enumerate(((came_key, key_both), (came_value, value_both))):
        came.wait_recv()
        all_back = both.reshape(2 * own * length, half)
        target = grad_attn.at[1 + m].reshape(width, half)

        def weight(i, _):
            at = pl.ds(pl.multiple_of(i * tile, 128), tile)
            target[at] = t_dot(all_tokens[:, at], all_back[...]).astype(bf16)
            return 0

        lax.fori_loop(0, width // tile, weight, 0)
        flows.begin(5 + inner_parts + m)

    def pump(count):
        for _ in range(min(count, len(order))):
            flows.advance(*order.pop(0))

    for copy in got_attn:
        copy.wait()
    query_matrix, key_matrix, value_matrix = (mats.at[m].reshape(width, width) for m in range(3))
    spread = sum_one[...] + dot_t(query_both[0], query_matrix[...])
    top = spread.astype(bf16)
    context_back[...] = top
    feed_rest = (spread - top.astype(f32)).astype(bf16)
    low_both[0, 3] = feed_rest
    place_ids = lax.broadcasted_iota(jnp.int32, (length, slots), 0)
    pump(2)
    for sequence in range(own):
        hits = places_ref[pl.ds(place.s * own + sequence, 1)] == place_ids
        hits = jnp.where(hits, 1.0, 0.0).astype(bf16)
        slot_at = pl.ds(sequence * slots, slots)
        for q in range(per_seq):
            at = slice(q * tile, (q + 1) * tile)
            result = dot_t(key_back[sequence, at], key_matrix[...])
            result = result + dot_t(value_back[sequence, at], value_matrix[...])
            result = result + dot(hits[at], context_back[slot_at])
            result = result + dot(hits[at], low_both[0, 3, slot_at])
            stage_tokens[sequence, at] = result.astype(bf16)
        send_rows(stage_tokens, grad_tokens_ref, sequence)
        vec_next(sequence)
        pump(3)

    for stage in range(own, place.levels):
        vec_next(stage)
        pump(3)
    vec_grad_ref[...] = vec_sum[place.levels]
    pump(len(order))

    final = (final_attn, final_in, final_out)
    for n in range(place.levels - place.bits - 1):
        for index in range(3):
            k = n * 3 + index
            copy = pltpu.make_async_remote_copy(
                src_ref=final[index],
                dst_ref=extra_land[index].at[n],
                send_sem=extra_send.at[k],
                recv_sem=extra_recv.at[k],
                device_id=place.partner(n + 1),
                device_id_type=MESH,
            )
            copy.start()
            copy.wait()
            final[index][...] = final[index][...] + extra_land[index][n]

    hbm = (final_attn_hbm, final_in_hbm, final_out_hbm)
    final_copies = []
    for index in range(3):
        for k, device in enumerate(place.mates()):
            n = index * (merge - 1) + k
            copy = pltpu.make_async_remote_copy(
                src_ref=final[index],
                dst_ref=hbm[index].at[place.member],
                send_sem=final_send.at[n],
                recv_sem=final_recv.at[n],
                device_id=device,
                device_id_type=MESH,
            )
            copy.start()
            final_copies.append(copy)
        copy = pltpu.make_async_copy(
            final[index], hbm[index].at[place.member], own_sem.at[len(owns)]
        )
        copy.start()
        owns.append(copy)
    total = jnp.zeros((1, 1), f32)
    for part in (final_attn[...], final_in[...], final_out[...]):
        part = jnp.sum((part * part).reshape(-1, part.shape[-1]), axis=0, keepdims=True)
        total = total + jnp.sum(part, axis=1, keepdims=True)
    square[...] = jnp.broadcast_to(total, (8, 128)) * (2.0 / merge)
    all_reduce(place, square, square_land, square_send, square_recv)
    rest = vec_sum[place.levels]
    rest = jnp.sum(jnp.sum(rest * rest, axis=0, keepdims=True), axis=1, keepdims=True)
    square_ref[...] = square[...] + rest

    flows.finish()
    for copy in pairs + sends:
        copy.wait_send()
    for copy in sends:
        copy.wait_recv()
    for copy in owns:
        copy.wait()
    for copy in final_copies:
        copy.wait()
    for stage in range(place.levels):
        vec_copy(stage).wait_send()


def all_reduce(place, block, land, send, recv):
    me = place.s * place.dp + place.d

    def copy(k):
        other = lax.rem(me + k, place.devices)
        return pltpu.make_async_remote_copy(
            src_ref=block,
            dst_ref=land.at[k],
            send_sem=send.at[k],
            recv_sem=recv.at[k],
            device_id=(other // place.dp, lax.rem(other, place.dp)),
            device_id_type=MESH,
        )

    def start(k, _):
        copy(k).start()
        return 0

    def wait_recv(k, _):
        copy(k).wait_recv()
        return 0

    def wait_send(k, _):
        copy(k).wait_send()
        return 0

    lax.fori_loop(1, place.devices, start, 0)
    land[0] = block[...]
    lax.fori_loop(1, place.devices, wait_recv, 0)
    lax.fori_loop(1, place.devices, wait_send, 0)
    def add(k, total):
        return total + land[lax.rem(me - k + place.devices, place.devices)]

    block[...] = lax.fori_loop(1, place.devices, add, land[me])


def backward_call(mesh, forward, positions, counts, cotangent, rows):
    attn, ffn_in, ffn_out, vec, high, query, key, value, output, slot_low, slot, slot_active, slope = forward
    place = Place(mesh, rows)
    own, length, width = high.shape
    inner = ffn_in.shape[-1]
    sequences = positions.shape[0]
    block = length // place.seq
    slots = positions.shape[1]
    count = own * slots
    half = width // 2
    bits = (2,) * place.bits
    joint, joint_out = ffn_in.shape[-2], ffn_out.shape[-2]
    merge = place.merge
    dma = pltpu.SemaphoreType.DMA
    vmem = pl.BlockSpec(memory_space=pltpu.VMEM)
    hbm = pl.BlockSpec(memory_space=pl.ANY)
    smem = pl.BlockSpec(memory_space=pltpu.SMEM)
    flow_count = (4 + inner // width + 3) * 3 * (place.bits + 1)
    tile = min(256, length)
    finals = [(4, joint, half), (joint, inner // 2), (joint_out, half)]
    extra = place.levels - place.bits - 1
    scratch = [
        pltpu.VMEM((4,) + bits + (joint, width), bf16),
        pltpu.VMEM(bits + (joint, width), bf16),
        pltpu.VMEM(bits + (joint_out, width), bf16),
    ]
    for _ in range(2):
        scratch += [
            pltpu.VMEM((4,) + bits + (joint, half), bf16),
            pltpu.VMEM(bits + (joint, inner // 2), bf16),
            pltpu.VMEM(bits + (joint_out, half), bf16),
        ]
    scratch += [pltpu.VMEM(shape, f32) for shape in finals]
    scratch += [
        pltpu.VMEM((2, own, length, width), bf16),
        pltpu.VMEM((own, length, width), bf16),
        pltpu.VMEM((own, length, width), bf16),
        pltpu.VMEM((2, count, inner), bf16),
        pltpu.VMEM((2, count, inner), bf16),
        pltpu.VMEM((max(count, tile), inner), f32),
        pltpu.VMEM((2, 4, count, width), bf16),
        pltpu.VMEM((3, count, width), f32),
        pltpu.VMEM((2, count, width), bf16),
        pltpu.VMEM((2, count, width), bf16),
        pltpu.VMEM((2, count, width), bf16),
        pltpu.VMEM((count, width), bf16),
        pltpu.VMEM((own, slots, width), f32),
        pltpu.VMEM((own, length, width), bf16),
        pltpu.VMEM((own, length, width), bf16),
        pltpu.VMEM((2, own, length, half), bf16),
        pltpu.VMEM((2, own, length, half), bf16),
        pltpu.VMEM((own, length, width), bf16),
        pltpu.VMEM((place.levels + 1, 16, width), f32),
        pltpu.VMEM((place.levels, 16, width), f32),
        pltpu.VMEM((8, 128), f32),
        pltpu.VMEM((place.devices, 8, 128), f32),
        dma((flow_count,)),
        dma((flow_count,)),
        dma((24,)),
        dma((16,)),
        dma((16,)),
        dma((2 * own * (place.seq - 1),)),
        dma((2 * own * (place.seq - 1),)),
        dma((2 * own + 3,)),
        dma((place.levels,)),
        dma((place.levels,)),
        dma((3 * (merge - 1),)),
        dma((3 * (merge - 1),)),
        dma((place.devices,)),
        dma((place.devices,)),
    ]
    if extra:
        scratch += [
            [pltpu.VMEM((extra,) + shape, f32) for shape in finals],
            dma((3 * extra,)),
            dma((3 * extra,)),
        ]
    results = [
        ((sequences, block, width), bf16),
        ((sequences, block, width), bf16),
        ((merge,) + finals[0], f32),
        ((merge,) + finals[1], f32),
        ((merge,) + finals[2], f32),
        ((16, width), f32),
        ((8, 128), f32),
    ]
    return pl.pallas_call(
        functools.partial(backward_kernel, place),
        out_shape=[jax.ShapeDtypeStruct(*one) for one in results],
        in_specs=[hbm, hbm, hbm, vmem] + [hbm] * 8 + [vmem, smem, hbm],
        out_specs=[hbm] * 5 + [vmem] * 2,
        scratch_shapes=scratch,
        compiler_params=pltpu.CompilerParams(
            collective_id=1, has_side_effects=True, vmem_limit_bytes=64 * 2**20 - 2**18
        ),
    )(
        attn, ffn_in, ffn_out, vec, high, key, value, output, slot_low, slot,
        slot_active, slope, positions, counts, cotangent,
    )


def total_kernel(place, block_ref, total_ref, block, land, send, recv):
    place.here()
    place.greet_all()
    block[...] = block_ref[...]
    all_reduce(place, block, land, send, recv)
    total_ref[...] = block[...]


def total_call(mesh, rows, values):
    place = Place(mesh, rows)
    padded = jnp.zeros((1024,), f32).at[: values.size].set(values.reshape(-1)).reshape(8, 128)
    vmem = pl.BlockSpec(memory_space=pltpu.VMEM)
    dma = pltpu.SemaphoreType.DMA
    total = pl.pallas_call(
        functools.partial(total_kernel, place),
        out_shape=jax.ShapeDtypeStruct((8, 128), f32),
        in_specs=[vmem],
        out_specs=vmem,
        scratch_shapes=[
            pltpu.VMEM((8, 128), f32),
            pltpu.VMEM((place.devices, 8, 128), f32),
            dma((place.devices,)),
            dma((place.devices,)),
        ],
        compiler_params=pltpu.CompilerParams(collective_id=2, has_side_effects=True),
    )(padded)
    return total.reshape(-1)[: values.size].reshape(values.shape)


def adam_direction(first_old, second_old, clipped):
    first_new = decay_rate * first_old + (1.0 - decay_rate) * clipped
    second_new = decay_rate * second_old + (1.0 - decay_rate) * clipped * clipped
    correct = 1.0 - decay_rate**STEP
    direction = first_new / correct / (jnp.sqrt(second_new / correct) + adam_eps)
    return (first_new, second_new, direction)


def body(
    mesh,
    tokens,
    positions,
    counts,
    cotangent,
    attn_weights,
    ffn_in,
    ffn_out,
    vectors,
    attn_first,
    ffn_in_first,
    ffn_out_first,
    vector_first,
    attn_second,
    ffn_in_second,
    ffn_out_second,
    vector_second,
):
    results = forward_call(mesh, tokens, positions, attn_weights, ffn_in, ffn_out, vectors)
    rows = ffn_in.shape[0]
    output, grad_tokens, *final, vec_total, square_sum = backward_call(
        mesh, results, positions, counts, cotangent, rows
    )
    place = Place(mesh, rows)
    d = lax.axis_index("dp")
    member = lax.rem(d, place.merge)
    owner = lax.axis_index("seq") * place.dp + d

    def share(part, axis):
        whole = jnp.concatenate([part[0], part[1]], axis=-1)
        size = whole.shape[axis] // place.merge
        return lax.dynamic_slice_in_dim(whole, member * size, size, axis)

    vec_count = vectors.shape[0]
    shares = (
        share(final[0], 1),
        share(final[1], 0),
        share(final[2], 0),
        lax.dynamic_slice_in_dim(vec_total.reshape(-1), owner * vec_count, vec_count, 0),
    )
    square_sum = square_sum[0, 0]
    output = output.astype(f32)
    grad_tokens = grad_tokens.astype(f32)
    grad_norm = jnp.sqrt(square_sum)
    clip_factor = 1.0 / jnp.maximum(grad_norm, 1.0)
    clipped = tuple((share * clip_factor for share in shares))
    params = (attn_weights, ffn_in, ffn_out, vectors)
    firsts = (attn_first, ffn_in_first, ffn_out_first, vector_first)
    seconds = (attn_second, ffn_in_second, ffn_out_second, vector_second)
    moved = [adam_direction(firsts[index], seconds[index], clipped[index]) for index in range(4)]
    directions = [moved[index][2] + weight_decay * params[index] for index in range(3)]
    weight_sq = jnp.concatenate(
        [
            jnp.sum(attn_weights * attn_weights, axis=(1, 2)),
            jnp.sum(ffn_in * ffn_in)[None],
            jnp.sum(ffn_out * ffn_out)[None],
        ]
    )
    dir_sq = jnp.concatenate(
        [
            jnp.sum(directions[0] * directions[0], axis=(1, 2)),
            jnp.sum(directions[1] * directions[1])[None],
            jnp.sum(directions[2] * directions[2])[None],
        ]
    )
    lamb_sq = total_call(mesh, rows, jnp.stack([weight_sq, dir_sq]))
    lamb_norms = jnp.sqrt(lamb_sq)
    trust_ratio = lamb_norms[0] / lamb_norms[1]
    new_attn = attn_weights - step_rate * trust_ratio[:4, None, None] * directions[0]
    new_ffn_in = ffn_in - step_rate * trust_ratio[4] * directions[1]
    new_ffn_out = ffn_out - step_rate * trust_ratio[5] * directions[2]
    new_vectors = vectors - step_rate * moved[3][2]
    return (
        output,
        grad_tokens,
        clipped[0],
        clipped[1],
        clipped[2],
        clipped[3],
        moved[0][0],
        moved[1][0],
        moved[2][0],
        moved[3][0],
        moved[0][1],
        moved[1][1],
        moved[2][1],
        moved[3][1],
        new_attn,
        new_ffn_in,
        new_ffn_out,
        new_vectors,
        new_attn.astype(bf16),
        new_ffn_in.astype(bf16),
        new_ffn_out.astype(bf16),
        lamb_norms,
        trust_ratio,
        grad_norm,
    )


def solution(mesh):
    return jax.shard_map(
        functools.partial(body, mesh),
        mesh=mesh,
        in_specs=(
            P("dp", "seq", None),
            P("dp", None),
            P("dp"),
            P("dp", None, None),
            P(None, ("seq", "dp"), None),
            P(("seq", "dp"), None),
            P(("seq", "dp"), None),
            P(("seq", "dp")),
            P(None, ("seq", "dp"), None),
            P(("seq", "dp"), None),
            P(("seq", "dp"), None),
            P(("seq", "dp")),
            P(None, ("seq", "dp"), None),
            P(("seq", "dp"), None),
            P(("seq", "dp"), None),
            P(("seq", "dp")),
        ),
        out_specs=(
            P("dp", "seq", None),
            P("dp", "seq", None),
            P(None, ("seq", "dp"), None),
            P(("seq", "dp"), None),
            P(("seq", "dp"), None),
            P(("seq", "dp")),
            P(None, ("seq", "dp"), None),
            P(("seq", "dp"), None),
            P(("seq", "dp"), None),
            P(("seq", "dp")),
            P(None, ("seq", "dp"), None),
            P(("seq", "dp"), None),
            P(("seq", "dp"), None),
            P(("seq", "dp")),
            P(None, ("seq", "dp"), None),
            P(("seq", "dp"), None),
            P(("seq", "dp"), None),
            P(("seq", "dp")),
            P(None, ("seq", "dp"), None),
            P(("seq", "dp"), None),
            P(("seq", "dp"), None),
            P(),
            P(),
            P(),
        ),
        check_vma=False,
    )
```

```python
import functools
import jax
import jax.numpy as jnp
from jax import lax
from jax.sharding import PartitionSpec as P
from jax.experimental import pallas as pl
from jax.experimental.pallas import tpu as pltpu

H = 12
HD = 64
STEP = 5

decay_rate = 0.5
step_rate = 0.3
weight_decay = 0.01
adam_eps = 1e-06
norm_eps = 1e-12
f32 = jnp.float32
bf16 = jnp.bfloat16
MESH = pl.DeviceIdType.MESH


class Place:
    def __init__(self, mesh, shard_rows):
        self.seq = mesh.shape["seq"]
        self.dp = mesh.shape["dp"]
        self.merge = 2
        while (self.merge * shard_rows) % 16:
            self.merge *= 2
        self.seq_bits = self.seq.bit_length() - 1
        self.far_bits = (self.dp // self.merge).bit_length() - 1
        self.bits = self.seq_bits + self.far_bits
        self.groups = self.seq * self.dp // self.merge
        self.devices = self.seq * self.dp
        self.levels = self.devices.bit_length() - 1

    def here(self):
        self.s = lax.axis_index("seq")
        self.d = lax.axis_index("dp")
        self.member = lax.rem(self.d, self.merge)
        self.core = lax.rem(self.d, 2)
        self.weight = []
        self.bit = []
        for dim in range(self.bits):
            if dim < self.seq_bits:
                w = 1 << (self.seq_bits - 1 - dim)
                self.bit.append(lax.rem(self.s // w, 2))
            else:
                w = self.merge << (self.bits - 1 - dim)
                self.bit.append(lax.rem(self.d // w, 2))
            self.weight.append(w)

    def across(self, dim):
        flip = self.weight[dim] * (1 - 2 * self.bit[dim])
        if dim < self.seq_bits:
            return (self.s + flip, self.d)
        return (self.s, self.d + flip)

    def other_core(self):
        return (self.s, self.d + 1 - 2 * self.core)

    def mates(self):
        base = self.d - self.member
        return [
            (self.s, base + lax.rem(self.member + k, self.merge)) for k in range(1, self.merge)
        ]

    def row_mates(self):
        return [(lax.rem(self.s + k, self.seq), self.d) for k in range(1, self.seq)]

    def greet(self):
        barrier = pltpu.get_barrier_semaphore()
        everyone = self.mates() + self.row_mates()
        everyone += [self.across(dim) for dim in range(self.seq_bits, self.bits)]
        for device in everyone:
            pl.semaphore_signal(barrier, inc=1, device_id=device, device_id_type=MESH)
        pl.semaphore_wait(barrier, len(everyone))

    def greet_all(self):
        barrier = pltpu.get_barrier_semaphore()
        everyone = self.row_mates()
        everyone += [(self.s, lax.rem(self.d + k, self.dp)) for k in range(1, self.dp)]
        for device in everyone:
            pl.semaphore_signal(barrier, inc=1, device_id=device, device_id_type=MESH)
        pl.semaphore_wait(barrier, len(everyone))

    def partner(self, level):
        inside = self.levels - self.bits
        if level >= inside:
            return self.across(level - inside)
        w = 1 << level
        return (self.s, self.d + w * (1 - 2 * lax.rem(self.d // w, 2)))

    def box(self, free):
        return tuple(slice(None) if dim in free else self.bit[dim] for dim in range(self.bits))


def erf(x):
    x = jnp.clip(x, -3.832506856900711, 3.832506856900711)
    x2 = x * x
    top = jnp.float32(0.00022905065861350646)
    for c in (
        0.0034082910107109506,
        0.050955695062380861,
        0.18520832239976145,
        1.128379143519084,
    ):
        top = top * x2 + jnp.float32(c)
    low = jnp.float32(-1.1791602954361697e-7)
    for c in (
        0.000023547966471313185,
        0.0010179625278914885,
        0.014070470171167667,
        0.11098505178285362,
        0.49746925110067538,
        1.0,
    ):
        low = low * x2 + jnp.float32(c)
    return x * top / low


def dot(a, b):
    return jnp.dot(a, b, preferred_element_type=f32)


def dot_t(a, b):
    return lax.dot_general(a, b, (((1,), (1,)), ((), ())), preferred_element_type=f32)


def t_dot(a, b):
    return lax.dot_general(a, b, (((0,), (0,)), ((), ())), preferred_element_type=f32)


def normalize(x):
    center = x - jnp.mean(x, -1, keepdims=True)
    inverse = lax.rsqrt(jnp.mean(center * center, -1, keepdims=True) + norm_eps)
    return center * inverse, inverse


FIRST = 3
LAG = 2
DURING = 5


class Flows:
    def __init__(self, place, chunks, send, recv):
        self.place = place
        self.chunks = chunks
        self.send = send
        self.recv = recv
        self.stages = place.bits

    def number(self, chunk, part, stage):
        return (chunk * 3 + part) * (self.stages + 1) + stage


class Gather(Flows):
    def copy(self, chunk, part, stage):
        place = self.place
        buf, rows, columns, order = self.chunks[chunk].part(part, place)
        n = self.number(chunk, part, stage)
        box = place.box(order[:stage]) + (rows, columns)
        return pltpu.make_async_remote_copy(
            src_ref=buf.at[box],
            dst_ref=buf.at[box],
            send_sem=self.send.at[n],
            recv_sem=self.recv.at[n],
            device_id=place.across(order[stage]),
            device_id_type=MESH,
        )

    def hand(self, chunk):
        place = self.place
        buf, rows, columns = self.chunks[chunk].half(place)
        n = self.number(chunk, 0, self.stages)
        box = tuple(slice(None) for _ in range(place.bits)) + (rows, columns)
        return pltpu.make_async_remote_copy(
            src_ref=buf.at[box],
            dst_ref=buf.at[box],
            send_sem=self.send.at[n],
            recv_sem=self.recv.at[n],
            device_id=place.other_core(),
            device_id_type=MESH,
        )

    def start(self, chunk):
        return max(0, chunk - FIRST)

    def lag(self, chunk):
        return 1 if chunk < 3 else LAG

    def step(self, t):
        for chunk in range(len(self.chunks)):
            stage, late = divmod(t - self.start(chunk), self.lag(chunk))
            if late or stage < 0:
                continue
            if stage <= self.stages:
                for part in range(3):
                    if stage > 0:
                        self.copy(chunk, part, stage - 1).wait_recv()
                    if stage < self.stages:
                        self.copy(chunk, part, stage).start()
                if stage == self.stages:
                    self.hand(chunk).start()
            if stage == self.stages + 1:
                self.hand(chunk).wait_recv()

    def last_step(self, chunk):
        return self.start(chunk) + self.lag(chunk) * (self.stages + 1)

    def pump(self, t):
        while self.now <= t:
            self.step(self.now)
            self.now += 1

    now = 0

    def finish(self):
        for chunk in range(len(self.chunks)):
            for part in range(3):
                for stage in range(self.stages):
                    self.copy(chunk, part, stage).wait_send()
            self.hand(chunk).wait_send()


class Chunk:
    def __init__(self, buf, first, width, orders, cuts=None):
        self.buf, self.first, self.width, self.orders, self.cuts = buf, first, width, orders, cuts

    def half(self, place):
        half = self.width // 2
        start = pl.multiple_of(self.first + place.core * half, 128)
        return self.buf, slice(None), pl.ds(start, half)

    def part(self, part, place):
        half = self.width // 2
        if self.cuts is None:
            third = half // 3
            start = pl.multiple_of(self.first + place.core * half + part * third, 128)
            return self.buf, slice(None), pl.ds(start, third), self.orders[part]
        start = pl.multiple_of(self.first + place.core * half, 128)
        rows = pl.ds(self.cuts[part], self.cuts[part + 1] - self.cuts[part])
        return self.buf, rows, pl.ds(start, half), self.orders[part]


def weight_chunks(place, attn, first_ffn, second_ffn, reverse):
    seq = list(range(place.seq_bits))
    far = list(range(place.seq_bits, place.bits))[::-1]
    left = far + seq[::-1]
    right = far + seq
    chunks = []

    def orders(index):
        a, b = (seq, seq[::-1]) if index % 2 else (seq[::-1], seq)
        if not reverse:
            third = far + a
        elif index % 4 < 2:
            third = a + far
        else:
            third = a[:1] + far + a[1:]
        out = [left, right, third]
        return [order[::-1] for order in out] if reverse else out

    width = attn.shape[-1]
    for m in range(4):
        chunks.append(Chunk(attn.at[m], 0, width, orders(m)))
    for j in range(first_ffn.shape[-1] // width):
        chunks.append(Chunk(first_ffn, j * width, width, orders(j)))
    rows = second_ffn.shape[-2]
    third = rows // 3 // 16 * 16
    for j in range(3):
        chunks.append(
            Chunk(second_ffn, j * width // 3, width // 3, orders(j), (0, third, 2 * third, rows))
        )
    return chunks


def forward_kernel(
    place,
    vec_rows,
    vec_count,
    tokens_ref,
    places_ref,
    attn_ref,
    in_ref,
    out_ref,
    vec_ref,
    attn_hbm,
    in_hbm,
    out_hbm,
    vec_hbm,
    high_hbm,
    query_hbm,
    key_hbm,
    value_hbm,
    output_hbm,
    slot_low_hbm,
    slot_hbm,
    slot_active_hbm,
    slot_slope_hbm,
    attn_buf,
    in_buf,
    out_buf,
    vec_buf,
    vec_acc,
    vec,
    attn_in,
    in_in,
    out_in,
    joined,
    send_high,
    send_rest,
    high,
    rest,
    query,
    key,
    value,
    norm,
    active,
    slot_low,
    slot,
    slot_active,
    slot_slope,
    flow_send,
    flow_recv,
    mate_send,
    mate_recv,
    local_sem,
    token_send,
    token_recv,
    vec_send,
    vec_recv,
    save_sem,
):
    place.here()
    place.greet()
    merge, seq = place.merge, place.seq
    width = tokens_ref.shape[-1]
    block = tokens_ref.shape[1]
    own = tokens_ref.shape[0] // seq
    length = block * seq
    rows = own * length
    slots = places_ref.shape[1]
    mine = place.box(())

    sources = (attn_ref, in_ref, out_ref)
    stages = (attn_in, in_in, out_in)
    mate_copies = []
    for index in range(3):
        for k, device in enumerate(place.mates()):
            n = index * (merge - 1) + k
            copy = pltpu.make_async_remote_copy(
                src_ref=sources[index],
                dst_ref=stages[index].at[place.member],
                send_sem=mate_send.at[n],
                recv_sem=mate_recv.at[n],
                device_id=device,
                device_id_type=MESH,
            )
            copy.start()
            mate_copies.append(copy)
    local = []
    for index in range(3):
        copy = pltpu.make_async_copy(
            sources[index], stages[index].at[place.member], local_sem.at[index]
        )
        copy.start()
        local.append(copy)
    vec_mates = []
    vec_buf.at[mine][place.member] = vec_ref[...]
    for k, device in enumerate(place.mates()):
        copy = pltpu.make_async_remote_copy(
            src_ref=vec_ref,
            dst_ref=vec_buf.at[mine].at[place.member],
            send_sem=vec_send.at[k],
            recv_sem=vec_recv.at[k],
            device_id=device,
            device_id_type=MESH,
        )
        copy.start()
        vec_mates.append(copy)

    def split(i, _):
        x = tokens_ref[i]
        top = x.astype(bf16)
        send_high[i] = top
        send_rest[i] = (x - top.astype(f32)).astype(bf16)
        return 0

    lax.fori_loop(0, own * seq, split, 0)
    token_copies = []
    my_columns = pl.ds(pl.multiple_of(place.s * block, block), block)
    for half, (source, target) in enumerate(((send_high, high), (send_rest, rest))):
        for k, device in enumerate(place.row_mates()):
            n = half * (seq - 1) + k
            token_copies.append(
                pltpu.make_async_remote_copy(
                    src_ref=source.at[pl.ds(device[0] * own, own)],
                    dst_ref=target.at[:, my_columns],
                    send_sem=token_send.at[n],
                    recv_sem=token_recv.at[n],
                    device_id=device,
                    device_id_type=MESH,
                )
            )
        target.at[:, my_columns][...] = source[pl.ds(place.s * own, own)]
    for copy in token_copies[: seq - 1]:
        copy.start()

    flows = Gather(place, weight_chunks(place, attn_buf, in_buf, out_buf, False), flow_send, flow_recv)

    def join(chunks, part):
        count = part.shape[1]
        for i in range(merge):
            joined[i * count : (i + 1) * count, : part.shape[-1]] = part[i]
        for chunk in chunks:
            buf, _, columns = chunk.half(place)
            buf.at[mine + (slice(None), columns)][...] = joined[: merge * count, columns].astype(bf16)

    for k in range(3):
        local[k].wait()
        for copy in mate_copies[k * (merge - 1) : (k + 1) * (merge - 1)]:
            copy.wait_recv()
        if k == 0:
            for m in range(4):
                join(flows.chunks[m : m + 1], attn_in.at[:, m])
        elif k == 1:
            join(flows.chunks[4:-3], in_in)
        else:
            join(flows.chunks[-3:], out_in)

    def vec_copy(stage):
        order = list(range(place.bits))
        box = place.box(order[:stage])
        return pltpu.make_async_remote_copy(
            src_ref=vec_buf.at[box],
            dst_ref=vec_buf.at[box],
            send_sem=vec_send.at[merge - 1 + stage],
            recv_sem=vec_recv.at[merge - 1 + stage],
            device_id=place.across(order[stage]),
            device_id_type=MESH,
        )

    for copy in vec_mates:
        copy.wait_recv()
    vec_copy(0).start()
    flows.pump(0)
    for t in range(1, flows.stages + 1):
        flows.pump(t)
        vec_copy(t - 1).wait_recv()
        if t < flows.stages:
            vec_copy(t).start()
    for copy in token_copies[seq - 1 :]:
        copy.start()

    vec_acc[...] = jnp.zeros_like(vec_acc)
    for owner in range(place.devices):
        group, member = divmod(owner, merge)
        bits = tuple((group >> (place.bits - 1 - dim)) & 1 for dim in range(place.bits))
        first, shift = divmod(vec_count * owner, 128)
        count = (shift + vec_count + 127) // 128
        vec_acc[first : first + count] += vec_buf.at[bits][member, :count]
    per = width // 128
    vec_acc[...] = vec_acc[...].astype(bf16).astype(f32)
    for row in range(vec_rows):
        vec[row : row + 1] = jnp.concatenate(
            [vec_acc[row * per + k : row * per + k + 1] for k in range(per)], axis=1
        )
    saves = []

    def save(source, target):
        copy = pltpu.make_async_copy(source, target, save_sem.at[len(saves)])
        copy.start()
        saves.append(copy)

    save(vec, vec_hbm)

    for copy in token_copies[: seq - 1]:
        copy.wait_recv()
    tile = min(256, length)
    per_seq = length // tile
    save(high, high_hbm)
    scale = HD**-0.5

    for m, target in enumerate((query, key, value)):
        flows.pump(flows.last_step(m))
        matrix = attn_buf.at[m].reshape(width, width)

        def project(i, _):
            sequence, at = i // per_seq, pl.ds(pl.multiple_of(lax.rem(i, per_seq) * tile, tile), tile)
            result = dot(high[sequence, at], matrix[...])
            if m == 0:
                result = (result + vec[0:1]).astype(bf16) * scale
            elif m == 2:
                result = result + vec[1:2]
            target[sequence, at] = result.astype(bf16)
            return 0

        lax.fori_loop(0, own * per_seq, project, 0)
        save(target, (query_hbm, key_hbm, value_hbm)[m])

    context = send_high.reshape(own, length, width)
    for copy in token_copies[: seq - 1]:
        copy.wait_send()
    pairs = width // 128
    turns = own * pairs
    lane = lax.broadcasted_iota(jnp.int32, (1, 128), 1)

    def attend(i, _):
        for k in range(during):
            @pl.when(i == (k + 1) * turns // (during + 1))
            def _():
                flows.step(flows.now + k)

        sequence, pair = i // pairs, lax.rem(i, pairs)
        at = pl.ds(pl.multiple_of(pair * 128, 128), 128)
        keys, values = key[sequence, :, at], value[sequence, :, at]
        for q in range(per_seq):
            places = slice(q * tile, (q + 1) * tile)
            queries = query[sequence, places, at]
            heads = []
            for head in range(2):
                picked = jnp.where(lane // HD == head, queries, jnp.zeros_like(queries))
                scores = dot_t(picked, keys)
                exponent = jnp.exp(scores - jnp.max(scores, -1, keepdims=True))
                total = jnp.sum(exponent, -1, keepdims=True)
                heads.append(dot(exponent.astype(bf16), values) / total)
            context[sequence, places, at] = jnp.where(lane < HD, heads[0], heads[1]).astype(bf16)
        return 0

    during = DURING
    lax.fori_loop(0, turns, attend, 0)
    flows.now += during
    flows.pump(flows.last_step(4))

    for copy in token_copies[seq - 1 :]:
        copy.wait_recv()
    out_matrix = attn_buf.at[3].reshape(width, width)

    def front(i, _):
        sequence, at = i // per_seq, pl.ds(pl.multiple_of(lax.rem(i, per_seq) * tile, tile), tile)
        x = high[sequence, at].astype(f32) + rest[sequence, at].astype(f32)
        x = x + (dot(context[sequence, at], out_matrix[...]) + vec[2:3])
        x, _ = normalize(x)
        norm[sequence, at] = x * vec[4:5] + vec[5:6]
        return 0

    lax.fori_loop(0, own * per_seq, front, 0)

    place_ids = lax.broadcasted_iota(jnp.int32, (length, slots), 0)
    for sequence in range(own):
        at = pl.ds(sequence * slots, slots)
        hits = places_ref[pl.ds(place.s * own + sequence, 1)] == place_ids
        hits = jnp.where(hits, 1.0, 0.0).astype(bf16)
        slot_high = t_dot(hits, high[sequence])
        slot_low[0, at] = slot_high.astype(bf16)
        slot_context = t_dot(hits, context[sequence]).astype(bf16)
        slot_low[1, at] = slot_context
        slot_low[2, at] = t_dot(hits, query[sequence]).astype(bf16)
        slot[0, at] = slot_high
        slot[1, at] = t_dot(hits, rest[sequence])
        x = slot[0, at] + slot[1, at]
        x = x + (dot(slot_context, out_matrix[...]) + vec[2:3])
        x, inverse = normalize(x)
        slot[0, at] = x
        slot[2, at] = jnp.broadcast_to(inverse, x.shape)
        x = x * vec[4:5] + vec[5:6]
        slot[1, at] = x
        slot_low[3, at] = x.astype(bf16)
    save(slot_low, slot_low_hbm)
    save(attn_buf, attn_hbm)

    in_matrix = in_buf.reshape(width, in_buf.shape[-1])
    for j in range(in_buf.shape[-1] // width):
        flows.pump(flows.last_step(4 + j))
        at = pl.ds(j * width, width)
        bias = vec[8 + j : 9 + j]

        def hidden(i, _):
            sequence, here = i // per_seq, pl.ds(pl.multiple_of(lax.rem(i, per_seq) * tile, tile), tile)
            x = dot(norm[sequence, here].astype(bf16), in_matrix[:, at]) + bias
            active[sequence, here, at] = (0.5 * x * (1.0 + erf(x * 0.5**0.5))).astype(bf16)
            return 0

        lax.fori_loop(0, own * per_seq, hidden, 0)
        x = dot(slot_low[3], in_matrix[:, at]) + bias
        half = 0.5 * (1.0 + erf(x * 0.5**0.5))
        slot_active[:, at] = (x * half).astype(bf16)
        slot_slope[:, at] = half + x * jnp.exp(-0.5 * x * x) * 0.3989422804014327
    save(slot_active, slot_active_hbm)
    save(slot_slope, slot_slope_hbm)
    save(in_buf, in_hbm)

    out_matrix = out_buf.reshape(out_buf.shape[-2] * place.groups, width)
    wide = width // 3
    for j in range(3):
        flows.pump(flows.last_step(len(flows.chunks) - 3 + j))
        at = slice(j * wide, (j + 1) * wide)
        save(out_buf.at[tuple(slice(None) for _ in range(place.bits + 1)) + (at,)],
             out_hbm.at[tuple(slice(None) for _ in range(place.bits + 1)) + (at,)])
        bias = vec[3:4, at]
        slot[1, :, at] = slot[1, :, at] + (dot(slot_active[...], out_matrix[:, at]) + bias)
        if j == 2:
            save(slot, slot_hbm)

        def feed(i, _):
            sequence, here = i // per_seq, pl.ds(pl.multiple_of(lax.rem(i, per_seq) * tile, tile), tile)
            x = dot(active[sequence, here], out_matrix[:, at]) + bias
            norm[sequence, here, at] = norm[sequence, here, at] + x
            return 0

        lax.fori_loop(0, own * per_seq, feed, 0)
    for copy in token_copies[seq - 1 :]:
        copy.wait_send()
    output = send_rest.reshape(own, length, width)

    def back(i, _):
        sequence, here = i // per_seq, pl.ds(pl.multiple_of(lax.rem(i, per_seq) * tile, tile), tile)
        x, _ = normalize(norm[sequence, here])
        output[sequence, here] = (x * vec[6:7] + vec[7:8]).astype(bf16)
        return 0

    lax.fori_loop(0, own * per_seq, back, 0)
    save(output, output_hbm)
    flows.finish()
    for copy in mate_copies + vec_mates:
        copy.wait_send()
    for stage in range(flows.stages):
        vec_copy(stage).wait_send()
    for copy in saves:
        copy.wait()


def forward_call(mesh, tokens, positions, attn_weights, ffn_in, ffn_out, vectors):
    place = Place(mesh, ffn_in.shape[0])
    sequences, block, width = tokens.shape
    inner = ffn_in.shape[1]
    slots = positions.shape[1]
    own = sequences // place.seq
    length = block * place.seq
    vec_count = vectors.shape[0]
    vec_rows = vec_count * place.devices // width
    owner = lax.axis_index("seq") * place.dp + lax.axis_index("dp")
    padded = lax.dynamic_update_slice_in_dim(
        jnp.zeros((1024,), f32), vectors.astype(bf16).astype(f32), lax.rem(vec_count * owner, 128), 0
    ).reshape(8, 128)
    bits = (2,) * place.bits
    r = ffn_in.shape[0]
    joint = r * place.merge
    joint_out = ffn_out.shape[0] * place.merge
    flow_count = (4 + inner // width + 3) * 3 * (place.bits + 1)
    attn_shape = (4,) + bits + (joint, width)
    in_shape = bits + (joint, inner)
    out_shape = bits + (joint_out, width)
    seq_shape = (own, length, width)
    rows = own * slots
    results = [
        (attn_shape, bf16),
        (in_shape, bf16),
        (out_shape, bf16),
        ((16, width), f32),
        (seq_shape, bf16),
        (seq_shape, bf16),
        (seq_shape, bf16),
        (seq_shape, bf16),
        (seq_shape, bf16),
        ((4, rows, width), bf16),
        ((3, rows, width), f32),
        ((rows, inner), bf16),
        ((rows, inner), f32),
    ]
    vmem = pl.BlockSpec(memory_space=pltpu.VMEM)
    hbm = pl.BlockSpec(memory_space=pl.ANY)
    dma = pltpu.SemaphoreType.DMA
    mates = place.merge - 1
    return pl.pallas_call(
        functools.partial(forward_kernel, place, vec_rows, vec_count),
        out_shape=[jax.ShapeDtypeStruct(*one) for one in results],
        in_specs=[vmem, vmem, hbm, hbm, hbm, vmem],
        out_specs=[hbm] * len(results),
        scratch_shapes=[
            pltpu.VMEM(attn_shape, bf16),
            pltpu.VMEM(in_shape, bf16),
            pltpu.VMEM(out_shape, bf16),
            pltpu.VMEM(bits + (place.merge, 8, 128), f32),
            pltpu.VMEM((vec_rows * width // 128 + 8, 128), f32),
            pltpu.VMEM((16, width), f32),
            pltpu.VMEM((place.merge,) + attn_weights.shape, f32),
            pltpu.VMEM((place.merge,) + ffn_in.shape, f32),
            pltpu.VMEM((place.merge,) + ffn_out.shape, f32),
            pltpu.VMEM((joint_out, inner), f32),
            pltpu.VMEM((sequences, block, width), bf16),
            pltpu.VMEM((sequences, block, width), bf16),
            pltpu.VMEM(seq_shape, bf16),
            pltpu.VMEM(seq_shape, bf16),
            pltpu.VMEM(seq_shape, bf16),
            pltpu.VMEM(seq_shape, bf16),
            pltpu.VMEM(seq_shape, bf16),
            pltpu.VMEM(seq_shape, f32),
            pltpu.VMEM((own, length, inner), bf16),
            pltpu.VMEM((4, rows, width), bf16),
            pltpu.VMEM((3, rows, width), f32),
            pltpu.VMEM((rows, inner), bf16),
            pltpu.VMEM((rows, inner), f32),
            dma((flow_count,)),
            dma((flow_count,)),
            dma((3 * mates,)),
            dma((3 * mates,)),
            dma((3,)),
            dma((2 * (place.seq - 1),)),
            dma((2 * (place.seq - 1),)),
            dma((mates + place.bits,)),
            dma((mates + place.bits,)),
            dma((len(results) + 2,)),
        ],
        compiler_params=pltpu.CompilerParams(
            collective_id=0, has_side_effects=True, vmem_limit_bytes=64 * 2**20 - 2**18
        ),
    )(tokens, positions, attn_weights, ffn_in, ffn_out, padded)


SPACING = 4
INSIDE = 8


class Scatter(Flows):
    def __init__(self, place, chunks, send, recv, landings, finals):
        super().__init__(place, chunks, send, recv)
        self.landings = landings
        self.finals = finals

    def boxes(self, order, stage):
        place = self.place
        done = order[:stage]
        dim = order[stage]
        out, mine, came = [], [], []
        for d in range(place.bits):
            if d in done:
                picks = (place.bit[d],) * 3
            elif d == dim:
                picks = (1 - place.bit[d], place.bit[d], 1 - place.bit[d])
            else:
                picks = (slice(None),) * 3
            out.append(picks[0])
            mine.append(picks[1])
            came.append(picks[2])
        return tuple(out), tuple(mine), tuple(came)

    def copy(self, chunk, part, stage):
        buf, rows, columns, order = self.chunks[chunk].part(part, self.place)
        n = self.number(chunk, part, stage)
        out, mine, _ = self.boxes(order, stage)
        return pltpu.make_async_remote_copy(
            src_ref=buf.at[out + (rows, columns)],
            dst_ref=self.landings[chunk].at[mine + (rows, columns)],
            send_sem=self.send.at[n],
            recv_sem=self.recv.at[n],
            device_id=self.place.across(order[stage]),
            device_id_type=MESH,
        )

    def begin(self, *chunks):
        for chunk in chunks:
            for part in range(3):
                self.copy(chunk, part, 0).start()

    def advance(self, chunk, stage):
        for part in range(3):
            self.sum_up(chunk, part, stage)

    def sum_up(self, chunk, part, stage):
        self.copy(chunk, part, stage).wait_recv()
        buf, rows, columns, order = self.chunks[chunk].part(part, self.place)
        _, mine, came = self.boxes(order, stage)
        tail = (rows, columns)
        total = buf.at[mine + tail][...].astype(f32)
        total = total + self.landings[chunk].at[came + tail][...].astype(f32)
        if stage + 1 < self.stages:
            buf.at[mine + tail][...] = total.astype(bf16)
            self.copy(chunk, part, stage + 1).start()
        else:
            self.finals[chunk].at[tail][...] = total

    def finish(self):
        for chunk in range(len(self.chunks)):
            for part in range(3):
                for stage in range(self.stages):
                    self.copy(chunk, part, stage).wait_send()


class Part:
    def __init__(self, buf, first, width, orders, cuts=None):
        self.buf, self.first, self.width, self.orders, self.cuts = buf, first, width, orders, cuts

    def size(self, part):
        rows = self.buf.shape[-2]
        if self.cuts is None:
            return rows * (self.width // 3)
        return (self.cuts[part + 1] - self.cuts[part]) * self.width

    def part(self, part, place):
        if self.cuts is None:
            third = self.width // 3
            columns = pl.ds(self.first + part * third, third)
            return self.buf, slice(None), columns, self.orders[part]
        rows = pl.ds(self.cuts[part], self.cuts[part + 1] - self.cuts[part])
        return self.buf, rows, pl.ds(self.first, self.width), self.orders[part]


def gradient_chunks(place, attn, first_ffn, second_ffn):
    forward = weight_chunks(place, attn, first_ffn, second_ffn, True)
    half = attn.shape[-1]
    chunks = []
    for j in range(3):
        chunks.append(
            Part(second_ffn, j * half // 3, half // 3, forward[-3 + j].orders, forward[-3 + j].cuts)
        )
    for j in range(first_ffn.shape[-1] // half):
        chunks.append(Part(first_ffn, j * half, half, forward[4 + j].orders))
    for m in (3, 0, 1, 2):
        chunks.append(Part(attn.at[m], 0, half, forward[m].orders))
    return chunks


def column_total(x):
    return jnp.sum(x, axis=0, keepdims=True)


def backward_kernel(
    place,
    attn_hbm,
    in_hbm,
    out_hbm,
    vec,
    high_hbm,
    key_hbm,
    value_hbm,
    output_hbm,
    slot_low_hbm,
    slot_hbm,
    slot_active_hbm,
    slot_slope_hbm,
    places_ref,
    counts_ref,
    cotangent_hbm,
    output_ref,
    grad_tokens_ref,
    final_attn_hbm,
    final_in_hbm,
    final_out_hbm,
    vec_grad_ref,
    square_ref,
    mats,
    last,
    out_buf,
    grad_attn,
    grad_in,
    grad_out,
    land_attn,
    land_in,
    land_out,
    final_attn,
    final_in,
    final_out,
    tokens_both,
    key,
    value,
    active_both,
    inner_both,
    slope,
    low_both,
    slot,
    feed_both,
    attended_both,
    query_both,
    context_back,
    sum_two,
    key_back,
    value_back,
    key_both,
    value_both,
    stage_tokens,
    vec_sum,
    vec_land,
    square,
    square_land,
    flow_send,
    flow_recv,
    load_sem,
    pair_send,
    pair_recv,
    row_send,
    row_recv,
    own_sem,
    vec_send,
    vec_recv,
    final_send,
    final_recv,
    square_send,
    square_recv,
    extra_land=None,
    extra_send=None,
    extra_recv=None,
):
    place.here()
    place.greet_all()
    merge, seq = place.merge, place.seq
    width = out_buf.shape[-1]
    inner = active_both.shape[-1]
    half = width // 2
    own, length = key.shape[:2]
    block = length // seq
    slots = sum_two.shape[1]
    rows = own * slots
    tile = min(256, length)
    per_seq = length // tile
    scale = HD**-0.5
    my_half = pl.ds(pl.multiple_of(place.core * half, 128), half)
    other_half = pl.ds(pl.multiple_of((1 - place.core) * half, 128), half)
    loads = []
    pairs = []
    sum_one = slope.at[:rows, :width]

    def load(source, target):
        copy = pltpu.make_async_copy(source, target, load_sem.at[len(loads)])
        copy.start()
        loads.append(copy)
        return copy

    def share(source, target):
        n = len(pairs)
        copy = pltpu.make_async_remote_copy(
            src_ref=source,
            dst_ref=target,
            send_sem=pair_send.at[n],
            recv_sem=pair_recv.at[n],
            device_id=place.other_core(),
            device_id_type=MESH,
        )
        copy.start()
        pairs.append(copy)
        return copy

    got_slot = load(slot_hbm, slot)
    got_cotangent = load(cotangent_hbm.at[pl.ds(place.s * own, own)], sum_two)
    got_out = load(out_hbm, out_buf)
    got_slope = load(slot_slope_hbm, slope.at[:rows])
    got_active = load(slot_active_hbm, active_both.at[0])
    came_active = share(slot_active_hbm, active_both.at[1])
    got_low = load(slot_low_hbm, low_both.at[0])
    came_low = share(slot_low_hbm, low_both.at[1])
    inner_parts = inner // width
    free = (slice(None),) * (place.bits + 1)
    got_in = [
        load(in_hbm.at[free + (pl.ds(j * width, width),)], mats.at[j]) for j in range(inner_parts)
    ]
    got_last = load(attn_hbm.at[3], last)
    got_key = load(key_hbm, key)
    got_value = load(value_hbm, value)
    got_tokens = load(high_hbm, tokens_both.at[0])
    came_tokens = share(high_hbm, tokens_both.at[1])

    sends = []
    owns = []

    def send_rows(stage, target, sequence):
        for k, device in enumerate(place.row_mates()):
            n = len(sends)
            copy = pltpu.make_async_remote_copy(
                src_ref=stage.at[sequence, pl.ds(pl.multiple_of(device[0] * block, block), block)],
                dst_ref=target.at[place.s * own + sequence],
                send_sem=row_send.at[n],
                recv_sem=row_recv.at[n],
                device_id=device,
                device_id_type=MESH,
            )
            copy.start()
            sends.append(copy)
        copy = pltpu.make_async_copy(
            stage.at[sequence, pl.ds(pl.multiple_of(place.s * block, block), block)],
            target.at[place.s * own + sequence],
            own_sem.at[len(owns)],
        )
        copy.start()
        owns.append(copy)

    for sequence in range(own):
        send_rows(output_hbm, output_ref, sequence)

    chunks = gradient_chunks(place, grad_attn, grad_in, grad_out)
    finals = [final_out] * 3 + [final_in] * inner_parts * 2 + [final_attn.at[m] for m in (3, 0, 1, 2)]
    landings = [land_out] * 3 + [land_in] * inner_parts + [land_attn.at[m] for m in (3, 0, 1, 2)]
    finals = [final_out] * 3 + [final_in] * inner_parts + finals[-4:]
    flows = Scatter(place, chunks, flow_send, flow_recv, landings, finals)

    vec_sum[...] = jnp.zeros_like(vec_sum)
    got_slot.wait()
    got_cotangent.wait()
    out_matrix = out_buf.reshape(inner, width)
    normal, inverse = normalize(slot[1])
    for sequence in range(own):
        slot_ids = lax.broadcasted_iota(jnp.int32, (slots, 1), 0)
        live = slot_ids < counts_ref[place.s * own + sequence]
        sum_two[sequence] = jnp.where(live, sum_two[sequence], 0.0)
    grad = sum_two[...].reshape(rows, width)
    vec_sum[0, 6:7] = column_total(grad * normal)
    vec_sum[0, 7:8] = column_total(grad)
    grad = grad * vec[6:7]
    grad = inverse * (
        grad
        - jnp.mean(grad, -1, keepdims=True)
        - normal * jnp.mean(grad * normal, -1, keepdims=True)
    )
    sum_two[...] = grad.reshape(own, slots, width)
    feed_low = grad.astype(bf16)
    feed_both[0] = feed_low
    vec_sum[0, 3:4] = column_total(feed_low.astype(f32))
    came_feed = share(feed_both.at[0], feed_both.at[1])

    got_slope.wait()
    got_out.wait()
    for j in range(inner_parts):
        at = pl.ds(j * width, width)
        back = dot_t(feed_both[0], out_matrix[at]) * slope[:rows, at]
        low = back.astype(bf16)
        inner_both[0, :, at] = low
        vec_sum[0, 8 + j : 9 + j] = column_total(low.astype(f32))
    came_inner = share(inner_both.at[0], inner_both.at[1])

    got_active.wait()
    came_active.wait_recv()
    came_feed.wait_recv()
    all_active = active_both.reshape(2 * rows, inner)
    all_feed = feed_both.reshape(2 * rows, width)
    out_rows = grad_out.reshape(inner, half)

    def second_matrix(i, _):
        at = pl.ds(pl.multiple_of(i * half, 128), half)
        out_rows[at] = t_dot(all_active[:, at], all_feed[:, my_half]).astype(bf16)
        return 0

    lax.fori_loop(0, inner // half, second_matrix, 0)
    flows.begin(0, 1, 2)

    got_low.wait()
    came_low.wait_recv()
    came_inner.wait_recv()
    all_inner = inner_both.reshape(2 * rows, inner)
    in_rows = grad_in.reshape(width, inner // 2)
    first_low = low_both[:, 3].reshape(2 * rows, width)
    for j in range(inner_parts):
        start = pl.multiple_of(place.core * (inner // 2) + j * half, 128)
        result = t_dot(first_low, all_inner[:, pl.ds(start, half)])
        in_rows[:, pl.ds(j * half, half)] = result.astype(bf16)
        flows.begin(3 + j)

    for copy in got_in:
        copy.wait()
    grad = sum_two[...].reshape(rows, width)
    for j in range(inner_parts):
        at = pl.ds(j * width, width)
        grad = grad + dot_t(inner_both[0, :, at], mats.at[j].reshape(width, width)[...])
    normal = slot[0]
    vec_sum[0, 4:5] = column_total(grad * normal)
    vec_sum[0, 5:6] = column_total(grad)
    grad = grad * vec[4:5]
    grad = slot[2] * (
        grad
        - jnp.mean(grad, -1, keepdims=True)
        - normal * jnp.mean(grad * normal, -1, keepdims=True)
    )
    sum_one[...] = grad
    low = grad.astype(bf16)
    attended_both[0] = low
    vec_sum[0, 2:3] = column_total(low.astype(f32))
    came_attended = share(attended_both.at[0], attended_both.at[1])
    got_attn = [load(attn_hbm.at[m], mats.at[m]) for m in range(3)]
    got_last.wait()
    context_back[...] = dot_t(low, last.reshape(width, width)[...]).astype(bf16)
    came_attended.wait_recv()
    result = t_dot(
        low_both[:, 1].reshape(2 * rows, width),
        attended_both.reshape(2 * rows, width)[:, my_half],
    )
    grad_attn.at[3].reshape(width, half)[...] = result.astype(bf16)
    flows.begin(3 + inner_parts)

    got_key.wait()
    got_value.wait()
    pair_count = width // 128
    turns = own * pair_count
    lane = lax.broadcasted_iota(jnp.int32, (1, 128), 1)
    order = sorted(
        ((chunk, stage) for chunk in range(len(chunks)) for stage in range(flows.stages)),
        key=lambda item: (item[0] + SPACING * item[1], item[0]),
    )
    during = order[:INSIDE]
    order = order[INSIDE:]

    def attend(i, _):
        for n, item in enumerate(during):
            @pl.when(i == n + 2)
            def _():
                flows.advance(*item)

        sequence, pair = i // pair_count, lax.rem(i, pair_count)
        at = pl.ds(pl.multiple_of(pair * 128, 128), 128)
        slot_at = pl.ds(pl.multiple_of(sequence * slots, slots), slots)
        keys, values = key[sequence, :, at], value[sequence, :, at]
        queries, backs = low_both[0, 2, slot_at, at], context_back[slot_at, at]
        zero = jnp.zeros_like(queries)
        outs = []
        for head in range(2):
            chosen = lane // HD == head
            scores = dot_t(jnp.where(chosen, queries, zero), keys)
            exponent = jnp.exp(scores - jnp.max(scores, -1, keepdims=True))
            probs = exponent / jnp.sum(exponent, -1, keepdims=True)
            grad_probs = dot_t(jnp.where(chosen, backs, zero), values)
            delta = jnp.sum(probs * grad_probs, -1, keepdims=True)
            scores_back = (probs * (grad_probs - delta)).astype(bf16)
            outs.append(
                (
                    dot(scores_back, keys) * scale,
                    t_dot(scores_back, queries),
                    t_dot(probs.astype(bf16), backs),
                )
            )
        left = lane < HD
        query_both[0, slot_at, at] = jnp.where(left, outs[0][0], outs[1][0]).astype(bf16)
        key_back[sequence, :, at] = jnp.where(left, outs[0][1], outs[1][1]).astype(bf16)
        value_back[sequence, :, at] = jnp.where(left, outs[0][2], outs[1][2]).astype(bf16)
        return 0

    lax.fori_loop(0, turns, attend, 0)
    came_query = share(query_both.at[0], query_both.at[1])
    came_key = share(key_back.at[:, :, other_half], key_both.at[1])
    came_value = share(value_back.at[:, :, other_half], value_both.at[1])
    key_both[0] = key_back[:, :, my_half]
    value_both[0] = value_back[:, :, my_half]
    total = jnp.zeros((1, width), f32)
    for sequence in range(own):
        total = total + column_total(value_back[sequence].astype(f32))
    vec_sum[0, 1:2] = total
    vec_sum[0, 0:1] = column_total(query_both[0].astype(f32))

    def vec_copy(stage):
        return pltpu.make_async_remote_copy(
            src_ref=vec_sum.at[stage],
            dst_ref=vec_land.at[stage],
            send_sem=vec_send.at[stage],
            recv_sem=vec_recv.at[stage],
            device_id=place.partner(stage),
            device_id_type=MESH,
        )

    vec_copy(0).start()

    def vec_next(stage):
        vec_copy(stage).wait_recv()
        vec_sum[stage + 1] = vec_sum[stage] + vec_land[stage]
        if stage + 1 < place.levels:
            vec_copy(stage + 1).start()

    came_query.wait_recv()
    result = t_dot(
        low_both[:, 0].reshape(2 * rows, width), query_both.reshape(2 * rows, width)[:, my_half]
    )
    grad_attn.at[0].reshape(width, half)[...] = result.astype(bf16)
    flows.begin(4 + inner_parts)
    got_tokens.wait()
    came_tokens.wait_recv()
    all_tokens = tokens_both.reshape(2 * own * length, width)
    for m, (came, both) in enumerate(((came_key, key_both), (came_value, value_both))):
        came.wait_recv()
        all_back = both.reshape(2 * own * length, half)
        target = grad_attn.at[1 + m].reshape(width, half)

        def weight(i, _):
            at = pl.ds(pl.multiple_of(i * tile, 128), tile)
            target[at] = t_dot(all_tokens[:, at], all_back[...]).astype(bf16)
            return 0

        lax.fori_loop(0, width // tile, weight, 0)
        flows.begin(5 + inner_parts + m)

    def pump(count):
        for _ in range(min(count, len(order))):
            flows.advance(*order.pop(0))

    for copy in got_attn:
        copy.wait()
    query_matrix, key_matrix, value_matrix = (mats.at[m].reshape(width, width) for m in range(3))
    spread = sum_one[...] + dot_t(query_both[0], query_matrix[...])
    top = spread.astype(bf16)
    context_back[...] = top
    feed_rest = (spread - top.astype(f32)).astype(bf16)
    low_both[0, 3] = feed_rest
    place_ids = lax.broadcasted_iota(jnp.int32, (length, slots), 0)
    pump(2)
    for sequence in range(own):
        hits = places_ref[pl.ds(place.s * own + sequence, 1)] == place_ids
        hits = jnp.where(hits, 1.0, 0.0).astype(bf16)
        slot_at = pl.ds(sequence * slots, slots)
        for q in range(per_seq):
            at = slice(q * tile, (q + 1) * tile)
            result = dot_t(key_back[sequence, at], key_matrix[...])
            result = result + dot_t(value_back[sequence, at], value_matrix[...])
            result = result + dot(hits[at], context_back[slot_at])
            result = result + dot(hits[at], low_both[0, 3, slot_at])
            stage_tokens[sequence, at] = result.astype(bf16)
        send_rows(stage_tokens, grad_tokens_ref, sequence)
        vec_next(sequence)
        pump(3)

    for stage in range(own, place.levels):
        vec_next(stage)
        pump(3)
    vec_grad_ref[...] = vec_sum[place.levels]
    pump(len(order))

    final = (final_attn, final_in, final_out)
    for n in range(place.levels - place.bits - 1):
        for index in range(3):
            k = n * 3 + index
            copy = pltpu.make_async_remote_copy(
                src_ref=final[index],
                dst_ref=extra_land[index].at[n],
                send_sem=extra_send.at[k],
                recv_sem=extra_recv.at[k],
                device_id=place.partner(n + 1),
                device_id_type=MESH,
            )
            copy.start()
            copy.wait()
            final[index][...] = final[index][...] + extra_land[index][n]

    hbm = (final_attn_hbm, final_in_hbm, final_out_hbm)
    final_copies = []
    for index in range(3):
        for k, device in enumerate(place.mates()):
            n = index * (merge - 1) + k
            copy = pltpu.make_async_remote_copy(
                src_ref=final[index],
                dst_ref=hbm[index].at[place.member],
                send_sem=final_send.at[n],
                recv_sem=final_recv.at[n],
                device_id=device,
                device_id_type=MESH,
            )
            copy.start()
            final_copies.append(copy)
        copy = pltpu.make_async_copy(
            final[index], hbm[index].at[place.member], own_sem.at[len(owns)]
        )
        copy.start()
        owns.append(copy)
    total = jnp.zeros((1, 1), f32)
    for part in (final_attn[...], final_in[...], final_out[...]):
        part = jnp.sum((part * part).reshape(-1, part.shape[-1]), axis=0, keepdims=True)
        total = total + jnp.sum(part, axis=1, keepdims=True)
    square[...] = jnp.broadcast_to(total, (8, 128)) * (2.0 / merge)
    all_reduce(place, square, square_land, square_send, square_recv)
    rest = vec_sum[place.levels]
    rest = jnp.sum(jnp.sum(rest * rest, axis=0, keepdims=True), axis=1, keepdims=True)
    square_ref[...] = square[...] + rest

    flows.finish()
    for copy in pairs + sends:
        copy.wait_send()
    for copy in sends:
        copy.wait_recv()
    for copy in owns:
        copy.wait()
    for copy in final_copies:
        copy.wait()
    for stage in range(place.levels):
        vec_copy(stage).wait_send()


def all_reduce(place, block, land, send, recv):
    for first, count, me, device in (
        (0, place.dp, place.d, lambda other: (place.s, other)),
        (place.dp, place.seq, place.s, lambda other: (other, place.d)),
    ):

        def copy(k, first=first, count=count, me=me, device=device):
            return pltpu.make_async_remote_copy(
                src_ref=block,
                dst_ref=land.at[first + k],
                send_sem=send.at[first + k],
                recv_sem=recv.at[first + k],
                device_id=device(lax.rem(me + k, count)),
                device_id_type=MESH,
            )

        for k in range(1, count):
            copy(k).start()
        land[first] = block[...]
        for k in range(1, count):
            copy(k).wait_recv()
        for k in range(1, count):
            copy(k).wait_send()
        total = land[first + me]
        for k in range(1, count):
            total = total + land[first + lax.rem(me - k + count, count)]
        block[...] = total


def backward_call(mesh, forward, positions, counts, cotangent, rows):
    attn, ffn_in, ffn_out, vec, high, query, key, value, output, slot_low, slot, slot_active, slope = forward
    place = Place(mesh, rows)
    own, length, width = high.shape
    inner = ffn_in.shape[-1]
    sequences = positions.shape[0]
    block = length // place.seq
    slots = positions.shape[1]
    count = own * slots
    half = width // 2
    bits = (2,) * place.bits
    joint, joint_out = ffn_in.shape[-2], ffn_out.shape[-2]
    merge = place.merge
    dma = pltpu.SemaphoreType.DMA
    vmem = pl.BlockSpec(memory_space=pltpu.VMEM)
    hbm = pl.BlockSpec(memory_space=pl.ANY)
    smem = pl.BlockSpec(memory_space=pltpu.SMEM)
    flow_count = (4 + inner // width + 3) * 3 * (place.bits + 1)
    tile = min(256, length)
    finals = [(4, joint, half), (joint, inner // 2), (joint_out, half)]
    extra = place.levels - place.bits - 1
    scratch = [
        pltpu.VMEM((4,) + bits + (joint, width), bf16),
        pltpu.VMEM(bits + (joint, width), bf16),
        pltpu.VMEM(bits + (joint_out, width), bf16),
    ]
    for _ in range(2):
        scratch += [
            pltpu.VMEM((4,) + bits + (joint, half), bf16),
            pltpu.VMEM(bits + (joint, inner // 2), bf16),
            pltpu.VMEM(bits + (joint_out, half), bf16),
        ]
    scratch += [pltpu.VMEM(shape, f32) for shape in finals]
    scratch += [
        pltpu.VMEM((2, own, length, width), bf16),
        pltpu.VMEM((own, length, width), bf16),
        pltpu.VMEM((own, length, width), bf16),
        pltpu.VMEM((2, count, inner), bf16),
        pltpu.VMEM((2, count, inner), bf16),
        pltpu.VMEM((max(count, tile), inner), f32),
        pltpu.VMEM((2, 4, count, width), bf16),
        pltpu.VMEM((3, count, width), f32),
        pltpu.VMEM((2, count, width), bf16),
        pltpu.VMEM((2, count, width), bf16),
        pltpu.VMEM((2, count, width), bf16),
        pltpu.VMEM((count, width), bf16),
        pltpu.VMEM((own, slots, width), f32),
        pltpu.VMEM((own, length, width), bf16),
        pltpu.VMEM((own, length, width), bf16),
        pltpu.VMEM((2, own, length, half), bf16),
        pltpu.VMEM((2, own, length, half), bf16),
        pltpu.VMEM((own, length, width), bf16),
        pltpu.VMEM((place.levels + 1, 16, width), f32),
        pltpu.VMEM((place.levels, 16, width), f32),
        pltpu.VMEM((8, 128), f32),
        pltpu.VMEM((place.dp + place.seq, 8, 128), f32),
        dma((flow_count,)),
        dma((flow_count,)),
        dma((24,)),
        dma((16,)),
        dma((16,)),
        dma((2 * own * (place.seq - 1),)),
        dma((2 * own * (place.seq - 1),)),
        dma((2 * own + 3,)),
        dma((place.levels,)),
        dma((place.levels,)),
        dma((3 * (merge - 1),)),
        dma((3 * (merge - 1),)),
        dma((place.dp + place.seq,)),
        dma((place.dp + place.seq,)),
    ]
    if extra:
        scratch += [
            [pltpu.VMEM((extra,) + shape, f32) for shape in finals],
            dma((3 * extra,)),
            dma((3 * extra,)),
        ]
    results = [
        ((sequences, block, width), bf16),
        ((sequences, block, width), bf16),
        ((merge,) + finals[0], f32),
        ((merge,) + finals[1], f32),
        ((merge,) + finals[2], f32),
        ((16, width), f32),
        ((8, 128), f32),
    ]
    return pl.pallas_call(
        functools.partial(backward_kernel, place),
        out_shape=[jax.ShapeDtypeStruct(*one) for one in results],
        in_specs=[hbm, hbm, hbm, vmem] + [hbm] * 8 + [vmem, smem, hbm],
        out_specs=[hbm] * 5 + [vmem] * 2,
        scratch_shapes=scratch,
        compiler_params=pltpu.CompilerParams(
            collective_id=1, has_side_effects=True, vmem_limit_bytes=64 * 2**20 - 2**18
        ),
    )(
        attn, ffn_in, ffn_out, vec, high, key, value, output, slot_low, slot,
        slot_active, slope, positions, counts, cotangent,
    )


def total_kernel(place, block_ref, total_ref, block, land, send, recv):
    place.here()
    place.greet_all()
    block[...] = block_ref[...]
    all_reduce(place, block, land, send, recv)
    total_ref[...] = block[...]


def total_call(mesh, rows, block):
    place = Place(mesh, rows)
    vmem = pl.BlockSpec(memory_space=pltpu.VMEM)
    dma = pltpu.SemaphoreType.DMA
    count = place.dp + place.seq
    return pl.pallas_call(
        functools.partial(total_kernel, place),
        out_shape=jax.ShapeDtypeStruct((8, 128), f32),
        in_specs=[vmem],
        out_specs=vmem,
        scratch_shapes=[
            pltpu.VMEM((8, 128), f32),
            pltpu.VMEM((count, 8, 128), f32),
            dma((count,)),
            dma((count,)),
        ],
        compiler_params=pltpu.CompilerParams(collective_id=2, has_side_effects=True),
    )(block)


def pieces_of(shapes):
    attn, first, second = shapes
    half = attn[-1] // 2
    found = []
    for m in range(attn[0]):
        for core in range(2):
            found.append((0, core, (m,), pl.ds(core * half, half), m))
    for n, shape in ((1, first), (2, second)):
        half = shape[-1] // 2
        for core in range(2):
            found.append((n, core, (), pl.ds(core * half, half), 3 + n))
    return found


def update_kernel(place, *refs):
    finals, square, olds, firsts, seconds = refs[:3], refs[3], refs[4:7], refs[7:10], refs[10:13]
    clipped, new_firsts, new_seconds, directions = refs[13:16], refs[16:19], refs[19:22], refs[22:25]
    sums = refs[25]
    place.here()
    clip = 1.0 / jnp.maximum(jnp.sqrt(square[0:1, 0:1]), 1.0)
    correct = 1.0 - decay_rate**STEP
    row = lax.broadcasted_iota(jnp.int32, (8, 128), 0)
    lane = lax.broadcasted_iota(jnp.int32, (8, 128), 1)

    def total_of(x):
        return jnp.sum(jnp.sum(x * x, axis=0, keepdims=True), axis=1, keepdims=True)

    for member in range(place.merge):

        @pl.when(place.member == member)
        def _():
            block = jnp.zeros((8, 128), f32)
            for n, core, lead, columns, which in pieces_of([ref.shape for ref in olds]):
                count = olds[n].shape[-2]
                at = lead + (slice(None), columns)
                grad = finals[n][(core,) + lead + (slice(member * count, (member + 1) * count),)]
                grad = grad * clip
                clipped[n][at] = grad
                first = decay_rate * firsts[n][at] + (1.0 - decay_rate) * grad
                second = decay_rate * seconds[n][at] + (1.0 - decay_rate) * grad * grad
                new_firsts[n][at] = first
                new_seconds[n][at] = second
                old = olds[n][at]
                way = first / correct / (jnp.sqrt(second / correct) + adam_eps)
                way = way + weight_decay * old
                directions[n][at] = way
                block = block + jnp.where((row == 0) & (lane == which), total_of(old), 0.0)
                block = block + jnp.where((row == 1) & (lane == which), total_of(way), 0.0)
            sums[...] = block


def update_call(mesh, finals, square, olds, firsts, seconds):
    place = Place(mesh, olds[1].shape[0])
    shapes = [jax.ShapeDtypeStruct(old.shape, f32) for old in olds]
    vmem = pl.BlockSpec(memory_space=pltpu.VMEM)
    results = pl.pallas_call(
        functools.partial(update_kernel, place),
        out_shape=shapes * 4 + [jax.ShapeDtypeStruct((8, 128), f32)],
        in_specs=[vmem] * 13,
        out_specs=[vmem] * 13,
        compiler_params=pltpu.CompilerParams(vmem_limit_bytes=32 * 2**20),
    )(*finals, square, *olds, *firsts, *seconds)
    return results[:3], results[3:6], results[6:9], results[9:12], results[12]


def step_kernel(total, *refs):
    olds, directions, news, lows = refs[:3], refs[3:6], refs[6:9], refs[9:12]
    norms = jnp.sqrt(total[0:2])
    for n, core, lead, columns, which in pieces_of([ref.shape for ref in olds]):
        at = lead + (slice(None), columns)
        trust = norms[0:1, which : which + 1] / norms[1:2, which : which + 1]
        new = olds[n][at] - step_rate * trust * directions[n][at]
        news[n][at] = new
        lows[n][at] = new.astype(bf16)


def step_call(total, olds, directions):
    vmem = pl.BlockSpec(memory_space=pltpu.VMEM)
    results = pl.pallas_call(
        step_kernel,
        out_shape=[jax.ShapeDtypeStruct(old.shape, f32) for old in olds]
        + [jax.ShapeDtypeStruct(old.shape, bf16) for old in olds],
        in_specs=[vmem] * 7,
        out_specs=[vmem] * 6,
        compiler_params=pltpu.CompilerParams(vmem_limit_bytes=32 * 2**20),
    )(total, *olds, *directions)
    return results[:3], results[3:]


def adam_direction(first_old, second_old, clipped):
    first_new = decay_rate * first_old + (1.0 - decay_rate) * clipped
    second_new = decay_rate * second_old + (1.0 - decay_rate) * clipped * clipped
    correct = 1.0 - decay_rate**STEP
    direction = first_new / correct / (jnp.sqrt(second_new / correct) + adam_eps)
    return (first_new, second_new, direction)


def body(
    mesh,
    tokens,
    positions,
    counts,
    cotangent,
    attn_weights,
    ffn_in,
    ffn_out,
    vectors,
    attn_first,
    ffn_in_first,
    ffn_out_first,
    vector_first,
    attn_second,
    ffn_in_second,
    ffn_out_second,
    vector_second,
):
    results = forward_call(mesh, tokens, positions, attn_weights, ffn_in, ffn_out, vectors)
    rows = ffn_in.shape[0]
    output, grad_tokens, *final, vec_total, square_sum = backward_call(
        mesh, results, positions, counts, cotangent, rows
    )
    olds = (attn_weights, ffn_in, ffn_out)
    clipped, new_firsts, new_seconds, directions, sums = update_call(
        mesh,
        final,
        square_sum,
        olds,
        (attn_first, ffn_in_first, ffn_out_first),
        (attn_second, ffn_in_second, ffn_out_second),
    )
    total = total_call(mesh, rows, sums)
    news, lows = step_call(total, olds, directions)
    lamb_norms = jnp.sqrt(total[:2, :6])
    trust_ratio = lamb_norms[0] / lamb_norms[1]
    grad_norm = jnp.sqrt(square_sum[0, 0])
    owner = lax.axis_index("seq") * lax.axis_size("dp") + lax.axis_index("dp")
    vec_count = vectors.shape[0]
    vec_share = lax.dynamic_slice_in_dim(vec_total.reshape(-1), owner * vec_count, vec_count, 0)
    vec_share = vec_share * (1.0 / jnp.maximum(grad_norm, 1.0))
    vec_moved = adam_direction(vector_first, vector_second, vec_share)
    new_vectors = vectors - step_rate * vec_moved[2]
    return (
        output.astype(f32),
        grad_tokens.astype(f32),
        *clipped,
        vec_share,
        *new_firsts,
        vec_moved[0],
        *new_seconds,
        vec_moved[1],
        *news,
        new_vectors,
        *lows,
        lamb_norms,
        trust_ratio,
        grad_norm,
    )


def solution(mesh):
    return jax.shard_map(
        functools.partial(body, mesh),
        mesh=mesh,
        in_specs=(
            P("dp", "seq", None),
            P("dp", None),
            P("dp"),
            P("dp", None, None),
            P(None, ("seq", "dp"), None),
            P(("seq", "dp"), None),
            P(("seq", "dp"), None),
            P(("seq", "dp")),
            P(None, ("seq", "dp"), None),
            P(("seq", "dp"), None),
            P(("seq", "dp"), None),
            P(("seq", "dp")),
            P(None, ("seq", "dp"), None),
            P(("seq", "dp"), None),
            P(("seq", "dp"), None),
            P(("seq", "dp")),
        ),
        out_specs=(
            P("dp", "seq", None),
            P("dp", "seq", None),
            P(None, ("seq", "dp"), None),
            P(("seq", "dp"), None),
            P(("seq", "dp"), None),
            P(("seq", "dp")),
            P(None, ("seq", "dp"), None),
            P(("seq", "dp"), None),
            P(("seq", "dp"), None),
            P(("seq", "dp")),
            P(None, ("seq", "dp"), None),
            P(("seq", "dp"), None),
            P(("seq", "dp"), None),
            P(("seq", "dp")),
            P(None, ("seq", "dp"), None),
            P(("seq", "dp"), None),
            P(("seq", "dp"), None),
            P(("seq", "dp")),
            P(None, ("seq", "dp"), None),
            P(("seq", "dp"), None),
            P(("seq", "dp"), None),
            P(),
            P(),
            P(),
        ),
        check_vma=False,
    )
```

```python
import functools
import jax
import jax.numpy as jnp
from jax import lax
from jax.sharding import PartitionSpec as P
from jax.experimental import pallas as pl
from jax.experimental.pallas import tpu as pltpu

H = 12
HD = 64
STEP = 5

decay_rate = 0.5
step_rate = 0.3
weight_decay = 0.01
adam_eps = 1e-06
norm_eps = 1e-12
f32 = jnp.float32
bf16 = jnp.bfloat16
MESH = pl.DeviceIdType.MESH


class Place:
    def __init__(self, mesh, shard_rows):
        self.seq = mesh.shape["seq"]
        self.dp = mesh.shape["dp"]
        self.merge = 2
        while (self.merge * shard_rows) % 16:
            self.merge *= 2
        self.seq_bits = self.seq.bit_length() - 1
        self.far_bits = (self.dp // self.merge).bit_length() - 1
        self.bits = self.seq_bits + self.far_bits
        self.groups = self.seq * self.dp // self.merge
        self.devices = self.seq * self.dp
        self.levels = self.devices.bit_length() - 1

    def here(self):
        self.s = lax.axis_index("seq")
        self.d = lax.axis_index("dp")
        self.member = lax.rem(self.d, self.merge)
        self.core = lax.rem(self.d, 2)
        self.weight = []
        self.bit = []
        for dim in range(self.bits):
            if dim < self.seq_bits:
                w = 1 << (self.seq_bits - 1 - dim)
                self.bit.append(lax.rem(self.s // w, 2))
            else:
                w = self.merge << (self.bits - 1 - dim)
                self.bit.append(lax.rem(self.d // w, 2))
            self.weight.append(w)

    def across(self, dim):
        flip = self.weight[dim] * (1 - 2 * self.bit[dim])
        if dim < self.seq_bits:
            return (self.s + flip, self.d)
        return (self.s, self.d + flip)

    def other_core(self):
        return (self.s, self.d + 1 - 2 * self.core)

    def mates(self):
        base = self.d - self.member
        return [
            (self.s, base + lax.rem(self.member + k, self.merge)) for k in range(1, self.merge)
        ]

    def row_mates(self):
        return [(lax.rem(self.s + k, self.seq), self.d) for k in range(1, self.seq)]

    def greet(self):
        barrier = pltpu.get_barrier_semaphore()
        everyone = self.mates() + self.row_mates()
        everyone += [self.across(dim) for dim in range(self.seq_bits, self.bits)]
        for device in everyone:
            pl.semaphore_signal(barrier, inc=1, device_id=device, device_id_type=MESH)
        pl.semaphore_wait(barrier, len(everyone))

    def greet_all(self):
        barrier = pltpu.get_barrier_semaphore()
        everyone = self.row_mates()
        everyone += [(self.s, lax.rem(self.d + k, self.dp)) for k in range(1, self.dp)]
        for device in everyone:
            pl.semaphore_signal(barrier, inc=1, device_id=device, device_id_type=MESH)
        pl.semaphore_wait(barrier, len(everyone))

    def partner(self, level):
        inside = self.levels - self.bits
        if level >= inside:
            return self.across(level - inside)
        w = 1 << level
        return (self.s, self.d + w * (1 - 2 * lax.rem(self.d // w, 2)))

    def box(self, free):
        return tuple(slice(None) if dim in free else self.bit[dim] for dim in range(self.bits))


def erf(x):
    x = jnp.clip(x, -3.832506856900711, 3.832506856900711)
    x2 = x * x
    top = jnp.float32(0.00022905065861350646)
    for c in (
        0.0034082910107109506,
        0.050955695062380861,
        0.18520832239976145,
        1.128379143519084,
    ):
        top = top * x2 + jnp.float32(c)
    low = jnp.float32(-1.1791602954361697e-7)
    for c in (
        0.000023547966471313185,
        0.0010179625278914885,
        0.014070470171167667,
        0.11098505178285362,
        0.49746925110067538,
        1.0,
    ):
        low = low * x2 + jnp.float32(c)
    return x * top / low


def dot(a, b):
    return jnp.dot(a, b, preferred_element_type=f32)


def dot_t(a, b):
    return lax.dot_general(a, b, (((1,), (1,)), ((), ())), preferred_element_type=f32)


def t_dot(a, b):
    return lax.dot_general(a, b, (((0,), (0,)), ((), ())), preferred_element_type=f32)


def normalize(x):
    center = x - jnp.mean(x, -1, keepdims=True)
    inverse = lax.rsqrt(jnp.mean(center * center, -1, keepdims=True) + norm_eps)
    return center * inverse, inverse


FIRST = 3
LAG = 2
DURING = 5


class Flows:
    def __init__(self, place, chunks, send, recv):
        self.place = place
        self.chunks = chunks
        self.send = send
        self.recv = recv
        self.stages = place.bits

    def number(self, chunk, part, stage):
        return (chunk * 3 + part) * (self.stages + 1) + stage


class Gather(Flows):
    def copy(self, chunk, part, stage):
        place = self.place
        buf, rows, columns, order = self.chunks[chunk].part(part, place)
        n = self.number(chunk, part, stage)
        box = place.box(order[:stage]) + (rows, columns)
        return pltpu.make_async_remote_copy(
            src_ref=buf.at[box],
            dst_ref=buf.at[box],
            send_sem=self.send.at[n],
            recv_sem=self.recv.at[n],
            device_id=place.across(order[stage]),
            device_id_type=MESH,
        )

    def hand(self, chunk):
        place = self.place
        buf, rows, columns = self.chunks[chunk].half(place)
        n = self.number(chunk, 0, self.stages)
        box = tuple(slice(None) for _ in range(place.bits)) + (rows, columns)
        return pltpu.make_async_remote_copy(
            src_ref=buf.at[box],
            dst_ref=buf.at[box],
            send_sem=self.send.at[n],
            recv_sem=self.recv.at[n],
            device_id=place.other_core(),
            device_id_type=MESH,
        )

    def start(self, chunk):
        return max(0, chunk - FIRST)

    def lag(self, chunk):
        return 1 if chunk < 3 else LAG

    def step(self, t):
        for chunk in range(len(self.chunks)):
            stage, late = divmod(t - self.start(chunk), self.lag(chunk))
            if late or stage < 0:
                continue
            if stage <= self.stages:
                for part in range(3):
                    if stage > 0:
                        self.copy(chunk, part, stage - 1).wait_recv()
                    if stage < self.stages:
                        self.copy(chunk, part, stage).start()
                if stage == self.stages:
                    self.hand(chunk).start()
            if stage == self.stages + 1:
                self.hand(chunk).wait_recv()

    def last_step(self, chunk):
        return self.start(chunk) + self.lag(chunk) * (self.stages + 1)

    def pump(self, t):
        while self.now <= t:
            self.step(self.now)
            self.now += 1

    now = 0

    def finish(self):
        for chunk in range(len(self.chunks)):
            for part in range(3):
                for stage in range(self.stages):
                    self.copy(chunk, part, stage).wait_send()
            self.hand(chunk).wait_send()


class Chunk:
    def __init__(self, buf, first, width, orders, cuts=None):
        self.buf, self.first, self.width, self.orders, self.cuts = buf, first, width, orders, cuts

    def half(self, place):
        half = self.width // 2
        start = pl.multiple_of(self.first + place.core * half, 128)
        return self.buf, slice(None), pl.ds(start, half)

    def part(self, part, place):
        half = self.width // 2
        if self.cuts is None:
            third = half // 3
            start = pl.multiple_of(self.first + place.core * half + part * third, 128)
            return self.buf, slice(None), pl.ds(start, third), self.orders[part]
        start = pl.multiple_of(self.first + place.core * half, 128)
        rows = pl.ds(self.cuts[part], self.cuts[part + 1] - self.cuts[part])
        return self.buf, rows, pl.ds(start, half), self.orders[part]


def weight_chunks(place, attn, first_ffn, second_ffn, reverse):
    seq = list(range(place.seq_bits))
    far = list(range(place.seq_bits, place.bits))[::-1]
    left = far + seq[::-1]
    right = far + seq
    chunks = []

    def orders(index):
        a, b = (seq, seq[::-1]) if index % 2 else (seq[::-1], seq)
        if not reverse:
            third = far + a
        elif index % 4 < 2:
            third = a + far
        else:
            third = a[:1] + far + a[1:]
        out = [left, right, third]
        return [order[::-1] for order in out] if reverse else out

    width = attn.shape[-1]
    for m in range(4):
        chunks.append(Chunk(attn.at[m], 0, width, orders(m)))
    for j in range(first_ffn.shape[-1] // width):
        chunks.append(Chunk(first_ffn, j * width, width, orders(j)))
    rows = second_ffn.shape[-2]
    third = rows // 3 // 16 * 16
    for j in range(3):
        chunks.append(
            Chunk(second_ffn, j * width // 3, width // 3, orders(j), (0, third, 2 * third, rows))
        )
    return chunks


def forward_kernel(
    place,
    vec_rows,
    vec_count,
    tokens_ref,
    places_ref,
    attn_ref,
    in_ref,
    out_ref,
    vec_ref,
    attn_hbm,
    in_hbm,
    out_hbm,
    vec_hbm,
    high_hbm,
    query_hbm,
    key_hbm,
    value_hbm,
    output_hbm,
    slot_low_hbm,
    slot_hbm,
    slot_active_hbm,
    slot_slope_hbm,
    attn_buf,
    in_buf,
    out_buf,
    vec_buf,
    vec_acc,
    vec,
    attn_in,
    in_in,
    out_in,
    joined,
    send_high,
    send_rest,
    high,
    rest,
    query,
    key,
    value,
    norm,
    active,
    slot_low,
    slot,
    slot_active,
    slot_slope,
    flow_send,
    flow_recv,
    mate_send,
    mate_recv,
    local_sem,
    token_send,
    token_recv,
    vec_send,
    vec_recv,
    save_sem,
):
    place.here()
    place.greet()
    merge, seq = place.merge, place.seq
    width = tokens_ref.shape[-1]
    block = tokens_ref.shape[1]
    own = tokens_ref.shape[0] // seq
    length = block * seq
    rows = own * length
    slots = places_ref.shape[1]
    mine = place.box(())

    sources = (attn_ref, in_ref, out_ref)
    stages = (attn_in, in_in, out_in)
    mate_copies = []
    for index in range(3):
        for k, device in enumerate(place.mates()):
            n = index * (merge - 1) + k
            copy = pltpu.make_async_remote_copy(
                src_ref=sources[index],
                dst_ref=stages[index].at[place.member],
                send_sem=mate_send.at[n],
                recv_sem=mate_recv.at[n],
                device_id=device,
                device_id_type=MESH,
            )
            copy.start()
            mate_copies.append(copy)
    local = []
    for index in range(3):
        copy = pltpu.make_async_copy(
            sources[index], stages[index].at[place.member], local_sem.at[index]
        )
        copy.start()
        local.append(copy)
    vec_mates = []
    vec_buf.at[mine][place.member] = vec_ref[...]
    for k, device in enumerate(place.mates()):
        copy = pltpu.make_async_remote_copy(
            src_ref=vec_ref,
            dst_ref=vec_buf.at[mine].at[place.member],
            send_sem=vec_send.at[k],
            recv_sem=vec_recv.at[k],
            device_id=device,
            device_id_type=MESH,
        )
        copy.start()
        vec_mates.append(copy)

    def split(i, _):
        x = tokens_ref[i]
        top = x.astype(bf16)
        send_high[i] = top
        send_rest[i] = (x - top.astype(f32)).astype(bf16)
        return 0

    lax.fori_loop(0, own * seq, split, 0)
    token_copies = []
    my_columns = pl.ds(pl.multiple_of(place.s * block, block), block)
    for half, (source, target) in enumerate(((send_high, high), (send_rest, rest))):
        for k, device in enumerate(place.row_mates()):
            n = half * (seq - 1) + k
            token_copies.append(
                pltpu.make_async_remote_copy(
                    src_ref=source.at[pl.ds(device[0] * own, own)],
                    dst_ref=target.at[:, my_columns],
                    send_sem=token_send.at[n],
                    recv_sem=token_recv.at[n],
                    device_id=device,
                    device_id_type=MESH,
                )
            )
        target.at[:, my_columns][...] = source[pl.ds(place.s * own, own)]
    for copy in token_copies[: seq - 1]:
        copy.start()

    flows = Gather(place, weight_chunks(place, attn_buf, in_buf, out_buf, False), flow_send, flow_recv)

    def join(chunks, part):
        count = part.shape[1]
        for i in range(merge):
            joined[i * count : (i + 1) * count, : part.shape[-1]] = part[i]
        for chunk in chunks:
            buf, _, columns = chunk.half(place)
            buf.at[mine + (slice(None), columns)][...] = joined[: merge * count, columns].astype(bf16)

    for k in range(3):
        local[k].wait()
        for copy in mate_copies[k * (merge - 1) : (k + 1) * (merge - 1)]:
            copy.wait_recv()
        if k == 0:
            for m in range(4):
                join(flows.chunks[m : m + 1], attn_in.at[:, m])
        elif k == 1:
            join(flows.chunks[4:-3], in_in)
        else:
            join(flows.chunks[-3:], out_in)

    def vec_copy(stage):
        order = list(range(place.bits))
        box = place.box(order[:stage])
        return pltpu.make_async_remote_copy(
            src_ref=vec_buf.at[box],
            dst_ref=vec_buf.at[box],
            send_sem=vec_send.at[merge - 1 + stage],
            recv_sem=vec_recv.at[merge - 1 + stage],
            device_id=place.across(order[stage]),
            device_id_type=MESH,
        )

    for copy in vec_mates:
        copy.wait_recv()
    vec_copy(0).start()
    flows.pump(0)
    for t in range(1, flows.stages + 1):
        flows.pump(t)
        vec_copy(t - 1).wait_recv()
        if t < flows.stages:
            vec_copy(t).start()
    for copy in token_copies[seq - 1 :]:
        copy.start()

    vec_acc[...] = jnp.zeros_like(vec_acc)
    for owner in range(place.devices):
        group, member = divmod(owner, merge)
        bits = tuple((group >> (place.bits - 1 - dim)) & 1 for dim in range(place.bits))
        first, shift = divmod(vec_count * owner, 128)
        count = (shift + vec_count + 127) // 128
        vec_acc[first : first + count] += vec_buf.at[bits][member, :count]
    per = width // 128
    vec_acc[...] = vec_acc[...].astype(bf16).astype(f32)
    for row in range(vec_rows):
        vec[row : row + 1] = jnp.concatenate(
            [vec_acc[row * per + k : row * per + k + 1] for k in range(per)], axis=1
        )
    saves = []

    def save(source, target):
        copy = pltpu.make_async_copy(source, target, save_sem.at[len(saves)])
        copy.start()
        saves.append(copy)

    save(vec, vec_hbm)

    for copy in token_copies[: seq - 1]:
        copy.wait_recv()
    tile = min(256, length)
    per_seq = length // tile
    save(high, high_hbm)
    scale = HD**-0.5

    for m, target in enumerate((query, key, value)):
        flows.pump(flows.last_step(m))
        matrix = attn_buf.at[m].reshape(width, width)

        def project(i, _):
            sequence, at = i // per_seq, pl.ds(pl.multiple_of(lax.rem(i, per_seq) * tile, tile), tile)
            result = dot(high[sequence, at], matrix[...])
            if m == 0:
                result = (result + vec[0:1]).astype(bf16) * scale
            elif m == 2:
                result = result + vec[1:2]
            target[sequence, at] = result.astype(bf16)
            return 0

        lax.fori_loop(0, own * per_seq, project, 0)
        save(target, (query_hbm, key_hbm, value_hbm)[m])

    context = send_high.reshape(own, length, width)
    for copy in token_copies[: seq - 1]:
        copy.wait_send()
    pairs = width // 128
    turns = own * pairs
    lane = lax.broadcasted_iota(jnp.int32, (1, 128), 1)

    def attend(i, _):
        for k in range(during):
            @pl.when(i == (k + 1) * turns // (during + 1))
            def _():
                flows.step(flows.now + k)

        sequence, pair = i // pairs, lax.rem(i, pairs)
        at = pl.ds(pl.multiple_of(pair * 128, 128), 128)
        keys, values = key[sequence, :, at], value[sequence, :, at]
        for q in range(per_seq):
            places = slice(q * tile, (q + 1) * tile)
            queries = query[sequence, places, at]
            heads = []
            for head in range(2):
                picked = jnp.where(lane // HD == head, queries, jnp.zeros_like(queries))
                scores = dot_t(picked, keys)
                exponent = jnp.exp(scores - jnp.max(scores, -1, keepdims=True))
                total = jnp.sum(exponent, -1, keepdims=True)
                heads.append(dot(exponent.astype(bf16), values) / total)
            context[sequence, places, at] = jnp.where(lane < HD, heads[0], heads[1]).astype(bf16)
        return 0

    during = DURING
    lax.fori_loop(0, turns, attend, 0)
    flows.now += during
    flows.pump(flows.last_step(4))

    for copy in token_copies[seq - 1 :]:
        copy.wait_recv()
    out_matrix = attn_buf.at[3].reshape(width, width)

    def front(i, _):
        sequence, at = i // per_seq, pl.ds(pl.multiple_of(lax.rem(i, per_seq) * tile, tile), tile)
        x = high[sequence, at].astype(f32) + rest[sequence, at].astype(f32)
        x = x + (dot(context[sequence, at], out_matrix[...]) + vec[2:3])
        x, _ = normalize(x)
        norm[sequence, at] = x * vec[4:5] + vec[5:6]
        return 0

    lax.fori_loop(0, own * per_seq, front, 0)

    place_ids = lax.broadcasted_iota(jnp.int32, (length, slots), 0)
    for sequence in range(own):
        at = pl.ds(sequence * slots, slots)
        hits = places_ref[pl.ds(place.s * own + sequence, 1)] == place_ids
        hits = jnp.where(hits, 1.0, 0.0).astype(bf16)
        slot_high = t_dot(hits, high[sequence])
        slot_low[0, at] = slot_high.astype(bf16)
        slot_context = t_dot(hits, context[sequence]).astype(bf16)
        slot_low[1, at] = slot_context
        slot_low[2, at] = t_dot(hits, query[sequence]).astype(bf16)
        slot[0, at] = slot_high
        slot[1, at] = t_dot(hits, rest[sequence])
        x = slot[0, at] + slot[1, at]
        x = x + (dot(slot_context, out_matrix[...]) + vec[2:3])
        x, inverse = normalize(x)
        slot[0, at] = x
        slot[2, at] = jnp.broadcast_to(inverse, x.shape)
        x = x * vec[4:5] + vec[5:6]
        slot[1, at] = x
        slot_low[3, at] = x.astype(bf16)
    save(slot_low, slot_low_hbm)
    save(attn_buf, attn_hbm)

    in_matrix = in_buf.reshape(width, in_buf.shape[-1])
    for j in range(in_buf.shape[-1] // width):
        flows.pump(flows.last_step(4 + j))
        at = pl.ds(j * width, width)
        bias = vec[8 + j : 9 + j]

        def hidden(i, _):
            sequence, here = i // per_seq, pl.ds(pl.multiple_of(lax.rem(i, per_seq) * tile, tile), tile)
            x = dot(norm[sequence, here].astype(bf16), in_matrix[:, at]) + bias
            active[sequence, here, at] = (0.5 * x * (1.0 + erf(x * 0.5**0.5))).astype(bf16)
            return 0

        lax.fori_loop(0, own * per_seq, hidden, 0)
        x = dot(slot_low[3], in_matrix[:, at]) + bias
        half = 0.5 * (1.0 + erf(x * 0.5**0.5))
        slot_active[:, at] = (x * half).astype(bf16)
        slot_slope[:, at] = half + x * jnp.exp(-0.5 * x * x) * 0.3989422804014327
    save(slot_active, slot_active_hbm)
    save(slot_slope, slot_slope_hbm)
    save(in_buf, in_hbm)

    out_matrix = out_buf.reshape(out_buf.shape[-2] * place.groups, width)
    wide = width // 3
    for j in range(3):
        flows.pump(flows.last_step(len(flows.chunks) - 3 + j))
        at = slice(j * wide, (j + 1) * wide)
        save(out_buf.at[tuple(slice(None) for _ in range(place.bits + 1)) + (at,)],
             out_hbm.at[tuple(slice(None) for _ in range(place.bits + 1)) + (at,)])
        bias = vec[3:4, at]
        slot[1, :, at] = slot[1, :, at] + (dot(slot_active[...], out_matrix[:, at]) + bias)
        if j == 2:
            save(slot, slot_hbm)

        def feed(i, _):
            sequence, here = i // per_seq, pl.ds(pl.multiple_of(lax.rem(i, per_seq) * tile, tile), tile)
            x = dot(active[sequence, here], out_matrix[:, at]) + bias
            norm[sequence, here, at] = norm[sequence, here, at] + x
            return 0

        lax.fori_loop(0, own * per_seq, feed, 0)
    for copy in token_copies[seq - 1 :]:
        copy.wait_send()
    output = send_rest.reshape(own, length, width)

    def back(i, _):
        sequence, here = i // per_seq, pl.ds(pl.multiple_of(lax.rem(i, per_seq) * tile, tile), tile)
        x, _ = normalize(norm[sequence, here])
        output[sequence, here] = (x * vec[6:7] + vec[7:8]).astype(bf16)
        return 0

    lax.fori_loop(0, own * per_seq, back, 0)
    save(output, output_hbm)
    flows.finish()
    for copy in mate_copies + vec_mates:
        copy.wait_send()
    for stage in range(flows.stages):
        vec_copy(stage).wait_send()
    for copy in saves:
        copy.wait()


def forward_call(mesh, tokens, positions, attn_weights, ffn_in, ffn_out, vectors):
    place = Place(mesh, ffn_in.shape[0])
    sequences, block, width = tokens.shape
    inner = ffn_in.shape[1]
    slots = positions.shape[1]
    own = sequences // place.seq
    length = block * place.seq
    vec_count = vectors.shape[0]
    vec_rows = vec_count * place.devices // width
    owner = lax.axis_index("seq") * place.dp + lax.axis_index("dp")
    padded = lax.dynamic_update_slice_in_dim(
        jnp.zeros((1024,), f32), vectors.astype(bf16).astype(f32), lax.rem(vec_count * owner, 128), 0
    ).reshape(8, 128)
    bits = (2,) * place.bits
    r = ffn_in.shape[0]
    joint = r * place.merge
    joint_out = ffn_out.shape[0] * place.merge
    flow_count = (4 + inner // width + 3) * 3 * (place.bits + 1)
    attn_shape = (4,) + bits + (joint, width)
    in_shape = bits + (joint, inner)
    out_shape = bits + (joint_out, width)
    seq_shape = (own, length, width)
    rows = own * slots
    results = [
        (attn_shape, bf16),
        (in_shape, bf16),
        (out_shape, bf16),
        ((16, width), f32),
        (seq_shape, bf16),
        (seq_shape, bf16),
        (seq_shape, bf16),
        (seq_shape, bf16),
        (seq_shape, bf16),
        ((4, rows, width), bf16),
        ((3, rows, width), f32),
        ((rows, inner), bf16),
        ((rows, inner), f32),
    ]
    vmem = pl.BlockSpec(memory_space=pltpu.VMEM)
    hbm = pl.BlockSpec(memory_space=pl.ANY)
    dma = pltpu.SemaphoreType.DMA
    mates = place.merge - 1
    return pl.pallas_call(
        functools.partial(forward_kernel, place, vec_rows, vec_count),
        out_shape=[jax.ShapeDtypeStruct(*one) for one in results],
        in_specs=[vmem, vmem, hbm, hbm, hbm, vmem],
        out_specs=[hbm] * len(results),
        scratch_shapes=[
            pltpu.VMEM(attn_shape, bf16),
            pltpu.VMEM(in_shape, bf16),
            pltpu.VMEM(out_shape, bf16),
            pltpu.VMEM(bits + (place.merge, 8, 128), f32),
            pltpu.VMEM((vec_rows * width // 128 + 8, 128), f32),
            pltpu.VMEM((16, width), f32),
            pltpu.VMEM((place.merge,) + attn_weights.shape, f32),
            pltpu.VMEM((place.merge,) + ffn_in.shape, f32),
            pltpu.VMEM((place.merge,) + ffn_out.shape, f32),
            pltpu.VMEM((joint_out, inner), f32),
            pltpu.VMEM((sequences, block, width), bf16),
            pltpu.VMEM((sequences, block, width), bf16),
            pltpu.VMEM(seq_shape, bf16),
            pltpu.VMEM(seq_shape, bf16),
            pltpu.VMEM(seq_shape, bf16),
            pltpu.VMEM(seq_shape, bf16),
            pltpu.VMEM(seq_shape, bf16),
            pltpu.VMEM(seq_shape, f32),
            pltpu.VMEM((own, length, inner), bf16),
            pltpu.VMEM((4, rows, width), bf16),
            pltpu.VMEM((3, rows, width), f32),
            pltpu.VMEM((rows, inner), bf16),
            pltpu.VMEM((rows, inner), f32),
            dma((flow_count,)),
            dma((flow_count,)),
            dma((3 * mates,)),
            dma((3 * mates,)),
            dma((3,)),
            dma((2 * (place.seq - 1),)),
            dma((2 * (place.seq - 1),)),
            dma((mates + place.bits,)),
            dma((mates + place.bits,)),
            dma((len(results) + 2,)),
        ],
        compiler_params=pltpu.CompilerParams(
            collective_id=0, has_side_effects=True, vmem_limit_bytes=64 * 2**20 - 2**18
        ),
    )(tokens, positions, attn_weights, ffn_in, ffn_out, padded)


SPACING = 4
INSIDE = 8


class Scatter(Flows):
    def __init__(self, place, chunks, send, recv, landings, finals):
        super().__init__(place, chunks, send, recv)
        self.landings = landings
        self.finals = finals

    def boxes(self, order, stage):
        place = self.place
        done = order[:stage]
        dim = order[stage]
        out, mine, came = [], [], []
        for d in range(place.bits):
            if d in done:
                picks = (place.bit[d],) * 3
            elif d == dim:
                picks = (1 - place.bit[d], place.bit[d], 1 - place.bit[d])
            else:
                picks = (slice(None),) * 3
            out.append(picks[0])
            mine.append(picks[1])
            came.append(picks[2])
        return tuple(out), tuple(mine), tuple(came)

    def copy(self, chunk, part, stage):
        buf, rows, columns, order = self.chunks[chunk].part(part, self.place)
        n = self.number(chunk, part, stage)
        out, mine, _ = self.boxes(order, stage)
        return pltpu.make_async_remote_copy(
            src_ref=buf.at[out + (rows, columns)],
            dst_ref=self.landings[chunk].at[mine + (rows, columns)],
            send_sem=self.send.at[n],
            recv_sem=self.recv.at[n],
            device_id=self.place.across(order[stage]),
            device_id_type=MESH,
        )

    def begin(self, *chunks):
        for chunk in chunks:
            for part in range(3):
                self.copy(chunk, part, 0).start()

    def advance(self, chunk, stage):
        for part in range(3):
            self.sum_up(chunk, part, stage)

    def sum_up(self, chunk, part, stage):
        self.copy(chunk, part, stage).wait_recv()
        buf, rows, columns, order = self.chunks[chunk].part(part, self.place)
        _, mine, came = self.boxes(order, stage)
        tail = (rows, columns)
        total = buf.at[mine + tail][...].astype(f32)
        total = total + self.landings[chunk].at[came + tail][...].astype(f32)
        if stage + 1 < self.stages:
            buf.at[mine + tail][...] = total.astype(bf16)
            self.copy(chunk, part, stage + 1).start()
        else:
            self.finals[chunk].at[tail][...] = total

    def finish(self):
        for chunk in range(len(self.chunks)):
            for part in range(3):
                for stage in range(self.stages):
                    self.copy(chunk, part, stage).wait_send()


class Part:
    def __init__(self, buf, first, width, orders, cuts=None):
        self.buf, self.first, self.width, self.orders, self.cuts = buf, first, width, orders, cuts

    def size(self, part):
        rows = self.buf.shape[-2]
        if self.cuts is None:
            return rows * (self.width // 3)
        return (self.cuts[part + 1] - self.cuts[part]) * self.width

    def part(self, part, place):
        if self.cuts is None:
            third = self.width // 3
            columns = pl.ds(self.first + part * third, third)
            return self.buf, slice(None), columns, self.orders[part]
        rows = pl.ds(self.cuts[part], self.cuts[part + 1] - self.cuts[part])
        return self.buf, rows, pl.ds(self.first, self.width), self.orders[part]


def gradient_chunks(place, attn, first_ffn, second_ffn):
    forward = weight_chunks(place, attn, first_ffn, second_ffn, True)
    half = attn.shape[-1]
    chunks = []
    for j in range(3):
        chunks.append(
            Part(second_ffn, j * half // 3, half // 3, forward[-3 + j].orders, forward[-3 + j].cuts)
        )
    for j in range(first_ffn.shape[-1] // half):
        chunks.append(Part(first_ffn, j * half, half, forward[4 + j].orders))
    for m in (3, 0, 1, 2):
        chunks.append(Part(attn.at[m], 0, half, forward[m].orders))
    return chunks


def column_total(x):
    return jnp.sum(x, axis=0, keepdims=True)


def backward_kernel(
    place,
    attn_hbm,
    in_hbm,
    out_hbm,
    vec,
    high_hbm,
    key_hbm,
    value_hbm,
    output_hbm,
    slot_low_hbm,
    slot_hbm,
    slot_active_hbm,
    slot_slope_hbm,
    places_ref,
    counts_ref,
    cotangent_hbm,
    output_ref,
    grad_tokens_ref,
    final_attn_hbm,
    final_in_hbm,
    final_out_hbm,
    vec_grad_ref,
    square_ref,
    mats,
    last,
    out_buf,
    grad_attn,
    grad_in,
    grad_out,
    land_attn,
    land_in,
    land_out,
    final_attn,
    final_in,
    final_out,
    tokens_both,
    key,
    value,
    active_both,
    inner_both,
    slope,
    low_both,
    slot,
    feed_both,
    attended_both,
    query_both,
    context_back,
    sum_two,
    key_back,
    value_back,
    key_both,
    value_both,
    stage_tokens,
    vec_sum,
    vec_land,
    square,
    square_land,
    flow_send,
    flow_recv,
    load_sem,
    pair_send,
    pair_recv,
    row_send,
    row_recv,
    own_sem,
    vec_send,
    vec_recv,
    final_send,
    final_recv,
    square_send,
    square_recv,
    extra_land=None,
    extra_send=None,
    extra_recv=None,
):
    place.here()
    place.greet_all()
    merge, seq = place.merge, place.seq
    width = out_buf.shape[-1]
    inner = active_both.shape[-1]
    half = width // 2
    own, length = key.shape[:2]
    block = length // seq
    slots = sum_two.shape[1]
    rows = own * slots
    tile = min(256, length)
    per_seq = length // tile
    scale = HD**-0.5
    my_half = pl.ds(pl.multiple_of(place.core * half, 128), half)
    other_half = pl.ds(pl.multiple_of((1 - place.core) * half, 128), half)
    loads = []
    pairs = []
    sum_one = slope.at[:rows, :width]

    def load(source, target):
        copy = pltpu.make_async_copy(source, target, load_sem.at[len(loads)])
        copy.start()
        loads.append(copy)
        return copy

    def share(source, target):
        n = len(pairs)
        copy = pltpu.make_async_remote_copy(
            src_ref=source,
            dst_ref=target,
            send_sem=pair_send.at[n],
            recv_sem=pair_recv.at[n],
            device_id=place.other_core(),
            device_id_type=MESH,
        )
        copy.start()
        pairs.append(copy)
        return copy

    got_slot = load(slot_hbm, slot)
    got_cotangent = load(cotangent_hbm.at[pl.ds(place.s * own, own)], sum_two)
    got_out = load(out_hbm, out_buf)
    got_slope = load(slot_slope_hbm, slope.at[:rows])
    got_active = load(slot_active_hbm, active_both.at[0])
    came_active = share(slot_active_hbm, active_both.at[1])
    got_low = load(slot_low_hbm, low_both.at[0])
    came_low = share(slot_low_hbm, low_both.at[1])
    inner_parts = inner // width
    free = (slice(None),) * (place.bits + 1)
    got_in = [
        load(in_hbm.at[free + (pl.ds(j * width, width),)], mats.at[j]) for j in range(inner_parts)
    ]
    got_last = load(attn_hbm.at[3], last)
    got_key = load(key_hbm, key)
    got_value = load(value_hbm, value)
    got_tokens = load(high_hbm, tokens_both.at[0])

    sends = []
    owns = []

    def send_rows(stage, target, sequence):
        for k, device in enumerate(place.row_mates()):
            n = len(sends)
            copy = pltpu.make_async_remote_copy(
                src_ref=stage.at[sequence, pl.ds(pl.multiple_of(device[0] * block, block), block)],
                dst_ref=target.at[place.s * own + sequence],
                send_sem=row_send.at[n],
                recv_sem=row_recv.at[n],
                device_id=device,
                device_id_type=MESH,
            )
            copy.start()
            sends.append(copy)
        copy = pltpu.make_async_copy(
            stage.at[sequence, pl.ds(pl.multiple_of(place.s * block, block), block)],
            target.at[place.s * own + sequence],
            own_sem.at[len(owns)],
        )
        copy.start()
        owns.append(copy)

    for sequence in range(own):
        send_rows(output_hbm, output_ref, sequence)

    chunks = gradient_chunks(place, grad_attn, grad_in, grad_out)
    finals = [final_out] * 3 + [final_in] * inner_parts * 2 + [final_attn.at[m] for m in (3, 0, 1, 2)]
    landings = [land_out] * 3 + [land_in] * inner_parts + [land_attn.at[m] for m in (3, 0, 1, 2)]
    finals = [final_out] * 3 + [final_in] * inner_parts + finals[-4:]
    flows = Scatter(place, chunks, flow_send, flow_recv, landings, finals)

    vec_sum[...] = jnp.zeros_like(vec_sum)
    got_slot.wait()
    got_cotangent.wait()
    out_matrix = out_buf.reshape(inner, width)
    normal, inverse = normalize(slot[1])
    for sequence in range(own):
        slot_ids = lax.broadcasted_iota(jnp.int32, (slots, 1), 0)
        live = slot_ids < counts_ref[place.s * own + sequence]
        sum_two[sequence] = jnp.where(live, sum_two[sequence], 0.0)
    grad = sum_two[...].reshape(rows, width)
    vec_sum[0, 6:7] = column_total(grad * normal)
    vec_sum[0, 7:8] = column_total(grad)
    grad = grad * vec[6:7]
    grad = inverse * (
        grad
        - jnp.mean(grad, -1, keepdims=True)
        - normal * jnp.mean(grad * normal, -1, keepdims=True)
    )
    sum_two[...] = grad.reshape(own, slots, width)
    feed_low = grad.astype(bf16)
    feed_both[0] = feed_low
    vec_sum[0, 3:4] = column_total(feed_low.astype(f32))
    came_feed = share(feed_both.at[0], feed_both.at[1])

    got_slope.wait()
    got_out.wait()
    for j in range(inner_parts):
        at = pl.ds(j * width, width)
        back = dot_t(feed_both[0], out_matrix[at]) * slope[:rows, at]
        low = back.astype(bf16)
        inner_both[0, :, at] = low
        vec_sum[0, 8 + j : 9 + j] = column_total(low.astype(f32))
    came_inner = share(inner_both.at[0], inner_both.at[1])

    got_active.wait()
    came_active.wait_recv()
    came_feed.wait_recv()
    all_active = active_both.reshape(2 * rows, inner)
    all_feed = feed_both.reshape(2 * rows, width)
    out_rows = grad_out.reshape(inner, half)

    def second_matrix(i, _):
        at = pl.ds(pl.multiple_of(i * half, 128), half)
        out_rows[at] = t_dot(all_active[:, at], all_feed[:, my_half]).astype(bf16)
        return 0

    lax.fori_loop(0, inner // half, second_matrix, 0)
    flows.begin(0, 1, 2)

    got_low.wait()
    came_low.wait_recv()
    came_inner.wait_recv()
    all_inner = inner_both.reshape(2 * rows, inner)
    in_rows = grad_in.reshape(width, inner // 2)
    first_low = low_both[:, 3].reshape(2 * rows, width)
    for j in range(inner_parts):
        start = pl.multiple_of(place.core * (inner // 2) + j * half, 128)
        result = t_dot(first_low, all_inner[:, pl.ds(start, half)])
        in_rows[:, pl.ds(j * half, half)] = result.astype(bf16)
        flows.begin(3 + j)

    for copy in got_in:
        copy.wait()
    grad = sum_two[...].reshape(rows, width)
    for j in range(inner_parts):
        at = pl.ds(j * width, width)
        grad = grad + dot_t(inner_both[0, :, at], mats.at[j].reshape(width, width)[...])
    normal = slot[0]
    vec_sum[0, 4:5] = column_total(grad * normal)
    vec_sum[0, 5:6] = column_total(grad)
    grad = grad * vec[4:5]
    grad = slot[2] * (
        grad
        - jnp.mean(grad, -1, keepdims=True)
        - normal * jnp.mean(grad * normal, -1, keepdims=True)
    )
    sum_one[...] = grad
    low = grad.astype(bf16)
    attended_both[0] = low
    vec_sum[0, 2:3] = column_total(low.astype(f32))
    came_attended = share(attended_both.at[0], attended_both.at[1])
    came_tokens = share(high_hbm, tokens_both.at[1])
    got_attn = [load(attn_hbm.at[m], mats.at[m]) for m in range(3)]
    got_last.wait()
    context_back[...] = dot_t(low, last.reshape(width, width)[...]).astype(bf16)
    came_attended.wait_recv()
    result = t_dot(
        low_both[:, 1].reshape(2 * rows, width),
        attended_both.reshape(2 * rows, width)[:, my_half],
    )
    grad_attn.at[3].reshape(width, half)[...] = result.astype(bf16)
    flows.begin(3 + inner_parts)

    got_key.wait()
    got_value.wait()
    pair_count = width // 128
    turns = own * pair_count
    lane = lax.broadcasted_iota(jnp.int32, (1, 128), 1)
    order = sorted(
        ((chunk, stage) for chunk in range(len(chunks)) for stage in range(flows.stages)),
        key=lambda item: (item[0] + SPACING * item[1], item[0]),
    )
    during = order[:INSIDE]
    order = order[INSIDE:]

    def attend(i, _):
        for n, item in enumerate(during):
            @pl.when(i == n + 2)
            def _():
                flows.advance(*item)

        sequence, pair = i // pair_count, lax.rem(i, pair_count)
        at = pl.ds(pl.multiple_of(pair * 128, 128), 128)
        slot_at = pl.ds(pl.multiple_of(sequence * slots, slots), slots)
        keys, values = key[sequence, :, at], value[sequence, :, at]
        queries, backs = low_both[0, 2, slot_at, at], context_back[slot_at, at]
        zero = jnp.zeros_like(queries)
        outs = []
        for head in range(2):
            chosen = lane // HD == head
            scores = dot_t(jnp.where(chosen, queries, zero), keys)
            exponent = jnp.exp(scores - jnp.max(scores, -1, keepdims=True))
            probs = exponent / jnp.sum(exponent, -1, keepdims=True)
            grad_probs = dot_t(jnp.where(chosen, backs, zero), values)
            delta = jnp.sum(probs * grad_probs, -1, keepdims=True)
            scores_back = (probs * (grad_probs - delta)).astype(bf16)
            outs.append(
                (
                    dot(scores_back, keys) * scale,
                    t_dot(scores_back, queries),
                    t_dot(probs.astype(bf16), backs),
                )
            )
        left = lane < HD
        query_both[0, slot_at, at] = jnp.where(left, outs[0][0], outs[1][0]).astype(bf16)
        key_back[sequence, :, at] = jnp.where(left, outs[0][1], outs[1][1]).astype(bf16)
        value_back[sequence, :, at] = jnp.where(left, outs[0][2], outs[1][2]).astype(bf16)
        return 0

    lax.fori_loop(0, turns, attend, 0)
    came_query = share(query_both.at[0], query_both.at[1])
    came_key = share(key_back.at[:, :, other_half], key_both.at[1])
    came_value = share(value_back.at[:, :, other_half], value_both.at[1])
    key_both[0] = key_back[:, :, my_half]
    value_both[0] = value_back[:, :, my_half]
    total = jnp.zeros((1, width), f32)
    for sequence in range(own):
        total = total + column_total(value_back[sequence].astype(f32))
    vec_sum[0, 1:2] = total
    vec_sum[0, 0:1] = column_total(query_both[0].astype(f32))

    def vec_copy(stage):
        return pltpu.make_async_remote_copy(
            src_ref=vec_sum.at[stage],
            dst_ref=vec_land.at[stage],
            send_sem=vec_send.at[stage],
            recv_sem=vec_recv.at[stage],
            device_id=place.partner(stage),
            device_id_type=MESH,
        )

    vec_copy(0).start()

    def vec_next(stage):
        vec_copy(stage).wait_recv()
        vec_sum[stage + 1] = vec_sum[stage] + vec_land[stage]
        if stage + 1 < place.levels:
            vec_copy(stage + 1).start()

    came_query.wait_recv()
    result = t_dot(
        low_both[:, 0].reshape(2 * rows, width), query_both.reshape(2 * rows, width)[:, my_half]
    )
    grad_attn.at[0].reshape(width, half)[...] = result.astype(bf16)
    flows.begin(4 + inner_parts)
    got_tokens.wait()
    came_tokens.wait_recv()
    all_tokens = tokens_both.reshape(2 * own * length, width)
    for m, (came, both) in enumerate(((came_key, key_both), (came_value, value_both))):
        came.wait_recv()
        all_back = both.reshape(2 * own * length, half)
        target = grad_attn.at[1 + m].reshape(width, half)

        def weight(i, _):
            at = pl.ds(pl.multiple_of(i * tile, 128), tile)
            target[at] = t_dot(all_tokens[:, at], all_back[...]).astype(bf16)
            return 0

        lax.fori_loop(0, width // tile, weight, 0)
        flows.begin(5 + inner_parts + m)

    def pump(count):
        for _ in range(min(count, len(order))):
            flows.advance(*order.pop(0))

    for copy in got_attn:
        copy.wait()
    query_matrix, key_matrix, value_matrix = (mats.at[m].reshape(width, width) for m in range(3))
    spread = sum_one[...] + dot_t(query_both[0], query_matrix[...])
    top = spread.astype(bf16)
    context_back[...] = top
    feed_rest = (spread - top.astype(f32)).astype(bf16)
    low_both[0, 3] = feed_rest
    place_ids = lax.broadcasted_iota(jnp.int32, (length, slots), 0)
    pump(2)
    for sequence in range(own):
        hits = places_ref[pl.ds(place.s * own + sequence, 1)] == place_ids
        hits = jnp.where(hits, 1.0, 0.0).astype(bf16)
        slot_at = pl.ds(sequence * slots, slots)
        for q in range(per_seq):
            at = slice(q * tile, (q + 1) * tile)
            result = dot_t(key_back[sequence, at], key_matrix[...])
            result = result + dot_t(value_back[sequence, at], value_matrix[...])
            result = result + dot(hits[at], context_back[slot_at])
            result = result + dot(hits[at], low_both[0, 3, slot_at])
            stage_tokens[sequence, at] = result.astype(bf16)
        send_rows(stage_tokens, grad_tokens_ref, sequence)
        vec_next(sequence)
        pump(3)

    for stage in range(own, place.levels):
        vec_next(stage)
        pump(3)
    vec_grad_ref[...] = vec_sum[place.levels]
    pump(len(order))

    final = (final_attn, final_in, final_out)
    for n in range(place.levels - place.bits - 1):
        for index in range(3):
            k = n * 3 + index
            copy = pltpu.make_async_remote_copy(
                src_ref=final[index],
                dst_ref=extra_land[index].at[n],
                send_sem=extra_send.at[k],
                recv_sem=extra_recv.at[k],
                device_id=place.partner(n + 1),
                device_id_type=MESH,
            )
            copy.start()
            copy.wait()
            final[index][...] = final[index][...] + extra_land[index][n]

    hbm = (final_attn_hbm, final_in_hbm, final_out_hbm)
    final_copies = []
    for index in range(3):
        for k, device in enumerate(place.mates()):
            n = index * (merge - 1) + k
            copy = pltpu.make_async_remote_copy(
                src_ref=final[index],
                dst_ref=hbm[index].at[place.member],
                send_sem=final_send.at[n],
                recv_sem=final_recv.at[n],
                device_id=device,
                device_id_type=MESH,
            )
            copy.start()
            final_copies.append(copy)
        copy = pltpu.make_async_copy(
            final[index], hbm[index].at[place.member], own_sem.at[len(owns)]
        )
        copy.start()
        owns.append(copy)
    total = jnp.zeros((1, 1), f32)
    for part in (final_attn[...], final_in[...], final_out[...]):
        part = jnp.sum((part * part).reshape(-1, part.shape[-1]), axis=0, keepdims=True)
        total = total + jnp.sum(part, axis=1, keepdims=True)
    square[...] = jnp.broadcast_to(total, (8, 128)) * (2.0 / merge)
    all_reduce(place, square, square_land, square_send, square_recv)
    rest = vec_sum[place.levels]
    rest = jnp.sum(jnp.sum(rest * rest, axis=0, keepdims=True), axis=1, keepdims=True)
    square_ref[...] = square[...] + rest

    flows.finish()
    for copy in pairs + sends:
        copy.wait_send()
    for copy in sends:
        copy.wait_recv()
    for copy in owns:
        copy.wait()
    for copy in final_copies:
        copy.wait()
    for stage in range(place.levels):
        vec_copy(stage).wait_send()


def all_reduce(place, block, land, send, recv):
    for first, count, me, device in (
        (0, place.dp, place.d, lambda other: (place.s, other)),
        (place.dp, place.seq, place.s, lambda other: (other, place.d)),
    ):

        def copy(k, first=first, count=count, me=me, device=device):
            return pltpu.make_async_remote_copy(
                src_ref=block,
                dst_ref=land.at[first + k],
                send_sem=send.at[first + k],
                recv_sem=recv.at[first + k],
                device_id=device(lax.rem(me + k, count)),
                device_id_type=MESH,
            )

        for k in range(1, count):
            copy(k).start()
        land[first] = block[...]
        for k in range(1, count):
            copy(k).wait_recv()
        for k in range(1, count):
            copy(k).wait_send()
        total = land[first + me]
        for k in range(1, count):
            total = total + land[first + lax.rem(me - k + count, count)]
        block[...] = total


def backward_call(mesh, forward, positions, counts, cotangent, rows):
    attn, ffn_in, ffn_out, vec, high, query, key, value, output, slot_low, slot, slot_active, slope = forward
    place = Place(mesh, rows)
    own, length, width = high.shape
    inner = ffn_in.shape[-1]
    sequences = positions.shape[0]
    block = length // place.seq
    slots = positions.shape[1]
    count = own * slots
    half = width // 2
    bits = (2,) * place.bits
    joint, joint_out = ffn_in.shape[-2], ffn_out.shape[-2]
    merge = place.merge
    dma = pltpu.SemaphoreType.DMA
    vmem = pl.BlockSpec(memory_space=pltpu.VMEM)
    hbm = pl.BlockSpec(memory_space=pl.ANY)
    smem = pl.BlockSpec(memory_space=pltpu.SMEM)
    flow_count = (4 + inner // width + 3) * 3 * (place.bits + 1)
    tile = min(256, length)
    finals = [(4, joint, half), (joint, inner // 2), (joint_out, half)]
    extra = place.levels - place.bits - 1
    scratch = [
        pltpu.VMEM((4,) + bits + (joint, width), bf16),
        pltpu.VMEM(bits + (joint, width), bf16),
        pltpu.VMEM(bits + (joint_out, width), bf16),
    ]
    for _ in range(2):
        scratch += [
            pltpu.VMEM((4,) + bits + (joint, half), bf16),
            pltpu.VMEM(bits + (joint, inner // 2), bf16),
            pltpu.VMEM(bits + (joint_out, half), bf16),
        ]
    scratch += [pltpu.VMEM(shape, f32) for shape in finals]
    scratch += [
        pltpu.VMEM((2, own, length, width), bf16),
        pltpu.VMEM((own, length, width), bf16),
        pltpu.VMEM((own, length, width), bf16),
        pltpu.VMEM((2, count, inner), bf16),
        pltpu.VMEM((2, count, inner), bf16),
        pltpu.VMEM((max(count, tile), inner), f32),
        pltpu.VMEM((2, 4, count, width), bf16),
        pltpu.VMEM((3, count, width), f32),
        pltpu.VMEM((2, count, width), bf16),
        pltpu.VMEM((2, count, width), bf16),
        pltpu.VMEM((2, count, width), bf16),
        pltpu.VMEM((count, width), bf16),
        pltpu.VMEM((own, slots, width), f32),
        pltpu.VMEM((own, length, width), bf16),
        pltpu.VMEM((own, length, width), bf16),
        pltpu.VMEM((2, own, length, half), bf16),
        pltpu.VMEM((2, own, length, half), bf16),
        pltpu.VMEM((own, length, width), bf16),
        pltpu.VMEM((place.levels + 1, 16, width), f32),
        pltpu.VMEM((place.levels, 16, width), f32),
        pltpu.VMEM((8, 128), f32),
        pltpu.VMEM((place.dp + place.seq, 8, 128), f32),
        dma((flow_count,)),
        dma((flow_count,)),
        dma((24,)),
        dma((16,)),
        dma((16,)),
        dma((2 * own * (place.seq - 1),)),
        dma((2 * own * (place.seq - 1),)),
        dma((2 * own + 3,)),
        dma((place.levels,)),
        dma((place.levels,)),
        dma((3 * (merge - 1),)),
        dma((3 * (merge - 1),)),
        dma((place.dp + place.seq,)),
        dma((place.dp + place.seq,)),
    ]
    if extra:
        scratch += [
            [pltpu.VMEM((extra,) + shape, f32) for shape in finals],
            dma((3 * extra,)),
            dma((3 * extra,)),
        ]
    results = [
        ((sequences, block, width), bf16),
        ((sequences, block, width), bf16),
        ((merge,) + finals[0], f32),
        ((merge,) + finals[1], f32),
        ((merge,) + finals[2], f32),
        ((16, width), f32),
        ((8, 128), f32),
    ]
    return pl.pallas_call(
        functools.partial(backward_kernel, place),
        out_shape=[jax.ShapeDtypeStruct(*one) for one in results],
        in_specs=[hbm, hbm, hbm, vmem] + [hbm] * 8 + [vmem, smem, hbm],
        out_specs=[hbm] * 5 + [vmem] * 2,
        scratch_shapes=scratch,
        compiler_params=pltpu.CompilerParams(
            collective_id=1, has_side_effects=True, vmem_limit_bytes=64 * 2**20 - 2**18
        ),
    )(
        attn, ffn_in, ffn_out, vec, high, key, value, output, slot_low, slot,
        slot_active, slope, positions, counts, cotangent,
    )


def total_kernel(place, block_ref, total_ref, block, land, send, recv):
    place.here()
    place.greet_all()
    block[...] = block_ref[...]
    all_reduce(place, block, land, send, recv)
    total_ref[...] = block[...]


def total_call(mesh, rows, block):
    place = Place(mesh, rows)
    vmem = pl.BlockSpec(memory_space=pltpu.VMEM)
    dma = pltpu.SemaphoreType.DMA
    count = place.dp + place.seq
    return pl.pallas_call(
        functools.partial(total_kernel, place),
        out_shape=jax.ShapeDtypeStruct((8, 128), f32),
        in_specs=[vmem],
        out_specs=vmem,
        scratch_shapes=[
            pltpu.VMEM((8, 128), f32),
            pltpu.VMEM((count, 8, 128), f32),
            dma((count,)),
            dma((count,)),
        ],
        compiler_params=pltpu.CompilerParams(collective_id=2, has_side_effects=True),
    )(block)


def pieces_of(shapes):
    attn, first, second = shapes
    half = attn[-1] // 2
    found = []
    for m in range(attn[0]):
        for core in range(2):
            found.append((0, core, (m,), pl.ds(core * half, half), m))
    for n, shape in ((1, first), (2, second)):
        half = shape[-1] // 2
        for core in range(2):
            found.append((n, core, (), pl.ds(core * half, half), 3 + n))
    return found


def update_kernel(place, *refs):
    finals, square, olds, firsts, seconds = refs[:3], refs[3], refs[4:7], refs[7:10], refs[10:13]
    clipped, new_firsts, new_seconds, directions = refs[13:16], refs[16:19], refs[19:22], refs[22:25]
    sums = refs[25]
    place.here()
    clip = 1.0 / jnp.maximum(jnp.sqrt(square[0:1, 0:1]), 1.0)
    correct = 1.0 - decay_rate**STEP
    row = lax.broadcasted_iota(jnp.int32, (8, 128), 0)
    lane = lax.broadcasted_iota(jnp.int32, (8, 128), 1)

    def total_of(x):
        return jnp.sum(jnp.sum(x * x, axis=0, keepdims=True), axis=1, keepdims=True)

    for member in range(place.merge):

        @pl.when(place.member == member)
        def _():
            block = jnp.zeros((8, 128), f32)
            for n, core, lead, columns, which in pieces_of([ref.shape for ref in olds]):
                count = olds[n].shape[-2]
                at = lead + (slice(None), columns)
                grad = finals[n][(core,) + lead + (slice(member * count, (member + 1) * count),)]
                grad = grad * clip
                clipped[n][at] = grad
                first = decay_rate * firsts[n][at] + (1.0 - decay_rate) * grad
                second = decay_rate * seconds[n][at] + (1.0 - decay_rate) * grad * grad
                new_firsts[n][at] = first
                new_seconds[n][at] = second
                old = olds[n][at]
                way = first / correct / (jnp.sqrt(second / correct) + adam_eps)
                way = way + weight_decay * old
                directions[n][at] = way
                block = block + jnp.where((row == 0) & (lane == which), total_of(old), 0.0)
                block = block + jnp.where((row == 1) & (lane == which), total_of(way), 0.0)
            sums[...] = block


def update_call(mesh, finals, square, olds, firsts, seconds):
    place = Place(mesh, olds[1].shape[0])
    shapes = [jax.ShapeDtypeStruct(old.shape, f32) for old in olds]
    vmem = pl.BlockSpec(memory_space=pltpu.VMEM)
    results = pl.pallas_call(
        functools.partial(update_kernel, place),
        out_shape=shapes * 4 + [jax.ShapeDtypeStruct((8, 128), f32)],
        in_specs=[vmem] * 13,
        out_specs=[vmem] * 13,
        compiler_params=pltpu.CompilerParams(vmem_limit_bytes=32 * 2**20),
    )(*finals, square, *olds, *firsts, *seconds)
    return results[:3], results[3:6], results[6:9], results[9:12], results[12]


def step_kernel(total, *refs):
    olds, directions, news, lows = refs[:3], refs[3:6], refs[6:9], refs[9:12]
    norms = jnp.sqrt(total[0:2])
    for n, core, lead, columns, which in pieces_of([ref.shape for ref in olds]):
        at = lead + (slice(None), columns)
        trust = norms[0:1, which : which + 1] / norms[1:2, which : which + 1]
        new = olds[n][at] - step_rate * trust * directions[n][at]
        news[n][at] = new
        lows[n][at] = new.astype(bf16)


def step_call(total, olds, directions):
    vmem = pl.BlockSpec(memory_space=pltpu.VMEM)
    results = pl.pallas_call(
        step_kernel,
        out_shape=[jax.ShapeDtypeStruct(old.shape, f32) for old in olds]
        + [jax.ShapeDtypeStruct(old.shape, bf16) for old in olds],
        in_specs=[vmem] * 7,
        out_specs=[vmem] * 6,
        compiler_params=pltpu.CompilerParams(vmem_limit_bytes=32 * 2**20),
    )(total, *olds, *directions)
    return results[:3], results[3:]


def adam_direction(first_old, second_old, clipped):
    first_new = decay_rate * first_old + (1.0 - decay_rate) * clipped
    second_new = decay_rate * second_old + (1.0 - decay_rate) * clipped * clipped
    correct = 1.0 - decay_rate**STEP
    direction = first_new / correct / (jnp.sqrt(second_new / correct) + adam_eps)
    return (first_new, second_new, direction)


def body(
    mesh,
    tokens,
    positions,
    counts,
    cotangent,
    attn_weights,
    ffn_in,
    ffn_out,
    vectors,
    attn_first,
    ffn_in_first,
    ffn_out_first,
    vector_first,
    attn_second,
    ffn_in_second,
    ffn_out_second,
    vector_second,
):
    results = forward_call(mesh, tokens, positions, attn_weights, ffn_in, ffn_out, vectors)
    rows = ffn_in.shape[0]
    output, grad_tokens, *final, vec_total, square_sum = backward_call(
        mesh, results, positions, counts, cotangent, rows
    )
    olds = (attn_weights, ffn_in, ffn_out)
    clipped, new_firsts, new_seconds, directions, sums = update_call(
        mesh,
        final,
        square_sum,
        olds,
        (attn_first, ffn_in_first, ffn_out_first),
        (attn_second, ffn_in_second, ffn_out_second),
    )
    total = total_call(mesh, rows, sums)
    news, lows = step_call(total, olds, directions)
    lamb_norms = jnp.sqrt(total[:2, :6])
    trust_ratio = lamb_norms[0] / lamb_norms[1]
    grad_norm = jnp.sqrt(square_sum[0, 0])
    owner = lax.axis_index("seq") * lax.axis_size("dp") + lax.axis_index("dp")
    vec_count = vectors.shape[0]
    vec_share = lax.dynamic_slice_in_dim(vec_total.reshape(-1), owner * vec_count, vec_count, 0)
    vec_share = vec_share * (1.0 / jnp.maximum(grad_norm, 1.0))
    vec_moved = adam_direction(vector_first, vector_second, vec_share)
    new_vectors = vectors - step_rate * vec_moved[2]
    return (
        output.astype(f32),
        grad_tokens.astype(f32),
        *clipped,
        vec_share,
        *new_firsts,
        vec_moved[0],
        *new_seconds,
        vec_moved[1],
        *news,
        new_vectors,
        *lows,
        lamb_norms,
        trust_ratio,
        grad_norm,
    )


def solution(mesh):
    return jax.shard_map(
        functools.partial(body, mesh),
        mesh=mesh,
        in_specs=(
            P("dp", "seq", None),
            P("dp", None),
            P("dp"),
            P("dp", None, None),
            P(None, ("seq", "dp"), None),
            P(("seq", "dp"), None),
            P(("seq", "dp"), None),
            P(("seq", "dp")),
            P(None, ("seq", "dp"), None),
            P(("seq", "dp"), None),
            P(("seq", "dp"), None),
            P(("seq", "dp")),
            P(None, ("seq", "dp"), None),
            P(("seq", "dp"), None),
            P(("seq", "dp"), None),
            P(("seq", "dp")),
        ),
        out_specs=(
            P("dp", "seq", None),
            P("dp", "seq", None),
            P(None, ("seq", "dp"), None),
            P(("seq", "dp"), None),
            P(("seq", "dp"), None),
            P(("seq", "dp")),
            P(None, ("seq", "dp"), None),
            P(("seq", "dp"), None),
            P(("seq", "dp"), None),
            P(("seq", "dp")),
            P(None, ("seq", "dp"), None),
            P(("seq", "dp"), None),
            P(("seq", "dp"), None),
            P(("seq", "dp")),
            P(None, ("seq", "dp"), None),
            P(("seq", "dp"), None),
            P(("seq", "dp"), None),
            P(("seq", "dp")),
            P(None, ("seq", "dp"), None),
            P(("seq", "dp"), None),
            P(("seq", "dp"), None),
            P(),
            P(),
            P(),
        ),
        check_vma=False,
    )
```
